128 devices in a mesh: dp: 16 (over y_lo, x, core), fsdp: 8 (over y_hi, z).
Axes of the slice: x: 4, y: 4 (y_hi: 2, y_lo: 2; y = y_hi * 2 + y_lo), z: 4, core: 2. Of those that a mesh axis runs over, the one named last changes fastest.
Arguments:
- tokens: bfloat16 [32768, 1024], P(('dp', 'fsdp')), may hold values from -24 to 24
- positions: int32 [32768], P(('dp', 'fsdp')), may hold values from 0 to 255, as said below
- w_query: bfloat16 [1024, 2048], P('dp', 'fsdp'), may hold values from -0.1875 to 0.1875
- w_key: bfloat16 [1024, 1024], P('dp', 'fsdp'), may hold values from -0.1875 to 0.1875
- w_value: bfloat16 [1024, 1024], P('dp', 'fsdp'), may hold values from -0.1875 to 0.1875
- w_out: bfloat16 [2048, 1024], P('fsdp', 'dp'), may hold values from -0.125 to 0.125
- w_gate: bfloat16 [1024, 3072], P('dp', 'fsdp'), may hold values from -0.1875 to 0.1875
- w_up: bfloat16 [1024, 3072], P('dp', 'fsdp'), may hold values from -0.1875 to 0.1875
- w_down: bfloat16 [3072, 1024], P('fsdp', 'dp'), may hold values from -0.109375 to 0.109375
- query_gain: bfloat16 [128], P('dp'), may hold values from 1 to 2
- key_gain: bfloat16 [128], P('dp'), may hold values from 1 to 2
- attn_gain: bfloat16 [1024], P('dp'), may hold values from 0.5 to 2
- ffn_gain: bfloat16 [1024], P('dp'), may hold values from 0.5 to 2
- cotangent: bfloat16 [32768, 1024], P(('dp', 'fsdp')), may hold values from -24 to 24
Outputs:
- mixed: bfloat16 [32768, 1024], P(('dp', 'fsdp'))
- tokens_grad: float32 [32768, 1024], P(('dp', 'fsdp'))
- w_query_grad: float32 [1024, 2048], P('dp', 'fsdp')
- w_key_grad: float32 [1024, 1024], P('dp', 'fsdp')
- w_value_grad: float32 [1024, 1024], P('dp', 'fsdp')
- w_out_grad: float32 [2048, 1024], P('fsdp', 'dp')
- w_gate_grad: float32 [1024, 3072], P('dp', 'fsdp')
- w_up_grad: float32 [1024, 3072], P('dp', 'fsdp')
- w_down_grad: float32 [3072, 1024], P('fsdp', 'dp')
- query_gain_grad: float32 [128], P('dp')
- key_gain_grad: float32 [128], P('dp')
- attn_gain_grad: float32 [1024], P('dp')
- ffn_gain_grad: float32 [1024], P('dp')
The draws below stay inside these ranges and needn't reach their ends.
Inputs may be any that keep to these rules, and one draw needn't show every extreme that they name: Every aligned block of 256 tokens holds whole sequences: each sequence's positions run 0, 1, 2, ... in consecutive slots, and every block begins with 0. In every draw one block holds a single sequence of 256 tokens.
All inputs are finite; a program needn't handle non-finite values.
Results may differ from the reference program's by a relative error of at most 0.025.
Values may be sent and summed in bfloat16 or wider, within the bound.
A program may use at most 192 MiB of HBM per device.

```python
import math
import jax
import jax.numpy as jnp
from jax import lax

D = 1024
H = 16
KVH = 8
HD = 128
FF = 3072
TOK_DEV = 256
TOKENS = 32768
N_DP = 16
N_FSDP = 8


def draw_positions(key, part):
    key = jax.random.fold_in(key, 11)
    rate_key, start_key, whole_key = jax.random.split(key, 3)
    devices = TOKENS // TOK_DEV
    spacing = jax.random.randint(rate_key, (devices, 1), 2, TOK_DEV + 1)
    marks = jax.random.randint(start_key, (devices, TOK_DEV), 0, 1 << 20) % spacing == 0
    whole = jax.random.randint(whole_key, (), 0, devices)
    slots = jnp.arange(TOK_DEV, dtype=jnp.int32)[None, :]
    device_index = jnp.arange(devices, dtype=jnp.int32)[:, None]
    starts = (marks | (slots == 0)) & ((device_index != whole) | (slots == 0))
    latest = lax.cummax(jnp.where(starts, slots, 0), axis=1)
    return (slots - latest).astype(jnp.int32).reshape(-1)


def with_spikes(values, own_key, source, target, shards_of, factor):
    def block_of(position):
        return (jnp.arange(values.shape[position]) // (values.shape[position] // shards_of)).reshape((-1,) + (1,) * (values.ndim - 1 - position))

    near = jax.random.permutation(own_key, shards_of)[block_of(target)]
    second = (block_of(target) + shards_of // 2) % shards_of
    return jnp.where((block_of(source) == near) | (block_of(source) == second), factor * values, values)


def block_scale(key, extent, cuts, low, largest):
    level = 1.0
    for dim, shards_of in cuts:
        steps = jax.random.uniform(jax.random.fold_in(jax.random.fold_in(key, 6), dim), (shards_of,), jnp.float32, low / len(cuts), largest / len(cuts))
        level = level * jnp.repeat(jnp.exp(steps), extent[dim] // shards_of).reshape((-1,) + (1,) * (len(extent) - 1 - dim))
    return level


def scatter_about(rng, shape, width, bound, cuts=(), held_as=jnp.bfloat16):
    result = width * jax.random.normal(rng, shape, jnp.float32)
    if cuts:
        result = result * block_scale(rng, shape, cuts, -0.22, 0.18)
    return jnp.clip(result, -bound, bound).astype(held_as)


def noise_with(own_key, shape, scale, limit, cuts, heavy, held_as=jnp.bfloat16):
    array = scale * jax.random.normal(own_key, shape, jnp.float32)
    if cuts:
        array = array * block_scale(own_key, shape, cuts, -0.22, 0.18)
    return jnp.clip(with_spikes(array, jax.random.fold_in(own_key, 3), *heavy), -limit, limit).astype(held_as)


def setup_inputs(seed: int = 0) -> dict:
    key_of = jax.random.split(jax.random.key(seed), 15)
    tokens = noise_with(key_of[0], (TOKENS, D), 1.0, 24.0, ((0, 128),), (0, 1, 128, 5.5))
    positions = draw_positions(jax.random.fold_in(key_of[14], 71), 0)
    w_query = scatter_about(key_of[2], (D, H * HD), D ** -0.5, 0.1875, ((0, 16), (1, 8)))
    w_key = scatter_about(key_of[3], (D, KVH * HD), D ** -0.5, 0.1875, ((0, 16), (1, 8)))
    w_value = scatter_about(key_of[4], (D, KVH * HD), D ** -0.5, 0.1875, ((0, 16), (1, 8)))
    w_out = scatter_about(key_of[5], (H * HD, D), (H * HD) ** -0.5, 0.125, ((0, 8), (1, 16)))
    w_gate = scatter_about(key_of[6], (D, FF), D ** -0.5, 0.1875, ((0, 16), (1, 8)))
    w_up = scatter_about(key_of[7], (D, FF), D ** -0.5, 0.1875, ((0, 16), (1, 8)))
    w_down = scatter_about(key_of[8], (FF, D), FF ** -0.5, 0.109375, ((0, 8), (1, 16)))
    query_gain = jnp.clip(jnp.exp(math.log(2.0) - 0.6931472 * jax.random.uniform(key_of[9], (HD,), jnp.float32) ** block_scale(key_of[9], (HD,), ((0, 16),), -0.2, 0.2)), 1.0, 2.0).astype(jnp.bfloat16)
    key_gain = jnp.clip(jnp.exp(math.log(2.0) - 0.6931472 * jax.random.uniform(key_of[10], (HD,), jnp.float32) ** block_scale(key_of[10], (HD,), ((0, 16),), -0.2, 0.2)), 1.0, 2.0).astype(jnp.bfloat16)
    attn_gain = jnp.clip(jnp.exp(math.log(2.0) - 1.3862944 * jax.random.uniform(key_of[11], (D,), jnp.float32) ** block_scale(key_of[11], (D,), ((0, 16),), -0.2, 0.2)), 0.5, 2.0).astype(jnp.bfloat16)
    ffn_gain = jnp.clip(jnp.exp(math.log(2.0) - 1.3862944 * jax.random.uniform(key_of[12], (D,), jnp.float32) ** block_scale(key_of[12], (D,), ((0, 16),), -0.2, 0.2)), 0.5, 2.0).astype(jnp.bfloat16)
    cotangent = noise_with(key_of[13], (TOKENS, D), 1.0, 24.0, ((0, 128),), (0, 1, 128, 5.5))
    return dict(tokens=tokens, positions=positions, w_query=w_query, w_key=w_key, w_value=w_value, w_out=w_out, w_gate=w_gate, w_up=w_up, w_down=w_down, query_gain=query_gain, key_gain=key_gain, attn_gain=attn_gain, ffn_gain=ffn_gain, cotangent=cotangent)


EPS = 1e-06
ROPE_BASE = 1000000.0
HIGHEST = lax.Precision.HIGHEST

@jax.custom_vjp
def low(v):
    return lax.optimization_barrier(v.astype(jnp.bfloat16)).astype(jnp.float32)

@jax.custom_vjp
def low_back(v):
    return v

def low_keep(v):
    return (low(v), None)

def low_pass(kept, grad):
    return (grad,)

def back_keep(v):
    return (v, None)

def back_low(kept, grad):
    return (low(grad),)
low.defvjp(low_keep, low_pass)
low_back.defvjp(back_keep, back_low)

def rope_tables(places, head_width):
    steps_up = jnp.arange(0, head_width, 2).astype(jnp.float32) / head_width
    inverse = ROPE_BASE ** (-steps_up)
    angles = places.astype(jnp.float32)[:, None] * inverse[None, :]
    cosine = jnp.cos(angles)
    sine_part = jnp.sin(angles)
    return (jnp.concatenate([cosine, cosine], -1), jnp.concatenate([sine_part, sine_part], -1))

def rms_scale(values_in, gain_in):
    return values_in * lax.rsqrt(lax.optimization_barrier(jnp.mean(values_in * values_in, axis=-1, keepdims=True)) + EPS) * gain_in

def rotate(values_in, cosine, sine_part):
    half_size = values_in.shape[-1] // 2
    turned = jnp.concatenate([-values_in[..., half_size:], values_in[..., :half_size]], -1)
    return values_in * cosine + turned * sine_part

def attention_block(query, keys, values, places):
    length = places.shape[0]
    slots = jnp.arange(length, dtype=jnp.int32)
    first = slots - places
    allowed = (slots[None, :] <= slots[:, None]) & (slots[None, :] >= first[:, None])
    scores = jnp.einsum('qgrd,kgd->grqk', query, keys, precision=HIGHEST) * query.shape[-1] ** (-0.5)
    scores = low_back(scores)
    scores = jnp.where(allowed[None, None], scores, -1e+30)
    row_top = lax.optimization_barrier(jnp.max(scores, axis=-1, keepdims=True))
    weights = jnp.exp(scores - row_top)
    probs = low(weights / lax.optimization_barrier(jnp.sum(weights, axis=-1, keepdims=True)))
    attended = jnp.einsum('grqk,kgd->qgrd', probs, values, precision=HIGHEST)
    return attended.reshape(length, -1)

def forward(inputs, w_query, w_key, w_value, w_out, w_gate, w_up, w_down, query_gain, key_gain, attn_gain, ffn_gain, cosine, sine_part, places):
    row_count = inputs.shape[0]
    head_count = w_query.shape[1] // HD
    kv_count = w_key.shape[1] // HD
    q_raw = low_back(jnp.dot(inputs, w_query, precision=HIGHEST))
    k_raw = low_back(jnp.dot(inputs, w_key, precision=HIGHEST))
    v_raw = low_back(jnp.dot(inputs, w_value, precision=HIGHEST))
    cos_heads = cosine[:, None, :]
    sin_heads = sine_part[:, None, :]
    query = low(rotate(rms_scale(q_raw.reshape(row_count, head_count, HD), query_gain), cos_heads, sin_heads))
    keys = low(rotate(rms_scale(k_raw.reshape(row_count, kv_count, HD), key_gain), cos_heads, sin_heads))
    values = low(v_raw)
    block_count = row_count // TOK_DEV
    query = query.reshape(block_count, TOK_DEV, kv_count, head_count // kv_count, HD)
    keys = keys.reshape(block_count, TOK_DEV, kv_count, HD)
    values = values.reshape(block_count, TOK_DEV, kv_count, HD)
    checked = jax.checkpoint(attention_block)
    attended = lax.map(lambda item: checked(item[0], item[1], item[2], item[3]), (query, keys, values, places.reshape(block_count, TOK_DEV)))
    attended = low(low_back(attended.reshape(row_count, head_count * HD)))
    branch = low_back(jnp.dot(attended, w_out, precision=HIGHEST))
    hidden = inputs + rms_scale(branch, attn_gain)
    hidden_low = low(hidden)
    gate = low_back(jnp.dot(hidden_low, w_gate, precision=HIGHEST))
    upward = low_back(jnp.dot(hidden_low, w_up, precision=HIGHEST))
    act_low = low(jax.nn.silu(gate) * upward)
    ffn = low_back(jnp.dot(act_low, w_down, precision=HIGHEST))
    return hidden + rms_scale(ffn, ffn_gain)

def reference(tokens, positions, w_query, w_key, w_value, w_out, w_gate, w_up, w_down, query_gain, key_gain, attn_gain, ffn_gain, cotangent):
    devices = N_DP * N_FSDP
    group = TOK_DEV * min(devices, max(1, 4096 // TOK_DEV))
    group_count = tokens.shape[0] // group
    params = tuple((weight.astype(jnp.float32) for weight in (w_query, w_key, w_value, w_out, w_gate, w_up, w_down, query_gain, key_gain, attn_gain, ffn_gain)))
    cosine, sine_part = rope_tables(positions, HD)

    def step(totals, item):
        inputs, places, cos_group, sin_group, grad_out = item

        def run(inputs_in, *weights):
            return forward(inputs_in, *weights, cos_group, sin_group, places)
        output, pull = jax.vjp(run, inputs, *params)
        grads = pull(grad_out)
        totals = tuple((total + grad_part for total, grad_part in zip(totals, grads[1:])))
        return (totals, (output, grads[0]))
    zeros = tuple((jnp.zeros(weight.shape, jnp.float32) for weight in params))
    inputs_all = (tokens.astype(jnp.float32).reshape(group_count, group, D), positions.reshape(group_count, group), cosine.reshape(group_count, group, HD), sine_part.reshape(group_count, group, HD), cotangent.astype(jnp.float32).reshape(group_count, group, D))
    totals, (outputs, input_grads) = lax.scan(step, zeros, inputs_all)
    return (outputs.reshape(-1, D).astype(jnp.bfloat16), input_grads.reshape(-1, D), totals[0], totals[1], totals[2], totals[3], totals[4], totals[5], totals[6], totals[7], totals[8], totals[9], totals[10])
```

```python
import numpy as np
import jax
import jax.numpy as jnp
from jax import lax
from jax.experimental import pallas as pl
from jax.experimental.pallas import tpu as pltpu
from jax.sharding import PartitionSpec as P

MESH = pl.DeviceIdType.MESH
F32, BF = jnp.float32, jnp.bfloat16
D, HD, TOK = 1024, 128, 256
EPS = 1e-6
ROPE_BASE = 1000000.0
MATS = (
    ("q", 256, 128, BF, "xyz"),
    ("kv", 256, 128, BF, "yzx"),
    ("o", 256, 128, BF, "zxy"),
    ("g", 384, 128, BF, "xyz"),
    ("u", 384, 128, BF, "yzx"),
    ("d", 384, 128, BF, "zxy"),
    ("n", 128, 16, F32, "zxy"),
)


def nn(a, b):
    return jnp.dot(a, b, preferred_element_type=F32)


def nt(a, b):
    return lax.dot_general(a, b, (((1,), (1,)), ((), ())), preferred_element_type=F32)


def tn(a, b):
    return lax.dot_general(a, b, (((0,), (0,)), ((), ())), preferred_element_type=F32)


def when(cond, body):
    if cond is None:
        body()
    else:
        pl.when(cond)(body)


class Place:
    def __init__(self):
        dp, fs = lax.axis_index("dp"), lax.axis_index("fsdp")
        self.dp = dp
        self.c = lax.rem(dp, 2)
        self.x = lax.rem(lax.div(dp, 2), 4)
        self.yl = lax.div(dp, 8)
        self.yh = lax.div(fs, 4)
        self.z = lax.rem(fs, 4)
        self.y = self.yh * 2 + self.yl
        self.zi = lax.div(self.z, 2)
        self.own = lax.rem(self.z, 2) == self.c
        self.other = lax.rem(self.z, 2) != self.c

    def device(self, x, y, z, c):
        return (lax.rem(y, 2) * 8 + x * 2 + c, lax.div(y, 2) * 4 + z)

    def step(self, axis, by):
        go = lambda v: lax.rem(v + (by + 4), 4)
        return self.device(
            go(self.x) if axis == "x" else self.x,
            go(self.y) if axis == "y" else self.y,
            go(self.z) if axis == "z" else self.z,
            self.c,
        )

    def sibling(self):
        return self.device(self.x, self.y, self.z, 1 - self.c)

    def at(self, axis, by=0):
        if axis == "z":
            return lax.div(lax.rem(self.z + (by + 4), 4), 2)
        return lax.rem((self.x if axis == "x" else self.y) + (by + 4), 4)


def block_index(cols, rows, cx, cy, cz, half):
    yh, yl = (slice(None), slice(None)) if cy is None else (lax.div(cy, 2), lax.rem(cy, 2))
    rr = slice(None) if half is None else pl.ds(half * (rows // 2), rows // 2)
    cc = slice(None) if cz is None else pl.ds(pl.multiple_of(cz * cols, 128), cols)
    return (yh, yl, slice(None) if cx is None else cx, rr, cc)


def block_shape(cols, rows, cx, cy, cz, half):
    lead = (() if cy is not None else (2, 2)) + (() if cx is not None else (4,))
    return lead + (rows // 2 if half else rows, cols if cz is not None else 2 * cols)


class Matrix:
    def __init__(self, number, ref, place, sems):
        self.number, self.ref, self.place = number, ref, place
        self.name, self.cols, self.rows, self.dtype, self.order = MATS[number]
        self.send, self.gather_recv, self.reduce_recv = sems
        self.bufs = None

    def slot(self, phase, kind):
        return (self.number * 3 + phase) * 4 + kind

    def coords(self, phase, order, v, half, gather):
        cur, done = order[phase], order[:phase]
        out = []
        for axis in "xyz":
            if axis == cur:
                out.append(v)
            elif (axis in done) == gather:
                out.append(None)
            else:
                out.append(self.place.at(axis))
        return (self.cols, self.rows, *out, half)

    def gblock(self, phase, v, half=None):
        return self.ref.at[block_index(*self.coords(phase, self.order, v, half, True))]

    def rblock(self, phase, v, half=None):
        return self.ref.at[block_index(*self.coords(phase, self.order[::-1], v, half, False))]

    def copy(self, src, dst, phase, kind, by, axis, recv):
        k = self.slot(phase, kind)
        return pltpu.make_async_remote_copy(
            src_ref=src,
            dst_ref=dst,
            send_sem=self.send.at[k],
            recv_sem=recv.at[k],
            device_id=self.place.step(axis, by),
            device_id_type=MESH,
        )

    def gcopy(self, phase, kind, v):
        half = None if kind < 2 else kind - 2
        ref = self.gblock(phase, v, half)
        return self.copy(
            ref, ref, phase, kind, 1 if kind % 2 == 0 else -1, self.order[phase], self.gather_recv
        )

    def gather_active(self, phase):
        axis = self.order[phase]
        if axis == "z" or "z" in self.order[:phase]:
            return None
        return self.place.own

    def gather1(self, phase):
        axis = self.order[phase]
        here = self.place.at(axis)

        def body():
            self.gcopy(phase, 0, here).start()
            self.gcopy(phase, 1, here).start()

        when(self.place.own if axis == "z" else self.gather_active(phase), body)

    def gather2(self, phase):
        axis = self.order[phase]
        left, right = self.place.at(axis, -1), self.place.at(axis, 1)

        def body():
            self.gcopy(phase, 0, left).wait_recv()
            self.gcopy(phase, 2, left).start()
            self.gcopy(phase, 1, right).wait_recv()
            self.gcopy(phase, 3, right).start()

        when(self.place.other if axis == "z" else self.gather_active(phase), body)

    def gather3(self, phase):
        axis = self.order[phase]
        far = self.place.at(axis, 2)

        def body():
            self.gcopy(phase, 2, far).wait_recv()
            self.gcopy(phase, 3, far).wait_recv()

        when(self.place.own if axis == "z" else self.gather_active(phase), body)

    def gather_drain(self):
        for phase in range(3):
            axis = self.order[phase]
            here = self.place.at(axis)

            def first(phase=phase, here=here):
                self.gcopy(phase, 0, here).wait_send()
                self.gcopy(phase, 1, here).wait_send()

            def second(phase=phase, here=here):
                self.gcopy(phase, 2, here).wait_send()
                self.gcopy(phase, 3, here).wait_send()

            if axis == "z":
                when(self.place.own, first)
                when(self.place.other, second)
            else:
                def both(first=first, second=second):
                    first()
                    second()

                when(self.gather_active(phase), both)

    def landing(self, phase, kind):
        axis = self.order[::-1][phase]
        whole, half = self.bufs[phase]
        if kind < 2:
            return whole.at[kind]
        if axis == "z":
            ref = whole.at[kind - 2]
            idx = (slice(None),) * (len(ref.shape) - 2) + (pl.ds(0, self.rows // 2),)
            return ref.at[idx]
        return half.at[kind - 2]

    def rcopy(self, phase, kind, v):
        half = None if kind < 2 else kind - 2
        return self.copy(
            self.rblock(phase, v, half),
            self.landing(phase, kind),
            phase,
            kind,
            1 if kind % 2 == 0 else -1,
            self.order[::-1][phase],
            self.reduce_recv,
        )

    def reduce_active(self, phase):
        order = self.order[::-1]
        return self.place.own if "z" in order[:phase] else None

    def add(self, phase, v, half, sources, out=None):
        cols, rows, cx, cy, cz, _ = self.coords(phase, self.order[::-1], v, half, False)
        ny, nx = (4 if cy is None else 1), (4 if cx is None else 1)
        height = rows if half is None else rows // 2
        step = min(64, height)
        first = 0 if half is None else half * height
        cc = slice(None) if cz is None else pl.ds(pl.multiple_of(cz * cols, 128), cols)

        def body(n, carry):
            part = lax.rem(n, height // step)
            m = lax.div(n, height // step)
            iy, ix = lax.div(m, nx), lax.rem(m, nx)
            y = iy if cy is None else cy
            x = ix if cx is None else cx
            lead = ((lax.div(iy, 2), lax.rem(iy, 2)) if cy is None else ()) + (
                (ix,) if cx is None else ()
            )
            idx = (
                lax.div(y, 2),
                lax.rem(y, 2),
                x,
                pl.ds(pl.multiple_of(first + part * step, 8), step),
                cc,
            )
            here = pl.ds(pl.multiple_of(part * step, 8), step)
            total = self.ref[idx].astype(F32)
            for src in sources:
                total = total + src[lead + (here, slice(None))].astype(F32)
            if out is None:
                self.ref[idx] = total.astype(self.dtype)
            else:
                out[here, :] = total
            return carry

        lax.fori_loop(0, ny * nx * (height // step), body, 0)

    def reduce1(self, phase):
        axis = self.order[::-1][phase]
        far = self.place.at(axis, 2)

        def body():
            self.rcopy(phase, 2, far).start()
            self.rcopy(phase, 3, far).start()

        when(self.place.own if axis == "z" else self.reduce_active(phase), body)

    def reduce2(self, phase):
        axis = self.order[::-1][phase]
        left, right = self.place.at(axis, -1), self.place.at(axis, 1)

        def body():
            self.rcopy(phase, 2, right).wait_recv()
            self.add(phase, right, 0, [self.landing(phase, 2)])
            self.rcopy(phase, 0, right).start()
            self.rcopy(phase, 3, left).wait_recv()
            self.add(phase, left, 1, [self.landing(phase, 3)])
            self.rcopy(phase, 1, left).start()

        when(self.place.other if axis == "z" else self.reduce_active(phase), body)

    def reduce3(self, phase, out=None):
        axis = self.order[::-1][phase]
        here = self.place.at(axis)

        def body():
            self.rcopy(phase, 0, here).wait_recv()
            self.rcopy(phase, 1, here).wait_recv()
            self.add(phase, here, None, [self.landing(phase, 0), self.landing(phase, 1)], out)

        when(self.place.own if axis == "z" else self.reduce_active(phase), body)

    def reduce_drain(self):
        for phase in range(3):
            axis = self.order[::-1][phase]
            here = self.place.at(axis)

            def first(phase=phase, here=here):
                self.rcopy(phase, 2, here).wait_send()
                self.rcopy(phase, 3, here).wait_send()

            def second(phase=phase, here=here):
                self.rcopy(phase, 0, here).wait_send()
                self.rcopy(phase, 1, here).wait_send()

            if axis == "z":
                when(self.place.own, first)
                when(self.place.other, second)
            else:
                def both(first=first, second=second):
                    first()
                    second()

                when(self.reduce_active(phase), both)


def reduce_shapes():
    shapes = []
    for name, cols, rows, dtype, order in MATS:
        back = order[::-1]
        for phase in range(3):
            known = set(back[: phase + 1])
            cx, cy, cz = (0 if a in known else None for a in "xyz")
            shapes.append(pltpu.VMEM((2,) + block_shape(cols, rows, cx, cy, cz, False), dtype))
            if back[phase] != "z":
                shapes.append(pltpu.VMEM((2,) + block_shape(cols, rows, cx, cy, cz, True), dtype))
    return shapes


PAIR = 48


def kernel(
    tok, small, inv, wq, wk, wv, wo, wg, wu, wd, cot,
    mixed, tgrad, oq, ok, ov, oo, og, ou, od, on,
    Wq, Wkv, Wo, Wg, Wu, Wd, Wn, *rest,
):
    nbuf = len(reduce_shapes())
    bufs, rest = list(rest[:nbuf]), rest[nbuf:]
    (
        send, grecv, rrecv, lsem, psend, precv,
        st_kv, st_o, st_d, X, H, FG, BG, T, CT, QR, KR, Q, K, V, ATT, BR, HID, ACT, H1, H2,
        COS, SIN, BIAS, ACC, SEND, RECV, TG, TU, GROW, GQK, POSR, DG, GP, GPR, FINC, FINF, FINN, DQ, DK, DV,
    ) = rest
    me = Place()
    c = me.c
    sib = me.sibling()
    mine = pl.multiple_of(c * TOK, TOK)
    theirs = pl.multiple_of((1 - c) * TOK, TOK)
    refs = (Wq, Wkv, Wo, Wg, Wu, Wd, Wn)
    mats = []
    for i, ref in enumerate(refs):
        m = Matrix(i, ref, me, (send, grecv, rrecv))
        m.bufs = []
        for phase in range(3):
            whole = bufs.pop(0)
            half = bufs.pop(0) if m.order[::-1][phase] != "z" else None
            m.bufs.append((whole, half))
        mats.append(m)
    mq, mkv, mo, mg, mu, md, mn = mats

    def pair(k, src, dst):
        return pltpu.make_async_remote_copy(
            src_ref=src, dst_ref=dst, send_sem=psend.at[k], recv_sem=precv.at[k],
            device_id=sib, device_id_type=MESH,
        )

    barrier = pltpu.get_barrier_semaphore()
    for target in [me.step(a, s) for a in "xyz" for s in (1, -1)] + [sib]:
        pl.semaphore_signal(barrier, inc=1, device_id=target, device_id_type=MESH)
    st_kv[:, :128] = wk[...]
    st_kv[:, 128:] = wv[...]
    st_o[...] = wo[...].T
    st_d[...] = wd[...].T
    tok_local = pltpu.make_async_copy(tok, X.at[pl.ds(mine, TOK)], lsem.at[8])
    tok_local.start()
    cot_local = pltpu.make_async_copy(cot, CT, lsem.at[9])
    cot_local.start()
    pl.semaphore_wait(barrier, 7)

    shards = [wq, st_kv, st_o, wg, wu, st_d, small.at[pl.ds(0, 8)]]

    def shard_place(m, core):
        h = m.rows // 2
        return m.ref.at[
            me.yh, me.yl, me.x, pl.ds(pl.multiple_of(core * h, 8), h),
            pl.ds(pl.multiple_of(me.zi * m.cols, 128), m.cols),
        ]

    @pl.when(me.own)
    def _():
        for k, m in enumerate(mats):
            pltpu.make_async_copy(shards[k], shard_place(m, c), lsem.at[k]).start()
        for k, m in enumerate(mats):
            pltpu.make_async_copy(shards[k], shard_place(m, c), lsem.at[k]).wait()
            pair(k, shard_place(m, 1 - c), shard_place(m, 1 - c)).wait_recv()

    @pl.when(me.other)
    def _():
        for k, m in enumerate(mats):
            pair(k, shards[k], shard_place(m, c)).start()
        for k, m in enumerate(mats):
            pair(k, shards[k], shard_place(m, c)).wait_send()

    for m in mats:
        m.gather1(0)
    pos_pair = pair(7, small.at[pl.ds(8, 8)], POSR)
    pos_pair.start()
    tok_pair = pair(8, tok, X.at[pl.ds(mine, TOK)])
    tok_pair.start()
    for m in mats:
        m.gather2(0)
    for m in mats:
        m.gather3(0)
        m.gather1(1)
    for m in mats:
        m.gather2(1)
    for m in mats:
        m.gather3(1)
        m.gather1(2)

    pos_pair.wait()
    lane = lax.broadcasted_iota(jnp.int32, (128, 128), 1)
    row = lax.broadcasted_iota(jnp.int32, (128, 128), 0)
    slots = lax.broadcasted_iota(jnp.int32, (128, 256), 1)
    rows2 = lax.broadcasted_iota(jnp.int32, (128, 256), 0)
    inv_row = jnp.broadcast_to(inv[...][:1], (128, 128))
    for b in range(2):
        for h in range(2):
            mine_row = small[8 + h : 9 + h, :]
            other_row = POSR[h : h + 1, :]
            place_row = jnp.where(c == b, mine_row, other_row)
            places = jnp.broadcast_to(place_row, (128, 128)).T
            angles = places * inv_row
            rs = pl.ds(b * 256 + h * 128, 128)
            COS[rs, :] = jnp.cos(angles)
            sine = jnp.sin(angles)
            SIN[rs, :] = jnp.where(lane < 64, -sine, sine)
            t = rows2 + h * 128
            first = t - jnp.concatenate([places, places], axis=1).astype(jnp.int32)
            allowed = (slots <= t) & (slots >= first)
            BIAS[b, pl.ds(h * 128, 128), :] = jnp.where(allowed, 0.0, -1e30)
    tok_local.wait()
    tok_pair.wait()
    cot_local.wait()

    for m in mats:
        m.gather2(2)
    for m in mats:
        m.gather3(2)

    for j in range(8):
        for r in range(2):
            GROW[r : r + 1, j * 128 : (j + 1) * 128] = (
                Wn[0, j // 4, j % 4, r : r + 1, 0:128] + Wn[0, j // 4, j % 4, 8 + r : 9 + r, 0:128]
            )
    gq = jnp.zeros((8, 128), F32)
    for j in range(8):
        gq = gq + Wn[0, j // 4, j % 4, 0:8, 0:128] + Wn[0, j // 4, j % 4, 8:16, 0:128]
    GQK[...] = gq
    qgain = GQK[2:3, :]
    kgain = GQK[3:4, :]

    def full(ref, f0, cols):
        return ref[f0, :, :, :, cols].reshape(1024, -1)

    def tile(ref, f0, j):
        return ref[f0, lax.div(j, 2), pl.ds(lax.rem(j, 2) * 2, 2), :, :].reshape(256, -1)

    def turn(v):
        return pltpu.roll(v, 64, 1)

    def project(f, carry):
        f0, f1 = lax.div(f, 2), lax.rem(f, 2)
        cols = pl.ds(pl.multiple_of(f1 * 256, 128), 256)
        QR[f] = nn(X[...], full(Wq, f0, cols))
        TG[...] = nn(X[...], full(Wkv, f0, cols))
        KR[f] = TG[:, 0:128]

        def head(n, carry):
            b = n
            rs = pl.ds(pl.multiple_of(b * 256, 256), 256)
            cosine, sine = COS[rs, :], SIN[rs, :]
            for r in range(2):
                v = QR[f, rs, pl.ds(r * 128, 128)]
                v = v * lax.rsqrt(jnp.mean(v * v, axis=-1, keepdims=True) + EPS) * qgain
                Q[f, b, pl.ds(r * 256, 256), :] = (v * cosine + turn(v) * sine).astype(BF)
            v = KR[f, rs, :]
            v = v * lax.rsqrt(jnp.mean(v * v, axis=-1, keepdims=True) + EPS) * kgain
            K[f, b] = (v * cosine + turn(v) * sine).astype(BF)
            V[f, b] = TG[rs, 128:256].astype(BF)
            return carry

        lax.fori_loop(0, 2, head, 0)
        return carry

    lax.fori_loop(0, 4, project, 0)

    scale = HD ** -0.5

    def softmax(f, b, r):
        s = nt(Q[f, b, pl.ds(r * 256, 256), :], K[f, b]) * scale + BIAS[b]
        e = jnp.exp(s - jnp.max(s, axis=-1, keepdims=True))
        return e * (1.0 / jnp.sum(e, axis=-1, keepdims=True))

    def attend(n, carry):
        f, b = lax.div(n, 2), lax.rem(n, 2)
        f0, f1 = lax.div(f, 2), lax.rem(f, 2)
        rs = pl.ds(pl.multiple_of(b * 256, 256), 256)
        for r in range(2):
            p = softmax(f, b, r).astype(BF)
            o = nn(p, V[f, b])
            ATT[f0, rs, pl.ds(pl.multiple_of(f1 * 256 + r * 128, 128), 128)] = o.astype(BF)
        return carry

    lax.fori_loop(0, 8, attend, 0)

    def pair_sum(base, slot, products):
        def one(j, carry):
            cols = pl.ds(pl.multiple_of(j * 256, 256), 256)
            TG[...] = products(j)
            SEND[:, cols] = TG[pl.ds(theirs, TOK), :].astype(BF)
            ACC[:, cols] = TG[pl.ds(mine, TOK), :]
            pair(base + j, SEND.at[:, cols], RECV.at[slot, :, cols]).start()
            return carry

        lax.fori_loop(0, 4, one, 0)

        def done(j, carry):
            cols = pl.ds(pl.multiple_of(j * 256, 256), 256)
            pair(base + j, SEND.at[:, cols], RECV.at[slot, :, cols]).wait()
            return carry

        lax.fori_loop(0, 4, done, 0)

    CH = 32
    PER = TOK // CH // 4

    def rows_then_send(base, dst, body):
        def piece(j):
            rs = pl.ds(pl.multiple_of(mine + j * 64, 64), 64)
            return pair(base + j, dst.at[rs], dst.at[rs])

        def theirs_piece(j):
            rs = pl.ds(pl.multiple_of(theirs + j * 64, 64), 64)
            return pair(base + j, dst.at[rs], dst.at[rs])

        def outer(j, carry):
            def inner(i, carry):
                at = pl.multiple_of(j * 64 + i * CH, CH)
                body(pl.ds(at, CH), pl.ds(pl.multiple_of(mine + at, CH), CH))
                return carry

            lax.fori_loop(0, PER, inner, 0)
            piece(j).start()
            return carry

        lax.fori_loop(0, 4, outer, 0)

        def done(j, carry):
            piece(j).wait_send()
            theirs_piece(j).wait_recv()
            return carry

        lax.fori_loop(0, 4, done, 0)

    pair_sum(9, 0, lambda j: nt(ATT[0], tile(Wo, 0, j)) + nt(ATT[1], tile(Wo, 1, j)))

    def hidden_rows(rs, abs_rs):
        v = ACC[rs, :] + RECV[0, rs, :].astype(F32)
        BR[rs, :] = v
        n = v * lax.rsqrt(jnp.mean(v * v, axis=-1, keepdims=True) + EPS) * GROW[0:1, :]
        hid = X[abs_rs, :].astype(F32) + n
        HID[rs, :] = hid
        H[abs_rs, :] = hid.astype(BF)

    rows_then_send(13, H, hidden_rows)

    def ffn_tile(n, carry):
        f0 = lax.div(n, 3)
        cols = pl.ds(pl.multiple_of(lax.rem(n, 3) * 256, 256), 256)
        TG[...] = nn(H[...], full(Wg, f0, cols))
        TU[...] = nn(H[...], full(Wu, f0, cols))

        def rowsof(i, carry):
            rs = pl.ds(pl.multiple_of(i * 64, 64), 64)
            g, u = TG[rs, :], TU[rs, :]
            s = 1.0 / (1.0 + jnp.exp(-g))
            silu = g * s
            ACT[f0, rs, cols] = (silu * u).astype(BF)
            H1[f0, rs, cols] = (s * (1.0 + g * (1.0 - s)) * u).astype(BF)
            H2[f0, rs, cols] = silu.astype(BF)
            return carry

        lax.fori_loop(0, 8, rowsof, 0)
        return carry

    lax.fori_loop(0, 6, ffn_tile, 0)
    pair_sum(17, 1, lambda j: nt(ACT[0], tile(Wd, 0, j)) + nt(ACT[1], tile(Wd, 1, j)))

    DG[...] = jnp.zeros_like(DG)

    def rms_back(v, gain, dn, at):
        r = lax.rsqrt(jnp.mean(v * v, axis=-1, keepdims=True) + EPS)
        gd = gain * dn
        vr = v * r
        grad = r * (gd - vr * jnp.mean(gd * vr, axis=-1, keepdims=True))
        dg = dn * vr
        DG[at, :, :] += jnp.sum(dg.reshape(CH // 8, 8, 1024), axis=0)
        return grad

    def ffn_rows(rs, abs_rs):
        v = ACC[rs, :] + RECV[1, rs, :].astype(F32)
        gain = GROW[1:2, :]
        r = lax.rsqrt(jnp.mean(v * v, axis=-1, keepdims=True) + EPS)
        mixed[rs, :] = (HID[rs, :] + v * r * gain).astype(BF)
        FG[abs_rs, :] = rms_back(v, gain, CT[rs, :].astype(F32), 1).astype(BF)

    rows_then_send(21, FG, ffn_rows)

    def transpose_to(src):
        def one(j, carry):
            cols = pl.ds(pl.multiple_of(j * 128, 128), 128)
            T[cols, :] = src[:, cols].T
            return carry

        lax.fori_loop(0, 8, one, 0)

    for m in mats:
        m.gather_drain()

    def weight_grad(ref, f0, cols, rhs):
        def one(j, carry):
            rs = pl.ds(pl.multiple_of(j * 512, 512), 512)
            out = nn(T[rs, :], rhs()).astype(BF)
            ref[f0, j, :, :, cols] = out.reshape(4, 128, out.shape[-1])
            return carry

        lax.fori_loop(0, 2, one, 0)

    transpose_to(FG)

    def ffn_back_tile(n, carry):
        f0 = lax.div(n, 3)
        cols = pl.ds(pl.multiple_of(lax.rem(n, 3) * 256, 256), 256)
        TG[...] = nn(FG[...], full(Wd, f0, cols))

        def rowsof(i, carry):
            rs = pl.ds(pl.multiple_of(i * 64, 64), 64)
            da = TG[rs, :]
            H1[f0, rs, cols] = (da * H1[f0, rs, cols].astype(F32)).astype(BF)
            H2[f0, rs, cols] = (da * H2[f0, rs, cols].astype(F32)).astype(BF)
            return carry

        lax.fori_loop(0, 8, rowsof, 0)
        weight_grad(Wd, f0, cols, lambda: ACT[f0, :, cols])
        return carry

    lax.fori_loop(0, 6, ffn_back_tile, 0)
    md.reduce1(0)

    pair_sum(
        25, 0,
        lambda j: (nt(H1[0], tile(Wg, 0, j)) + nt(H1[1], tile(Wg, 1, j)))
        + (nt(H2[0], tile(Wu, 0, j)) + nt(H2[1], tile(Wu, 1, j))),
    )
    transpose_to(H)

    def gate_up_grad(n, carry):
        f0 = lax.div(n, 3)
        cols = pl.ds(pl.multiple_of(lax.rem(n, 3) * 256, 256), 256)
        weight_grad(Wg, f0, cols, lambda: H1[f0, :, cols])
        weight_grad(Wu, f0, cols, lambda: H2[f0, :, cols])
        return carry

    lax.fori_loop(0, 6, gate_up_grad, 0)
    mg.reduce1(0)
    mu.reduce1(0)
    md.reduce2(0)

    def branch_rows(rs, abs_rs):
        dn = CT[rs, :].astype(F32) + ACC[rs, :] + RECV[0, rs, :].astype(F32)
        HID[rs, :] = dn
        BG[abs_rs, :] = rms_back(BR[rs, :], GROW[0:1, :], dn, 0).astype(BF)

    rows_then_send(29, BG, branch_rows)
    mg.reduce2(0)
    mu.reduce2(0)

    transpose_to(BG)
    DO = FG

    def out_grad(f, carry):
        f0, f1 = lax.div(f, 2), lax.rem(f, 2)
        cols = pl.ds(pl.multiple_of(f1 * 256, 256), 256)
        DO[:, pl.ds(pl.multiple_of(f * 256, 256), 256)] = nn(BG[...], full(Wo, f0, cols)).astype(BF)
        weight_grad(Wo, f0, cols, lambda: ATT[f0, :, cols])
        return carry

    lax.fori_loop(0, 4, out_grad, 0)
    mo.reduce1(0)
    md.reduce3(0)
    md.reduce1(1)

    GP[...] = jnp.zeros_like(GP)

    def head_back(raw, gain, dn, cosine, sine, row_at):
        d = dn * cosine - turn(dn) * sine
        r = lax.rsqrt(jnp.mean(raw * raw, axis=-1, keepdims=True) + EPS)
        gd = gain * d
        vr = raw * r
        GP[pl.ds(row_at, 8), :] += jnp.sum((d * vr).reshape(32, 8, 128), axis=0)
        return (r * (gd - vr * jnp.mean(gd * vr, axis=-1, keepdims=True))).astype(BF)

    QG, KVG = ACT, H1

    def attend_back(n, carry):
        f, b = lax.div(n, 2), lax.rem(n, 2)
        f0, f1 = lax.div(f, 2), lax.rem(f, 2)
        rs = pl.ds(pl.multiple_of(b * 256, 256), 256)
        for r in range(2):
            p = softmax(f, b, r)
            do = DO[rs, pl.ds(pl.multiple_of(f * 256 + r * 128, 128), 128)]
            dp = nt(do, V[f, b])
            ds = (p * (dp - jnp.sum(p * dp, axis=-1, keepdims=True))).astype(BF)
            q = Q[f, b, pl.ds(r * 256, 256), :]
            dv = tn(p.astype(BF), do)
            dk = tn(ds, q)
            DQ[r] = nn(ds, K[f, b]) * scale
            if r == 0:
                DV[...] = dv
                DK[...] = dk
            else:
                DV[...] += dv
                DK[...] += dk
        cosine, sine = COS[rs, :], SIN[rs, :]
        at = pl.multiple_of(f1 * 256, 256)
        for r in range(2):
            QG[f0, rs, pl.ds(pl.multiple_of(at + r * 128, 128), 128)] = head_back(
                QR[f, rs, pl.ds(r * 128, 128)], qgain, DQ[r], cosine, sine, 0
            )
        KVG[f0, rs, pl.ds(at, 128)] = head_back(
            KR[f, rs, :], kgain, DK[...] * scale, cosine, sine, 8
        )
        KVG[f0, rs, pl.ds(pl.multiple_of(at + 128, 128), 128)] = DV[...].astype(BF)
        return carry

    lax.fori_loop(0, 8, attend_back, 0)
    mg.reduce3(0)
    mg.reduce1(1)
    mu.reduce3(0)
    mu.reduce1(1)
    mo.reduce2(0)
    md.reduce2(1)

    pair_sum(
        33, 1,
        lambda j: (nt(QG[0, :, 0:512], tile(Wq, 0, j)) + nt(QG[1, :, 0:512], tile(Wq, 1, j)))
        + (nt(KVG[0, :, 0:512], tile(Wkv, 0, j)) + nt(KVG[1, :, 0:512], tile(Wkv, 1, j))),
    )
    transpose_to(X)

    def qkv_grad(f, carry):
        f0, f1 = lax.div(f, 2), lax.rem(f, 2)
        cols = pl.ds(pl.multiple_of(f1 * 256, 256), 256)
        weight_grad(Wq, f0, cols, lambda: QG[f0, :, cols])
        weight_grad(Wkv, f0, cols, lambda: KVG[f0, :, cols])
        return carry

    lax.fori_loop(0, 4, qkv_grad, 0)
    mq.reduce1(0)
    mkv.reduce1(0)

    def gain_rows(at, row_at):
        total = jnp.sum(DG[at], axis=0, keepdims=True)
        for j in range(8):
            GP[row_at + j : row_at + j + 1, :] = total[:, j * 128 : (j + 1) * 128]

    qsum = jnp.sum(GP[0:8, :], axis=0, keepdims=True)
    ksum = jnp.sum(GP[8:16, :], axis=0, keepdims=True)
    gain_rows(0, 16)
    gain_rows(1, 24)
    GP[0:1, :] = qsum
    GP[8:9, :] = ksum
    gain_pair = pair(37, GP, GPR)
    gain_pair.start()

    def out_rows(i, carry):
        rs = pl.ds(pl.multiple_of(i * CH, CH), CH)
        tgrad[rs, :] = HID[rs, :] + ACC[rs, :] + RECV[1, rs, :].astype(F32)
        return carry

    lax.fori_loop(0, TOK // CH, out_rows, 0)
    gain_pair.wait()
    GPR[...] += GP[...]
    Wn[...] = jnp.zeros_like(Wn)
    for j in range(8):
        for f0 in range(2):
            for f1 in range(2):
                cols = slice(f1 * 128, (f1 + 1) * 128)
                Wn[f0, j // 4, j % 4, 0:1, cols] = GPR[16 + j : 17 + j, :]
                Wn[f0, j // 4, j % 4, 1:2, cols] = GPR[24 + j : 25 + j, :]
                Wn[f0, j // 4, j % 4, 8:9, cols] = GPR[0:1, :]
                Wn[f0, j // 4, j % 4, 9:10, cols] = GPR[8:9, :]
    mn.reduce1(0)

    mq.reduce2(0)
    mkv.reduce2(0)
    mn.reduce2(0)
    for m in (mo, mq, mkv, mn):
        m.reduce3(0)
        m.reduce1(1)
    for m in (mg, mu, mo, mq, mkv, mn):
        m.reduce2(1)
    for m in (md, mg, mu, mo, mq, mkv, mn):
        m.reduce3(1)
        m.reduce1(2)
    for m in (md, mg, mu, mo, mq, mkv, mn):
        m.reduce2(2)

    fins = {m.name: (FINC.at[k] if k < 3 else FINF.at[k - 3]) for k, m in enumerate(mats[:6])}
    fins["n"] = FINN

    def fin_rows(m, core):
        if m.name == "n":
            return fins["n"]
        return fins[m.name].at[pl.ds(pl.multiple_of(core * 64, 64), 64)]

    order = (md, mg, mu, mo, mq, mkv, mn)
    for m in order:
        m.reduce3(2, out=fins[m.name])

        @pl.when(me.own)
        def _(m=m):
            pair(38 + m.number, fin_rows(m, 1 - c), fin_rows(m, 1 - c)).start()

    for m in order:

        @pl.when(me.own)
        def _(m=m):
            pair(38 + m.number, fin_rows(m, 1 - c), fin_rows(m, 1 - c)).wait_send()

        @pl.when(me.other)
        def _(m=m):
            pair(38 + m.number, fin_rows(m, c), fin_rows(m, c)).wait_recv()

    mrows = pl.ds(pl.multiple_of(c * 64, 64), 64)
    oq[...] = FINC[0, mrows, :]
    ok[...] = FINC[1, mrows, 0:128]
    ov[...] = FINC[1, mrows, 128:256]
    oo[...] = FINC[2, mrows, :].T
    og[...] = FINF[0, mrows, :]
    ou[...] = FINF[1, mrows, :]
    od[...] = FINF[2, mrows, :].T
    on[...] = FINN[...]
    for m in mats:
        m.reduce_drain()


def on_device(
    tokens, positions, w_query, w_key, w_value, w_out, w_gate, w_up, w_down,
    query_gain, key_gain, attn_gain, ffn_gain, cotangent,
):
    dp = lax.axis_index("dp")
    core = dp % 2
    zeros = jnp.zeros((128,), F32)
    put = lambda v, at: lax.dynamic_update_slice(zeros, v.astype(F32), (at,))
    small = jnp.concatenate(
        [
            jnp.stack(
                [
                    put(attn_gain, core * 64),
                    put(ffn_gain, core * 64),
                    put(query_gain, dp * 8),
                    put(key_gain, dp * 8),
                ]
            ),
            jnp.zeros((4, 128), F32),
            positions.astype(F32).reshape(2, 128),
            jnp.zeros((6, 128), F32),
        ]
    )
    steps_up = np.arange(0, HD, 2).astype(np.float32) / np.float32(HD)
    inverse = (np.float32(ROPE_BASE) ** (-steps_up)).astype(np.float32)
    inv = jnp.asarray(np.tile(np.concatenate([inverse, inverse])[None], (8, 1)))
    vm = pl.BlockSpec(memory_space=pltpu.VMEM)
    hbm = pl.BlockSpec(memory_space=pl.ANY)
    n = 84
    V = pltpu.VMEM
    gathered = [V((2, 2, 4, rows, 2 * cols), dt) for _, cols, rows, dt, _ in MATS]
    sems = [pltpu.SemaphoreType.DMA((n,))] * 3 + [
        pltpu.SemaphoreType.DMA((10,)),
        pltpu.SemaphoreType.DMA((PAIR,)),
        pltpu.SemaphoreType.DMA((PAIR,)),
    ]
    work = [
        V((64, 256), BF), V((64, 256), BF), V((64, 384), BF),
        V((512, D), BF), V((512, D), BF), V((512, D), BF), V((512, D), BF), V((D, 512), BF),
        V((TOK, D), BF),
        V((4, 512, 256), F32), V((4, 512, 128), F32),
        V((4, 2, 512, 128), BF), V((4, 2, 256, 128), BF), V((4, 2, 256, 128), BF),
        V((2, 512, 512), BF),
        V((TOK, D), F32), V((TOK, D), F32),
        V((2, 512, 768), BF), V((2, 512, 768), BF), V((2, 512, 768), BF),
        V((512, 128), F32), V((512, 128), F32), V((2, 256, 256), F32),
        V((TOK, D), F32), V((TOK, D), BF), V((2, TOK, D), BF),
        V((512, 256), F32), V((512, 256), F32),
        V((8, D), F32), V((8, 128), F32), V((8, 128), F32), V((2, 8, D), F32),
        V((32, 128), F32), V((32, 128), F32),
        V((3, 128, 256), F32), V((3, 128, 384), F32), V((16, 128), F32),
        V((2, 256, 128), F32), V((256, 128), F32), V((256, 128), F32),
    ]
    f = lambda *s: jax.ShapeDtypeStruct(s, F32)
    outs = pl.pallas_call(
        kernel,
        out_shape=(
            jax.ShapeDtypeStruct((TOK, D), BF), f(TOK, D),
            f(64, 256), f(64, 128), f(64, 128), f(256, 64), f(64, 384), f(64, 384), f(384, 64),
            f(16, 128),
        ),
        in_specs=[hbm] + [vm] * 9 + [hbm],
        out_specs=[vm] * 10,
        scratch_shapes=gathered + reduce_shapes() + sems + work,
        compiler_params=pltpu.CompilerParams(
            collective_id=1, has_side_effects=True, vmem_limit_bytes=int(63.5 * 2**20)
        ),
        cost_estimate=pl.CostEstimate(flops=26 * 10**9, bytes_accessed=4 * 10**6, transcendentals=0),
    )(tokens, small, inv, w_query, w_key, w_value, w_out, w_gate, w_up, w_down, cotangent)
    mixed, tgrad, gq, gk, gv, go, gg, gu, gd, gn = outs
    cut = lambda r, at, size: lax.dynamic_slice(gn[r], (at,), (size,))
    return (
        mixed, tgrad, gq, gk, gv, go, gg, gu, gd,
        cut(8, dp * 8, 8), cut(9, dp * 8, 8), cut(0, core * 64, 64), cut(1, core * 64, 64),
    )


def solution(mesh):
    both, w, wt = P(("dp", "fsdp"), None), P("dp", "fsdp"), P("fsdp", "dp")
    return jax.shard_map(
        on_device,
        mesh=mesh,
        in_specs=(both, P(("dp", "fsdp")), w, w, w, wt, w, w, wt, P("dp"), P("dp"), P("dp"), P("dp"), both),
        out_specs=(both, both, w, w, w, wt, w, w, wt, P("dp"), P("dp"), P("dp"), P("dp")),
        check_vma=False,
    )
```

```python
import math

import numpy as np
import jax
import jax.numpy as jnp
from jax import lax
from jax.experimental import pallas as pl
from jax.experimental.pallas import tpu as pltpu
from jax.sharding import PartitionSpec as P

MESH = pl.DeviceIdType.MESH
F32, BF = jnp.float32, jnp.bfloat16
D, HD, TOK = 1024, 128, 256
EPS = 1e-6
ROPE_BASE = 1000000.0
GATHER = ("q0", "q1", "k", "v", "o0", "o1", "g0", "u0", "g1", "u1", "g2", "u2", "d0", "d1", "d2")
REDUCE = ("d0", "d1", "d2", "g0", "u0", "g1", "u1", "g2", "u2", "o0", "o1", "q0", "q1", "k", "v")
ORDERS = ("xyz", "yzx", "zxy")
SHARD = ("q0", "q1", "k", "v", "o0", "o1", "g0", "g1", "g2", "u0", "u1", "u2", "d0", "d1", "d2")
UNIT = {name: i for i, name in enumerate(SHARD)}
NU = len(SHARD)
LATENCY = 2.6


def nn(a, b):
    return jnp.dot(a, b, preferred_element_type=F32)


def nt(a, b):
    return lax.dot_general(a, b, (((1,), (1,)), ((), ())), preferred_element_type=F32)


def tn(a, b):
    return lax.dot_general(a, b, (((0,), (0,)), ((), ())), preferred_element_type=F32)


def when(cond, body):
    if cond is None:
        body()
    else:
        pl.when(cond)(body)


class Place:
    def __init__(self):
        dp, fs = lax.axis_index("dp"), lax.axis_index("fsdp")
        self.c = lax.rem(dp, 2)
        self.x = lax.rem(lax.div(dp, 2), 4)
        self.yl = lax.div(dp, 8)
        self.yh = lax.div(fs, 4)
        self.z = lax.rem(fs, 4)
        self.y = self.yh * 2 + self.yl
        self.zi = lax.div(self.z, 2)
        self.own = lax.rem(self.z, 2) == self.c
        self.other = lax.rem(self.z, 2) != self.c

    def device(self, x, y, z, c):
        return (lax.rem(y, 2) * 8 + x * 2 + c, lax.div(y, 2) * 4 + z)

    def step(self, axis, by):
        go = lambda v: lax.rem(v + (by + 4), 4)
        return self.device(
            go(self.x) if axis == "x" else self.x,
            go(self.y) if axis == "y" else self.y,
            go(self.z) if axis == "z" else self.z,
            self.c,
        )

    def sibling(self):
        return self.device(self.x, self.y, self.z, 1 - self.c)

    def at(self, axis, by=0):
        if axis == "z":
            return lax.div(lax.rem(self.z + (by + 4), 4), 2)
        return lax.rem((self.x if axis == "x" else self.y) + (by + 4), 4)


def block_shape(rows, cx, cy, cz, half):
    lead = (2 if cy is None else 0, 2 if cz is None else 0, 2 if cy is None else 0, 4 if cx is None else 0)
    return tuple(v for v in lead if v) + (rows // 2 if half else rows, 128)


class Unit:
    def __init__(self, number, name, ref, lead, rows, dtype, gorder, rorder, gdirect, rdirect, place, sems, bufs):
        self.number, self.name, self.ref, self.lead = number, name, ref, lead
        self.rows, self.dtype, self.place = rows, dtype, place
        self.gorder, self.rorder = gorder, rorder
        self.gdirect, self.rdirect = gdirect, rdirect
        self.send, self.grecv, self.rrecv = sems
        self.bufs = bufs

    def coords(self, phase, order, v, gather):
        cur, done = order[phase], order[:phase]
        out = []
        for axis in "xyz":
            if axis == cur:
                out.append(v)
            elif (axis in done) == gather:
                out.append(None)
            else:
                out.append(self.place.at(axis))
        return out

    def index(self, cx, cy, cz, half):
        s = slice(None)
        yh, yl = (s, s) if cy is None else (lax.div(cy, 2), lax.rem(cy, 2))
        rr = s if half is None else pl.ds(half * (self.rows // 2), self.rows // 2)
        return self.lead + (yh, s if cz is None else cz, yl, s if cx is None else cx, rr, s)

    def block(self, phase, order, v, half, gather):
        return self.ref.at[self.index(*self.coords(phase, order, v, gather), half)]

    def copy(self, src, dst, phase, kind, axis, recv, by):
        k = (self.number * 3 + phase) * 4 + kind
        return pltpu.make_async_remote_copy(
            src_ref=src,
            dst_ref=dst,
            send_sem=self.send.at[k],
            recv_sem=recv.at[k],
            device_id=self.place.step(axis, by),
            device_id_type=MESH,
        )

    def way(self, kind, direct):
        if direct:
            return None, (1, -1, 2)[kind]
        return (None if kind < 2 else kind - 2), (1 if kind % 2 == 0 else -1)

    def gcopy(self, phase, kind, v):
        half, by = self.way(kind, phase in self.gdirect)
        ref = self.block(phase, self.gorder, v, half, True)
        return self.copy(ref, ref, phase, kind, self.gorder[phase], self.grecv, by)

    def gactive(self, phase, z_side):
        axis = self.gorder[phase]
        if axis == "z":
            return z_side
        return None if "z" in self.gorder[:phase] else self.place.own

    def gather1(self, phase):
        here = self.place.at(self.gorder[phase])

        def body():
            for kind in (0, 1, 2) if phase in self.gdirect else (0, 1):
                self.gcopy(phase, kind, here).start()

        when(self.gactive(phase, self.place.own), body)

    def gather2(self, phase):
        axis = self.gorder[phase]
        left, right = self.place.at(axis, -1), self.place.at(axis, 1)

        def body():
            self.gcopy(phase, 0, left).wait_recv()
            self.gcopy(phase, 2, left).start()
            self.gcopy(phase, 1, right).wait_recv()
            self.gcopy(phase, 3, right).start()

        when(self.gactive(phase, self.place.other), body)

    def gather3(self, phase):
        axis = self.gorder[phase]
        far = self.place.at(axis, 2)
        left, right = self.place.at(axis, -1), self.place.at(axis, 1)

        def near():
            self.gcopy(phase, 0, left).wait_recv()
            self.gcopy(phase, 1, right).wait_recv()

        if phase in self.gdirect:
            when(self.gactive(phase, self.place.other), near)
            when(self.gactive(phase, self.place.own), lambda: self.gcopy(phase, 2, far).wait_recv())
            return

        def body():
            self.gcopy(phase, 2, far).wait_recv()
            self.gcopy(phase, 3, far).wait_recv()

        when(self.gactive(phase, self.place.own), body)

    def gather_drain(self):
        for phase in range(3):
            here = self.place.at(self.gorder[phase])

            def sent(kinds, phase=phase, here=here):
                for kind in kinds:
                    self.gcopy(phase, kind, here).wait_send()

            if phase in self.gdirect:
                when(self.gactive(phase, self.place.own), lambda s=sent: s((0, 1, 2)))
            elif self.gorder[phase] == "z":
                when(self.place.own, lambda s=sent: s((0, 1)))
                when(self.place.other, lambda s=sent: s((2, 3)))
            else:
                when(self.gactive(phase, None), lambda s=sent: s((0, 1, 2, 3)))

    def landing(self, phase, kind):
        whole, half, lead = self.bufs[phase]
        if kind < 2 or phase in self.rdirect:
            return whole.at[lead + (kind,)]
        if self.rorder[phase] == "z":
            dims = len(whole.shape) - len(lead) - 3
            return whole.at[lead + (kind - 2,) + (slice(None),) * dims + (pl.ds(0, self.rows // 2),)]
        return half.at[lead + (kind - 2,)]

    def rcopy(self, phase, kind, v):
        half, by = self.way(kind, phase in self.rdirect)
        return self.copy(
            self.block(phase, self.rorder, v, half, False),
            self.landing(phase, kind),
            phase,
            kind,
            self.rorder[phase],
            self.rrecv,
            by,
        )

    def ractive(self, phase, z_side):
        if self.rorder[phase] == "z":
            return z_side
        return self.place.own if "z" in self.rorder[:phase] else None

    def add(self, phase, v, half, sources, out=None):
        cx, cy, cz = self.coords(phase, self.rorder, v, False)
        height = self.rows if half is None else self.rows // 2
        first = 0 if half is None else half * height
        every = slice(None)
        for yh in (0, 1) if cy is None else (lax.div(cy, 2),):
            for zi in (0, 1) if cz is None else (cz,):
                for yl in (0, 1) if cy is None else (lax.rem(cy, 2),):
                    lead = (yh,) * (cy is None) + (zi,) * (cz is None) + (yl,) * (cy is None)
                    idx = self.lead + (yh, zi, yl, every if cx is None else cx, pl.ds(first, height))
                    if len(sources) == 1 and out is None:
                        self.ref[idx] = self.ref[idx] + sources[0][lead]
                        continue
                    total = self.ref[idx].astype(F32)
                    for src in sources:
                        total = total + src[lead].astype(F32)
                    if out is None:
                        self.ref[idx] = total.astype(self.dtype)
                    else:
                        out[...] = total

    def reduce1(self, phase):
        axis = self.rorder[phase]
        far = self.place.at(axis, 2)
        left, right = self.place.at(axis, -1), self.place.at(axis, 1)

        def body():
            self.rcopy(phase, 2, far).start()
            if phase not in self.rdirect:
                self.rcopy(phase, 3, far).start()

        when(self.ractive(phase, self.place.own), body)
        if phase in self.rdirect:

            def near():
                self.rcopy(phase, 0, right).start()
                self.rcopy(phase, 1, left).start()

            when(self.ractive(phase, self.place.other), near)

    def reduce2(self, phase):
        axis = self.rorder[phase]
        left, right = self.place.at(axis, -1), self.place.at(axis, 1)

        def body():
            self.rcopy(phase, 2, right).wait_recv()
            self.add(phase, right, 0, [self.landing(phase, 2)])
            self.rcopy(phase, 0, right).start()
            self.rcopy(phase, 3, left).wait_recv()
            self.add(phase, left, 1, [self.landing(phase, 3)])
            self.rcopy(phase, 1, left).start()

        when(self.ractive(phase, self.place.other), body)

    def reduce3(self, phase, out=None):
        here = self.place.at(self.rorder[phase])

        def body():
            kinds = (0, 1, 2) if phase in self.rdirect else (0, 1)
            for kind in kinds:
                self.rcopy(phase, kind, here).wait_recv()
            self.add(phase, here, None, [self.landing(phase, kind) for kind in kinds], out)

        when(self.ractive(phase, self.place.own), body)

    def reduce_drain(self):
        for phase in range(3):
            here = self.place.at(self.rorder[phase])

            def sent(kinds, phase=phase, here=here):
                for kind in kinds:
                    self.rcopy(phase, kind, here).wait_send()

            far = (2,) if phase in self.rdirect else (2, 3)
            if self.rorder[phase] == "z":
                when(self.place.own, lambda s=sent, far=far: s(far))
                when(self.place.other, lambda s=sent: s((0, 1)))
            else:
                when(self.ractive(phase, None), lambda s=sent, far=far: s((0, 1) + far))


class Job:
    def __init__(self, steps):
        self.steps = steps
        self.next, self.ready = 0, 0.0

    @property
    def done(self):
        return self.next == len(self.steps)


class Schedule:
    def __init__(self):
        self.now, self.busy, self.jobs = 0.0, dict(x=0.0, y=0.0, z=0.0), []

    def add(self, job):
        job.ready = self.now
        self.jobs.append(job)
        self.poll()

    def emit(self, job):
        body, axis, link, cost = job.steps[job.next]
        body()
        job.next += 1
        self.now += cost
        if axis is not None:
            self.busy[axis] = max(self.now, self.busy[axis]) + link
            job.ready = self.busy[axis] + LATENCY

    def poll(self):
        again = True
        while again:
            again = False
            for job in self.jobs:
                if not job.done and job.ready <= self.now:
                    self.emit(job)
                    again = True

    def tick(self, time):
        self.now += time
        self.poll()

    def need(self, jobs):
        while not all(j.done for j in jobs):
            job = min((j for j in self.jobs if not j.done), key=lambda j: j.ready)
            self.now = max(self.now, job.ready)
            self.emit(job)


def gather_steps(unit, size):
    steps = []
    for phase in range(3):
        axis, share = unit.gorder[phase], size * 5.6 / 4 ** (2 - phase)
        direct = phase in unit.gdirect

        def one(phase=phase):
            if phase:
                unit.gather3(phase - 1)
            unit.gather1(phase)

        steps.append((one, axis, share * (2 if direct else 1), 0.25))
        if not direct:
            steps.append((lambda phase=phase: unit.gather2(phase), axis, share / 2, 0.25))
    steps.append((lambda: unit.gather3(2), None, 0.0, 0.1))
    return steps


def reduce_steps(unit, size, finish):
    steps = []
    for phase in range(3):
        axis, share = unit.rorder[phase], size * 5.6 / 4 ** phase
        cost = size * 0.3 / 4 ** phase
        direct = phase in unit.rdirect

        def one(phase=phase):
            if phase:
                unit.reduce3(phase - 1)
            unit.reduce1(phase)

        steps.append((one, axis, share * (2 if direct else 0.5), 0.2 + (4 * cost if phase else 0)))
        if not direct:
            steps.append((lambda phase=phase: unit.reduce2(phase), axis, share, 0.25 + cost))
    steps.append((finish, None, 0.0, 0.3))
    return steps


ROUNDS = [("".join(reversed(o))) for o in ORDERS]


def rdirect_of(name):
    if name == "n":
        return (0, 1, 2)
    return (1, 2) if REDUCE.index(name) >= 11 else (2,)


def landing_shapes(rows, dtype, many):
    shapes = []
    for k, order in enumerate(ROUNDS if many else ROUNDS[:1]):
        for phase in range(3):
            known = order[: phase + 1]
            c = [0 if a in known else None for a in "xyz"]
            slots = 2 if many and phase == 0 else 3
            lead = (many, slots) if many else (slots,)
            shapes.append(pltpu.VMEM(lead + block_shape(rows, *c, False), dtype))
            if many and phase < 2 and order[phase] != "z":
                shapes.append(pltpu.VMEM((many, 2) + block_shape(rows, *c, True), dtype))
    return shapes


PAIR = 64


def kernel(
    tok, pos, inv, ga, gf, gq, gk, wq, wk, wv, wo, wg, wu, wd, cot,
    mixed, tgrad, fin, on,
    W, Wn, *rest,
):
    rest = list(rest)
    place = Place()
    me = place
    c = me.c
    sib = me.sibling()
    mine = pl.multiple_of(c * TOK, TOK)
    theirs = pl.multiple_of((1 - c) * TOK, TOK)
    bufs = []
    for order in ROUNDS:
        bufs.append([(rest.pop(0), rest.pop(0) if order[p] != "z" and p < 2 else None) for p in range(3)])
    nbufs = [(rest.pop(0), None, ()) for p in range(3)]
    (
        send, grecv, rrecv, lsem, psend, precv,
        X, H, FG, BG, CT, QR, KR, Q, K, VA, ATT, RL, BR, HID, ACT, H1, H2,
        COS, SIN, BIAS, BIAST, ACC, SEND, RECV, MIX, GROW, GQK, SM, POSM, POSR, DG, GP, GPR, FIN, FINN,
    ) = rest

    units = {}
    for i, name in enumerate(SHARD):
        k = REDUCE.index(name)
        units[name] = Unit(
            i, name, W, (i,), 128, BF, ORDERS[GATHER.index(name) % 3], ROUNDS[k % 3],
            (0, 1) if GATHER.index(name) < 3 else (0,), rdirect_of(name), me, (send, grecv, rrecv), [(w, h, (k // 3,)) for w, h in bufs[k % 3]],
        )
    gains = Unit(
        NU, "n", Wn, (), 16, F32, ORDERS[2], ROUNDS[0], (0, 1, 2), rdirect_of("n"), me,
        (send, grecv, rrecv), nbufs,
    )
    every = list(units.values()) + [gains]

    def pair(k, src, dst):
        return pltpu.make_async_remote_copy(
            src_ref=src, dst_ref=dst, send_sem=psend.at[k], recv_sem=precv.at[k],
            device_id=sib, device_id_type=MESH,
        )

    barrier = pltpu.get_barrier_semaphore()
    for target in [me.step(a, s) for a in "xyz" for s in (1, -1, 2)] + [sib]:
        pl.semaphore_signal(barrier, inc=1, device_id=target, device_id_type=MESH)
    tok_local = pltpu.make_async_copy(tok, X.at[pl.ds(mine, TOK)], lsem.at[NU + 1])
    tok_local.start()
    cot_local = pltpu.make_async_copy(cot, CT, lsem.at[NU + 2])
    cot_local.start()
    dp = lax.axis_index("dp")
    SM[...] = jnp.zeros_like(SM)
    SM[0:1, 0:64] = ga[...].astype(F32)
    SM[1:2, 0:64] = gf[...].astype(F32)
    SM[2:3, 0:8] = gq[...].astype(F32)
    SM[3:4, 0:8] = gk[...].astype(F32)
    rows8 = lax.broadcasted_iota(jnp.int32, (8, 128), 0)
    SM[...] = jnp.where(rows8 < 2, pltpu.roll(SM[...], c * 64, 1), pltpu.roll(SM[...], dp * 8, 1))
    POSM[...] = jnp.zeros_like(POSM)
    POSM[0:2, :] = pos[...].astype(F32)
    pl.semaphore_wait(barrier, 10)

    sources = dict(q=wq, k=wk, v=wv, o=wo, g=wg, u=wu, d=wd)

    def shard(unit):
        if unit.name == "n":
            return SM
        part = int(unit.name[1:] or 0)
        return sources[unit.name[0]].at[:, pl.ds(part * 128, 128)]

    def shard_place(unit, core):
        h = unit.rows // 2
        return unit.ref.at[
            unit.lead + (me.yh, me.zi, me.yl, me.x, pl.ds(pl.multiple_of(core * h, 8), h))
        ]

    sequence = [units[n] for n in GATHER[:3]] + [gains] + [units[n] for n in GATHER[3:]]

    @pl.when(me.own)
    def _():
        for u in sequence:
            pltpu.make_async_copy(shard(u), shard_place(u, c), lsem.at[u.number]).start()

    @pl.when(me.other)
    def _():
        for u in sequence:
            pair(u.number, shard(u), shard_place(u, c)).start()

    sched = Schedule()
    jobs = {}
    for u in sequence:

        @pl.when(me.own)
        def _(u=u):
            pltpu.make_async_copy(shard(u), shard_place(u, c), lsem.at[u.number]).wait()
            pair(u.number, shard_place(u, 1 - c), shard_place(u, 1 - c)).wait_recv()

        jobs[u.name] = Job(gather_steps(u, 0.02 if u is gains else 1.0))
        sched.add(jobs[u.name])

    pos_pair = pair(NU + 1, POSM, POSR)
    pos_pair.start()
    tok_pair = pair(NU + 2, tok, X.at[pl.ds(mine, TOK)])
    tok_pair.start()
    sched.tick(0.8)

    @pl.when(me.other)
    def _():
        for u in sequence:
            pair(u.number, shard(u), shard_place(u, c)).wait_send()

    pos_pair.wait()

    lane = lax.broadcasted_iota(jnp.int32, (128, 128), 1)
    slots = lax.broadcasted_iota(jnp.int32, (128, 256), 1)
    rows2 = lax.broadcasted_iota(jnp.int32, (128, 256), 0)
    inv_row = jnp.broadcast_to(inv[...][:1], (128, 128))

    def tables(b, h):
        place_row = jnp.where(c == b, POSM[h : h + 1, :], POSR[h : h + 1, :])
        places = jnp.broadcast_to(place_row, (128, 128)).T
        angles = places * inv_row
        rs = pl.ds(b * 256 + h * 128, 128)
        COS[rs, :] = jnp.cos(angles)
        sine = jnp.sin(angles)
        SIN[rs, :] = jnp.where(lane < 64, -sine, sine)
        t = rows2 + h * 128
        first = t - jnp.concatenate([places, places], axis=1).astype(jnp.int32)
        allowed = (slots <= t) & (slots >= first)
        bias = jnp.where(allowed, 0.0, -1e30)
        BIAS[b, pl.ds(h * 128, 128), :] = bias
        BIAST[b, :, pl.ds(h * 128, 128)] = bias.T

    for b in range(2):
        for h in range(2):
            tables(b, h)
            sched.tick(0.5)
    ones = jnp.ones((256, 128), BF)
    with_ones = lambda f, b: jnp.concatenate([VA[f, b], ones], axis=1)
    tok_local.wait()
    tok_pair.wait()
    cot_local.wait()

    def full(u, yh):
        return [W[UNIT[u], yh, zi].reshape(1024, 128) for zi in range(2)]

    def wide(u):
        return jnp.concatenate(full(u, 0) + full(u, 1), axis=1)

    def tile(names, yh, j):
        at = lambda u, zi: W[UNIT[u], yh, zi, j // 2, pl.ds(j % 2 * 2, 2)].reshape(256, 128)
        return jnp.concatenate([at(u, zi) for u in names for zi in range(2)], axis=1)

    def turn(v):
        return pltpu.roll(v, 64, 1)

    def normed(v, gain, b):
        rs = pl.ds(b * 256, 256)
        v = v * lax.rsqrt(jnp.mean(v * v, axis=-1, keepdims=True) + EPS) * gain
        return (v * COS[rs, :] + turn(v) * SIN[rs, :]).astype(BF)

    sched.need([jobs[n] for n in ("q0", "q1", "k", "n")])
    for j in range(8):
        for r in range(2):
            GROW[r : r + 1, j * 128 : (j + 1) * 128] = (
                Wn[0, 0, j // 4, j % 4, r : r + 1, :] + Wn[0, 0, j // 4, j % 4, 8 + r : 9 + r, :]
            )
    gq = jnp.zeros((8, 128), F32)
    for j in range(8):
        gq = gq + Wn[0, 0, j // 4, j % 4, 0:8, :] + Wn[0, 0, j // 4, j % 4, 8:16, :]
    GQK[...] = gq
    qgain = GQK[2:3, :]
    kgain = GQK[3:4, :]
    sched.tick(0.3)

    for r in range(2):
        raw = nn(X[...], wide("q%d" % r))
        for yh in range(2):
            QR[yh, r] = raw[:, yh * 256 : yh * 256 + 256]
        for yh in range(2):
            for b in range(2):
                for zi in range(2):
                    v = QR[yh, r, pl.ds(b * 256, 256), pl.ds(zi * 128, 128)]
                    Q[yh * 2 + zi, b, pl.ds(r * 256, 256), :] = normed(v, qgain, b)
            sched.tick(0.6)
    raw = nn(X[...], wide("k"))
    for yh in range(2):
        KR[yh] = raw[:, yh * 256 : yh * 256 + 256]
    for yh in range(2):
        for b in range(2):
            for zi in range(2):
                v = KR[yh, pl.ds(b * 256, 256), pl.ds(zi * 128, 128)]
                K[yh * 2 + zi, b] = normed(v, kgain, b)
        sched.tick(0.6)

    sched.need([jobs["v"]])
    raw = nn(X[...], wide("v")).astype(BF)
    for f in range(4):
        for b in range(2):
            VA[f, b] = raw[b * 256 : b * 256 + 256, f * 128 : f * 128 + 128]
    sched.tick(0.8)

    scale = HD ** -0.5
    power = scale * math.log2(math.e)

    def attend(f, b):
        yh, zi = f // 2, f % 2
        rs = pl.ds(b * 256, 256)
        for r in range(2):
            s = nt(Q[f, b, pl.ds(r * 256, 256), :], K[f, b])
            e = jnp.exp2(s * power + BIAS[b]).astype(BF)
            ol = nn(e, with_ones(f, b))
            rl = 1.0 / ol[:, 128:256]
            at = pl.ds(r * 256 + zi * 128, 128)
            ATT[yh, rs, at] = (ol[:, 0:128] * rl).astype(BF)
            RL[yh, rs, at] = rl.astype(BF)

    for f in range(4):
        for b in range(2):
            attend(f, b)
            sched.tick(0.35)

    def pair_piece(base, slot, j):
        cols = pl.ds(j * 256, 256)
        return pair(base + j, SEND.at[:, cols], RECV.at[slot, :, cols])

    def pair_sum(base, slot, products, time):
        def one(rows, j):
            out = None
            for left, names, yh in products:
                p = nt(left(rows), tile(names, yh, j))
                out = p if out is None else out + p
            return out

        for j in range(4):
            SEND[:, pl.ds(j * 256, 256)] = one(pl.ds(theirs, TOK), j).astype(BF)
            pair_piece(base, slot, j).start()
            sched.tick(time / 4)
        for j in range(4):
            ACC[:, pl.ds(j * 256, 256)] = one(pl.ds(mine, TOK), j)
            sched.tick(time / 4)

    def pair_done(base, slot):
        for j in range(4):
            pair_piece(base, slot, j).wait()

    CH = 64

    def rows_then_send(base, dst, body):
        for j in range(TOK // CH):
            rs = pl.ds(pl.multiple_of(mine + j * CH, CH), CH)
            body(pl.ds(j * CH, CH), rs)
            pair(base + j, dst.at[rs], dst.at[rs]).start()
        sched.tick(0.5)

    def rows_done(base, dst):
        for j in range(TOK // CH):
            rs = pl.ds(pl.multiple_of(mine + j * CH, CH), CH)
            pair(base + j, dst.at[rs], dst.at[rs]).wait_send()
            rs = pl.ds(pl.multiple_of(theirs + j * CH, CH), CH)
            pair(base + j, dst.at[rs], dst.at[rs]).wait_recv()

    sched.need([jobs["o0"], jobs["o1"]])

    pair_sum(
        20, 0, [(lambda rows, yh=yh: ATT[yh, rows, :], ("o0", "o1"), yh) for yh in range(2)], 0.8
    )
    pair_done(20, 0)

    def hidden_rows(rs, abs_rs):
        v = ACC[rs, :] + RECV[0, rs, :].astype(F32)
        BR[rs, :] = v
        n = v * lax.rsqrt(jnp.mean(v * v, axis=-1, keepdims=True) + EPS) * GROW[0:1, :]
        hid = X[abs_rs, :].astype(F32) + n
        HID[rs, :] = hid
        H[abs_rs, :] = hid.astype(BF)

    rows_then_send(24, H, hidden_rows)

    def ffn_tile(s, rows):
        h = H[rows, :]
        g = nn(h, wide("g%d" % s))
        u = nn(h, wide("u%d" % s))
        sg = 0.5 * jnp.tanh(0.5 * g) + 0.5
        silu = g * sg
        act = (silu * u).astype(BF)
        h1 = ((sg + silu * (1.0 - sg)) * u).astype(BF)
        h2 = silu.astype(BF)
        for yh in range(2):
            cols, part = pl.ds(s * 256, 256), slice(yh * 256, yh * 256 + 256)
            ACT[yh, rows, cols] = act[:, part]
            H1[yh, rows, cols] = h1[:, part]
            H2[yh, rows, cols] = h2[:, part]

    sched.need([jobs["g0"], jobs["u0"]])
    ffn_tile(0, pl.ds(mine, 256))
    sched.tick(0.75)
    rows_done(24, H)
    ffn_tile(0, pl.ds(theirs, 256))
    sched.tick(0.75)
    for s in (1, 2):
        sched.need([jobs["g%d" % s], jobs["u%d" % s]])
        for m in range(2):
            ffn_tile(s, pl.ds(m * 256, 256))
            sched.tick(0.75)
    sched.need([jobs["d%d" % s] for s in range(3)])
    pair_sum(
        28, 1, [(lambda rows, yh=yh: ACT[yh, rows, :], ("d0", "d1", "d2"), yh) for yh in range(2)], 1.1
    )
    DG[...] = jnp.zeros_like(DG)
    GP[...] = jnp.zeros_like(GP)
    for u in every:
        u.gather_drain()
    pair_done(28, 1)

    def rms_back(v, r, gain, dn, at):
        gd = gain * dn
        vr = v * r
        grad = r * (gd - vr * jnp.mean(gd * vr, axis=-1, keepdims=True))
        dg = dn * vr
        DG[at, :, :] += jnp.sum(dg.reshape(CH // 8, 8, 1024), axis=0)
        return grad

    def ffn_rows(rs, abs_rs):
        v = ACC[rs, :] + RECV[1, rs, :].astype(F32)
        gain = GROW[1:2, :]
        r = lax.rsqrt(jnp.mean(v * v, axis=-1, keepdims=True) + EPS)
        MIX[rs, :] = (HID[rs, :] + v * r * gain).astype(BF)
        FG[abs_rs, :] = rms_back(v, r, gain, CT[rs, :].astype(F32), 1).astype(BF)

    rows_then_send(32, FG, ffn_rows)
    mixed_out = pltpu.make_async_copy(MIX, mixed, lsem.at[0])
    mixed_out.start()

    def weight_grad(u, left, right):
        out = tn(left[...], jnp.concatenate([right(0), right(1)], axis=1)).astype(BF)
        for yh in range(2):
            for zi in range(2):
                at = (yh * 2 + zi) * 128
                W[UNIT[u], yh, zi] = out[:, at : at + 128].reshape(2, 4, 128, 128)

    fin_jobs = []

    def start_reduce(u):
        unit = gains if u == "n" else units[u]
        out = FINN if u == "n" else FIN.at[unit.number]

        def finish():
            unit.reduce3(2, out)

            @pl.when(me.own)
            def _():
                fin_pair(unit, 1 - c).start()

        job = Job(reduce_steps(unit, 0.02 if u == "n" else 1.0, finish))
        fin_jobs.append(job)
        sched.add(job)

    def fin_pair(unit, core):
        if unit.name == "n":
            ref = FINN
        else:
            ref = FIN.at[unit.number, pl.ds(pl.multiple_of(core * 64, 64), 64)]
        return pair(48 + unit.number, ref, ref)

    rows_done(32, FG)
    for s in range(3):
        cols = pl.ds(s * 256, 256)
        for m in range(2):
            rs = pl.ds(m * 256, 256)
            da = nn(FG[rs, :], wide("d%d" % s))
            for yh in range(2):
                part = da[:, yh * 256 : yh * 256 + 256]
                H1[yh, rs, cols] = (part * H1[yh, rs, cols].astype(F32)).astype(BF)
                H2[yh, rs, cols] = (part * H2[yh, rs, cols].astype(F32)).astype(BF)
        weight_grad("d%d" % s, FG, lambda yh: ACT[yh, :, cols])
        sched.tick(1.6)
        start_reduce("d%d" % s)

    pair_sum(
        36, 0,
        [(lambda rows, yh=yh: H1[yh, rows, :], ("g0", "g1", "g2"), yh) for yh in range(2)]
        + [(lambda rows, yh=yh: H2[yh, rows, :], ("u0", "u1", "u2"), yh) for yh in range(2)],
        2.2,
    )

    def gate_up(u):
        cols = pl.ds(int(u[1]) * 256, 256)
        part = H1 if u[0] == "g" else H2
        weight_grad(u, H, lambda yh: part[yh, :, cols])
        sched.tick(0.85)
        start_reduce(u)

    gate_up("g0")
    gate_up("u0")
    pair_done(36, 0)

    def branch_rows(rs, abs_rs):
        dn = CT[rs, :].astype(F32) + ACC[rs, :] + RECV[0, rs, :].astype(F32)
        HID[rs, :] = dn
        v = BR[rs, :]
        r = lax.rsqrt(jnp.mean(v * v, axis=-1, keepdims=True) + EPS)
        BG[abs_rs, :] = rms_back(v, r, GROW[0:1, :], dn, 0).astype(BF)

    rows_then_send(40, BG, branch_rows)
    gate_up("g1")
    gate_up("u1")
    rows_done(40, BG)

    DO = FG
    for r in range(2):
        out = nn(BG[...], wide("o%d" % r)).astype(BF)
        for yh in range(2):
            DO[:, pl.ds(yh * 512 + r * 256, 256)] = out[:, yh * 256 : yh * 256 + 256]
        sched.tick(0.8)
    gate_up("g2")
    gate_up("u2")

    def head_back(raw, gain, d, rs, row_at):
        d = d * COS[rs, :] - turn(d) * SIN[rs, :]
        r = lax.rsqrt(jnp.mean(raw * raw, axis=-1, keepdims=True) + EPS)
        gd = gain * d
        vr = raw * r
        GP[pl.ds(row_at, 8), :] += jnp.sum((d * vr).reshape(32, 8, 128), axis=0)
        return (r * (gd - vr * jnp.mean(gd * vr, axis=-1, keepdims=True))).astype(BF)

    QG, KVG = ACT, H1

    def attend_back(f, b):
        yh, zi = f // 2, f % 2
        rs = pl.ds(b * 256, 256)
        dk, dv = None, None
        for r in range(2):
            at = pl.ds(r * 256 + zi * 128, 128)
            q = Q[f, b, pl.ds(r * 256, 256), :]
            do = DO[rs, pl.ds(yh * 512 + r * 256 + zi * 128, 128)].astype(F32) * RL[yh, rs, at].astype(F32)
            dol = do.astype(BF)
            doa = jnp.concatenate([dol, (-(do * ATT[yh, rs, at].astype(F32))).astype(BF)], axis=1)
            e = jnp.exp2(nt(K[f, b], q) * power + BIAST[b])
            ds = (e * nt(with_ones(f, b), doa)).astype(BF)
            dv_r = nn(e.astype(BF), dol)
            dk_r = nn(ds, q)
            dv = dv_r if dv is None else dv + dv_r
            dk = dk_r if dk is None else dk + dk_r
            dq = tn(ds, K[f, b]) * scale
            QG[yh, rs, at] = head_back(QR[yh, r, rs, pl.ds(zi * 128, 128)], qgain, dq, rs, 0)
        KVG[yh, rs, pl.ds(zi * 128, 128)] = head_back(
            KR[yh, rs, pl.ds(zi * 128, 128)], kgain, dk * scale, rs, 8
        )
        KVG[yh, rs, pl.ds(256 + zi * 128, 128)] = dv.astype(BF)

    for f in range(4):
        for b in range(2):
            attend_back(f, b)
            sched.tick(1.0)
        if f % 2:
            r = f // 2
            weight_grad("o%d" % r, BG, lambda yh, r=r: ATT[yh, :, pl.ds(r * 256, 256)])
            sched.tick(0.85)
            start_reduce("o%d" % r)

    def gain_rows(at, row_at):
        summed = jnp.sum(DG[at], axis=0, keepdims=True)
        for j in range(8):
            GP[row_at + j : row_at + j + 1, :] = summed[:, j * 128 : (j + 1) * 128]

    qsum = jnp.sum(GP[0:8, :], axis=0, keepdims=True)
    ksum = jnp.sum(GP[8:16, :], axis=0, keepdims=True)
    gain_rows(0, 16)
    gain_rows(1, 24)
    GP[0:1, :] = qsum
    GP[8:9, :] = ksum
    gain_pair = pair(NU + 3, GP, GPR)
    gain_pair.start()

    pair_sum(
        44, 1,
        [(lambda rows, yh=yh: QG[yh, rows, pl.ds(0, 512)], ("q0", "q1"), yh) for yh in range(2)]
        + [(lambda rows, yh=yh: KVG[yh, rows, pl.ds(0, 512)], ("k", "v"), yh) for yh in range(2)],
        1.4,
    )
    gain_pair.wait()
    GPR[...] += GP[...]
    Wn[...] = jnp.zeros_like(Wn)
    for j in range(8):
        for f0 in range(2):
            for f1 in range(2):
                Wn[f0, f1, j // 4, j % 4, 0:1, :] = GPR[16 + j : 17 + j, :]
                Wn[f0, f1, j // 4, j % 4, 1:2, :] = GPR[24 + j : 25 + j, :]
                Wn[f0, f1, j // 4, j % 4, 8:9, :] = GPR[0:1, :]
                Wn[f0, f1, j // 4, j % 4, 9:10, :] = GPR[8:9, :]
    start_reduce("n")
    for u, src, at in (("q0", QG, 0), ("q1", QG, 256), ("k", KVG, 0), ("v", KVG, 256)):
        weight_grad(u, X, lambda yh: src[yh, :, pl.ds(at, 256)])
        sched.tick(0.85)
        start_reduce(u)

    pair_done(44, 1)

    for j in range(TOK // CH):
        rs = pl.ds(j * CH, CH)
        HID[rs, :] = HID[rs, :] + ACC[rs, :] + RECV[1, rs, :].astype(F32)
    tgrad_out = pltpu.make_async_copy(HID, tgrad, lsem.at[1])
    tgrad_out.start()
    sched.tick(0.6)

    sched.need(fin_jobs)
    for u in every:

        @pl.when(me.own)
        def _(u=u):
            fin_pair(u, 1 - c).wait_send()

        @pl.when(me.other)
        def _(u=u):
            fin_pair(u, c).wait_recv()

    mrows = pl.ds(pl.multiple_of(c * 64, 64), 64)
    fin_out = pltpu.make_async_copy(FIN.at[:, mrows], fin, lsem.at[2])
    fin_out.start()
    on[...] = FINN[...]
    for u in every:
        u.reduce_drain()
    mixed_out.wait()
    tgrad_out.wait()
    fin_out.wait()


def finish_kernel(mixed_in, tgrad_in, fin, gn, mixed, tgrad, oq, ok, ov, oo, og, ou, od, oqg, okg, oag, ofg, sem):
    dp = lax.axis_index("dp")
    core = lax.rem(dp, 2)
    copies = [(mixed_in, mixed), (tgrad_in, tgrad)]
    targets = dict(q=oq, k=ok, v=ov, o=oo, g=og, u=ou, d=od)
    for i, name in enumerate(SHARD):
        part = int(name[1:] or 0)
        copies.append((fin.at[i], targets[name[0]].at[:, pl.ds(part * 128, 128)]))
    copies = [pltpu.make_async_copy(a, b, sem.at[i]) for i, (a, b) in enumerate(copies)]
    for copy in copies:
        copy.start()
    odd = core == 1
    for ref, row in ((oag, 0), (ofg, 1)):
        v = gn[...]
        v = jnp.where(odd, pltpu.roll(v, 64, 1), v)
        ref[...] = v[row : row + 1, 0:64]
    v = gn[...]
    back = lax.rem(128 - dp * 8, 128)
    v = pltpu.roll(v, back, 1)
    oqg[...] = v[8:9, 0:8]
    okg[...] = v[9:10, 0:8]
    for copy in copies:
        copy.wait()


def on_device(
    tokens, positions, w_query, w_key, w_value, w_out, w_gate, w_up, w_down,
    query_gain, key_gain, attn_gain, ffn_gain, cotangent,
):
    steps_up = np.arange(0, HD, 2).astype(np.float32) / np.float32(HD)
    inverse = (np.float32(ROPE_BASE) ** (-steps_up)).astype(np.float32)
    inv = jnp.asarray(np.tile(np.concatenate([inverse, inverse])[None], (8, 1)))
    vm = pl.BlockSpec(memory_space=pltpu.VMEM)
    hbm = pl.BlockSpec(memory_space=pl.ANY)
    far = pl.BlockSpec(memory_space=pltpu.HBM)
    n = (NU + 1) * 12
    V = pltpu.VMEM
    sems = [pltpu.SemaphoreType.DMA((n,))] * 3 + [
        pltpu.SemaphoreType.DMA((NU + 3,)),
        pltpu.SemaphoreType.DMA((PAIR,)),
        pltpu.SemaphoreType.DMA((PAIR,)),
    ]
    work = [
        V((512, D), BF), V((512, D), BF), V((512, D), BF), V((512, D), BF),
        V((TOK, D), BF),
        V((2, 2, 512, 256), F32), V((2, 512, 256), F32),
        V((4, 2, 512, 128), BF), V((4, 2, 256, 128), BF), V((4, 2, 256, 128), BF),
        V((2, 512, 512), BF), V((2, 512, 512), BF),
        V((TOK, D), F32), V((TOK, D), F32),
        V((2, 512, 768), BF), V((2, 512, 768), BF), V((2, 512, 768), BF),
        V((512, 128), F32), V((512, 128), F32), V((2, 256, 256), F32), V((2, 256, 256), F32),
        V((TOK, D), F32), V((TOK, D), BF), V((2, TOK, D), BF),
        V((TOK, D), BF),
        V((8, D), F32), V((8, 128), F32), V((8, 128), F32), V((8, 128), F32), V((8, 128), F32), V((2, 8, D), F32),
        V((32, 128), F32), V((32, 128), F32),
        V((NU, 128, 128), F32), V((16, 128), F32),
    ]
    f = lambda *s: jax.ShapeDtypeStruct(s, F32)
    main_out = pl.pallas_call(
        kernel,
        out_shape=(jax.ShapeDtypeStruct((TOK, D), BF), f(TOK, D), f(NU, 64, 128), f(16, 128)),
        in_specs=[hbm] + [vm] * 13 + [hbm],
        out_specs=[hbm, hbm, hbm, vm],
        scratch_shapes=[V((NU, 2, 2, 2, 4, 128, 128), BF), V((2, 2, 2, 4, 16, 128), F32)]
        + landing_shapes(128, BF, 5) + landing_shapes(16, F32, 0) + sems + work,
        compiler_params=pltpu.CompilerParams(
            collective_id=1, has_side_effects=True, vmem_limit_bytes=int(63.5 * 2**20)
        ),
        cost_estimate=pl.CostEstimate(flops=26 * 10**9, bytes_accessed=4 * 10**6, transcendentals=0),
    )(
        tokens, positions.reshape(2, 128), inv,
        attn_gain.reshape(1, 64), ffn_gain.reshape(1, 64), query_gain.reshape(1, 8), key_gain.reshape(1, 8),
        w_query, w_key, w_value, w_out.T, w_gate, w_up, w_down.T, cotangent,
    )
    outs = pl.pallas_call(
        finish_kernel,
        out_shape=(
            jax.ShapeDtypeStruct((TOK, D), BF), f(TOK, D),
            f(64, 256), f(64, 128), f(64, 128), f(64, 256), f(64, 384), f(64, 384), f(64, 384),
            f(1, 8), f(1, 8), f(1, 64), f(1, 64),
        ),
        in_specs=[vm] * 4,
        out_specs=[far] * 9 + [vm] * 4,
        scratch_shapes=[pltpu.SemaphoreType.DMA((NU + 2,))],
        compiler_params=pltpu.CompilerParams(vmem_limit_bytes=int(63.5 * 2**20)),
    )(*main_out)
    mixed, tgrad, gq, gk, gv, go, gg, gu, gd, nq, nk, na, nf = outs
    return (
        mixed, tgrad, gq, gk, gv, go.T, gg, gu, gd.T,
        nq.reshape(8), nk.reshape(8), na.reshape(64), nf.reshape(64),
    )


def solution(mesh):
    both, w, wt = P(("dp", "fsdp"), None), P("dp", "fsdp"), P("fsdp", "dp")
    return jax.shard_map(
        on_device,
        mesh=mesh,
        in_specs=(both, P(("dp", "fsdp")), w, w, w, wt, w, w, wt, P("dp"), P("dp"), P("dp"), P("dp"), both),
        out_specs=(both, both, w, w, w, wt, w, w, wt, P("dp"), P("dp"), P("dp"), P("dp")),
        check_vma=False,
    )
```

```python
import math

import numpy as np
import jax
import jax.numpy as jnp
from jax import lax
from jax.experimental import pallas as pl
from jax.experimental.pallas import tpu as pltpu
from jax.sharding import PartitionSpec as P

MESH = pl.DeviceIdType.MESH
F32, BF = jnp.float32, jnp.bfloat16
D, HD, TOK = 1024, 128, 256
EPS = 1e-6
ROPE_BASE = 1000000.0
GATHER = ("q0", "q1", "k", "v", "o0", "o1", "g0", "u0", "g1", "u1", "g2", "u2", "d0", "d1", "d2")
REDUCE = ("d0", "d1", "d2", "g0", "u0", "g1", "u1", "g2", "u2", "o0", "o1", "q0", "q1", "k", "v")
ORDERS = ("xyz", "yzx", "zxy")
SHARD = ("q0", "q1", "k", "v", "o0", "o1", "g0", "g1", "g2", "u0", "u1", "u2", "d0", "d1", "d2")
UNIT = {name: i for i, name in enumerate(SHARD)}
NU = len(SHARD)
LATENCY = 2.6
GATHER_BACKLOG, REDUCE_BACKLOG, AHEAD = 1000.0, 6.0, 2
SPARE = 4
PLACE = dict(
    d0=15, d1=16, d2="d0", g0="d1", u0="d2", g1="g0", u1="u0", g2="g1", u2="u1", o0="g2", o1="u2", q0="o0", q1="o1",
    k=17, v=18,
)


def nn(a, b):
    return jnp.dot(a, b, preferred_element_type=F32)


def nt(a, b):
    return lax.dot_general(a, b, (((1,), (1,)), ((), ())), preferred_element_type=F32)


def tn(a, b):
    return lax.dot_general(a, b, (((0,), (0,)), ((), ())), preferred_element_type=F32)


def when(cond, body):
    if cond is None:
        body()
    else:
        pl.when(cond)(body)


class Place:
    def __init__(self):
        dp, fs = lax.axis_index("dp"), lax.axis_index("fsdp")
        self.c = lax.rem(dp, 2)
        self.x = lax.rem(lax.div(dp, 2), 4)
        self.yl = lax.div(dp, 8)
        self.yh = lax.div(fs, 4)
        self.z = lax.rem(fs, 4)
        self.y = self.yh * 2 + self.yl
        self.zi = lax.div(self.z, 2)
        self.own = lax.rem(self.z, 2) == self.c
        self.other = lax.rem(self.z, 2) != self.c

    def device(self, x, y, z, c):
        return (lax.rem(y, 2) * 8 + x * 2 + c, lax.div(y, 2) * 4 + z)

    def step(self, axis, by):
        go = lambda v: lax.rem(v + (by + 4), 4)
        return self.device(
            go(self.x) if axis == "x" else self.x,
            go(self.y) if axis == "y" else self.y,
            go(self.z) if axis == "z" else self.z,
            self.c,
        )

    def sibling(self):
        return self.device(self.x, self.y, self.z, 1 - self.c)

    def at(self, axis, by=0):
        if axis == "z":
            return lax.div(lax.rem(self.z + (by + 4), 4), 2)
        return lax.rem((self.x if axis == "x" else self.y) + (by + 4), 4)


def block_shape(rows, cx, cy, cz, half):
    lead = (2 if cy is None else 0, 2 if cz is None else 0, 2 if cy is None else 0, 4 if cx is None else 0)
    return tuple(v for v in lead if v) + (rows // 2 if half else rows, 128)


class Unit:
    def __init__(self, number, name, ref, lead, rlead, rows, dtype, gorder, rorder, gdirect, rdirect, place, sems, bufs):
        self.number, self.name, self.ref, self.lead, self.rlead = number, name, ref, lead, rlead
        self.rows, self.dtype, self.place = rows, dtype, place
        self.gorder, self.rorder = gorder, rorder
        self.gdirect, self.rdirect = gdirect, rdirect
        self.send, self.grecv, self.rrecv = sems
        self.bufs = bufs

    def coords(self, phase, order, v, gather):
        cur, done = order[phase], order[:phase]
        out = []
        for axis in "xyz":
            if axis == cur:
                out.append(v)
            elif (axis in done) == gather:
                out.append(None)
            else:
                out.append(self.place.at(axis))
        return out

    def index(self, cx, cy, cz, half):
        s = slice(None)
        yh, yl = (s, s) if cy is None else (lax.div(cy, 2), lax.rem(cy, 2))
        rr = s if half is None else pl.ds(half * (self.rows // 2), self.rows // 2)
        return (yh, s if cz is None else cz, yl, s if cx is None else cx, rr, s)

    def block(self, phase, order, v, half, gather):
        lead = self.lead if gather else self.rlead
        return self.ref.at[lead + self.index(*self.coords(phase, order, v, gather), half)]

    def copy(self, src, dst, phase, kind, axis, recv, by):
        k = (self.number * 3 + phase) * 4 + kind
        return pltpu.make_async_remote_copy(
            src_ref=src,
            dst_ref=dst,
            send_sem=self.send.at[k],
            recv_sem=recv.at[k],
            device_id=self.place.step(axis, by),
            device_id_type=MESH,
        )

    def way(self, kind, direct):
        if direct:
            return None, (1, -1, 2)[kind]
        return (None if kind < 2 else kind - 2), (1 if kind % 2 == 0 else -1)

    def gcopy(self, phase, kind, v):
        half, by = self.way(kind, phase in self.gdirect)
        ref = self.block(phase, self.gorder, v, half, True)
        return self.copy(ref, ref, phase, kind, self.gorder[phase], self.grecv, by)

    def gactive(self, phase, z_side):
        axis = self.gorder[phase]
        if axis == "z":
            return z_side
        return None if "z" in self.gorder[:phase] else self.place.own

    def gather1(self, phase):
        here = self.place.at(self.gorder[phase])

        def body():
            for kind in (0, 1, 2) if phase in self.gdirect else (0, 1):
                self.gcopy(phase, kind, here).start()

        when(self.gactive(phase, self.place.own), body)

    def gather2(self, phase):
        axis = self.gorder[phase]
        left, right = self.place.at(axis, -1), self.place.at(axis, 1)

        def body():
            self.gcopy(phase, 0, left).wait_recv()
            self.gcopy(phase, 2, left).start()
            self.gcopy(phase, 1, right).wait_recv()
            self.gcopy(phase, 3, right).start()

        when(self.gactive(phase, self.place.other), body)

    def gather3(self, phase):
        axis = self.gorder[phase]
        far = self.place.at(axis, 2)
        left, right = self.place.at(axis, -1), self.place.at(axis, 1)

        def near():
            self.gcopy(phase, 0, left).wait_recv()
            self.gcopy(phase, 1, right).wait_recv()

        if phase in self.gdirect:
            when(self.gactive(phase, self.place.other), near)
            when(self.gactive(phase, self.place.own), lambda: self.gcopy(phase, 2, far).wait_recv())
            return

        def body():
            self.gcopy(phase, 2, far).wait_recv()
            self.gcopy(phase, 3, far).wait_recv()

        when(self.gactive(phase, self.place.own), body)

    def gather_drain(self):
        for phase in range(3):
            here = self.place.at(self.gorder[phase])

            def sent(kinds, phase=phase, here=here):
                for kind in kinds:
                    self.gcopy(phase, kind, here).wait_send()

            if phase in self.gdirect:
                when(self.gactive(phase, self.place.own), lambda s=sent: s((0, 1, 2)))
            elif self.gorder[phase] == "z":
                when(self.place.own, lambda s=sent: s((0, 1)))
                when(self.place.other, lambda s=sent: s((2, 3)))
            else:
                when(self.gactive(phase, None), lambda s=sent: s((0, 1, 2, 3)))

    def landing(self, phase, kind):
        whole, half, lead = self.bufs[phase]
        if kind < 2 or phase in self.rdirect:
            return whole.at[lead + (kind,)]
        if self.rorder[phase] == "z":
            dims = len(whole.shape) - len(lead) - 3
            return whole.at[lead + (kind - 2,) + (slice(None),) * dims + (pl.ds(0, self.rows // 2),)]
        return half.at[lead + (kind - 2,)]

    def rcopy(self, phase, kind, v):
        half, by = self.way(kind, phase in self.rdirect)
        return self.copy(
            self.block(phase, self.rorder, v, half, False),
            self.landing(phase, kind),
            phase,
            kind,
            self.rorder[phase],
            self.rrecv,
            by,
        )

    def ractive(self, phase, z_side):
        if self.rorder[phase] == "z":
            return z_side
        return self.place.own if "z" in self.rorder[:phase] else None

    def add(self, phase, v, half, sources, out=None):
        cx, cy, cz = self.coords(phase, self.rorder, v, False)
        height = self.rows if half is None else self.rows // 2
        first = 0 if half is None else half * height
        every = slice(None)
        for yh in (0, 1) if cy is None else (lax.div(cy, 2),):
            for zi in (0, 1) if cz is None else (cz,):
                for yl in (0, 1) if cy is None else (lax.rem(cy, 2),):
                    lead = (yh,) * (cy is None) + (zi,) * (cz is None) + (yl,) * (cy is None)
                    idx = self.rlead + (yh, zi, yl, every if cx is None else cx, pl.ds(first, height))
                    if len(sources) == 1 and out is None:
                        self.ref[idx] = self.ref[idx] + sources[0][lead]
                        continue
                    total = self.ref[idx].astype(F32)
                    for src in sources:
                        total = total + src[lead].astype(F32)
                    if out is None:
                        self.ref[idx] = total.astype(self.dtype)
                    else:
                        out[...] = total

    def reduce1(self, phase):
        axis = self.rorder[phase]
        far = self.place.at(axis, 2)
        left, right = self.place.at(axis, -1), self.place.at(axis, 1)

        def body():
            self.rcopy(phase, 2, far).start()
            if phase not in self.rdirect:
                self.rcopy(phase, 3, far).start()

        when(self.ractive(phase, self.place.own), body)
        if phase in self.rdirect:

            def near():
                self.rcopy(phase, 0, right).start()
                self.rcopy(phase, 1, left).start()

            when(self.ractive(phase, self.place.other), near)

    def reduce2(self, phase):
        axis = self.rorder[phase]
        left, right = self.place.at(axis, -1), self.place.at(axis, 1)

        def body():
            self.rcopy(phase, 2, right).wait_recv()
            self.add(phase, right, 0, [self.landing(phase, 2)])
            self.rcopy(phase, 0, right).start()
            self.rcopy(phase, 3, left).wait_recv()
            self.add(phase, left, 1, [self.landing(phase, 3)])
            self.rcopy(phase, 1, left).start()

        when(self.ractive(phase, self.place.other), body)

    def reduce3(self, phase, out=None):
        here = self.place.at(self.rorder[phase])

        def body():
            kinds = (0, 1, 2) if phase in self.rdirect else (0, 1)
            for kind in kinds:
                self.rcopy(phase, kind, here).wait_recv()
            self.add(phase, here, None, [self.landing(phase, kind) for kind in kinds], out)

        when(self.ractive(phase, self.place.own), body)

    def reduce_drain(self):
        for phase in range(3):
            here = self.place.at(self.rorder[phase])

            def sent(kinds, phase=phase, here=here):
                for kind in kinds:
                    self.rcopy(phase, kind, here).wait_send()

            far = (2,) if phase in self.rdirect else (2, 3)
            if self.rorder[phase] == "z":
                when(self.place.own, lambda s=sent, far=far: s(far))
                when(self.place.other, lambda s=sent: s((0, 1)))
            else:
                when(self.ractive(phase, None), lambda s=sent, far=far: s((0, 1) + far))


class Job:
    def __init__(self, steps, backlog):
        self.steps, self.backlog, self.gate = steps, backlog, None
        self.next, self.ready = 0, 0.0

    @property
    def done(self):
        return self.next == len(self.steps)


class Schedule:
    def __init__(self):
        self.now, self.busy, self.jobs = 0.0, dict(x=0.0, y=0.0, z=0.0), []

    def add(self, job):
        job.ready = self.now
        self.jobs.append(job)
        self.poll()

    def emit(self, job):
        body, axis, link, cost = job.steps[job.next]
        body()
        job.next += 1
        self.now += cost
        if axis is not None:
            self.busy[axis] = max(self.now, self.busy[axis]) + link
            job.ready = self.busy[axis] + LATENCY

    def when(self, job):
        axis = job.steps[job.next][1]
        if job.gate is not None and job.next == job.gate[0] and job.gate[1].next < job.gate[2]:
            return math.inf
        return job.ready if axis is None else max(job.ready, self.busy[axis] - job.backlog)

    def poll(self):
        while True:
            job = next((j for j in self.jobs if not j.done and self.when(j) <= self.now), None)
            if job is None:
                return
            self.emit(job)

    def tick(self, time):
        self.now += time
        self.poll()

    def need(self, jobs):
        while not all(j.done for j in jobs):
            job = min((j for j in self.jobs if not j.done), key=self.when)
            self.now = max(self.now, self.when(job))
            self.emit(job)


def gather_steps(unit, size):
    steps = []
    for phase in range(3):
        axis, share = unit.gorder[phase], size * 5.6 / 4 ** (2 - phase)
        direct = phase in unit.gdirect

        def one(phase=phase):
            if phase:
                unit.gather3(phase - 1)
            unit.gather1(phase)

        steps.append((one, axis, share * (2 if direct else 1), 0.25))
        if not direct:
            steps.append((lambda phase=phase: unit.gather2(phase), axis, share / 2, 0.25))
    steps.append((lambda: unit.gather3(2), None, 0.0, 0.1))
    return steps


def reduce_steps(unit, size, finish):
    steps = []
    for phase in range(3):
        axis, share = unit.rorder[phase], size * 5.6 / 4 ** phase
        cost = size * 0.3 / 4 ** phase
        direct = phase in unit.rdirect

        def one(phase=phase):
            if phase:
                unit.reduce3(phase - 1)
            unit.reduce1(phase)

        steps.append((one, axis, share * (2 if direct else 0.5), 0.2 + (4 * cost if phase else 0)))
        if not direct:
            steps.append((lambda phase=phase: unit.reduce2(phase), axis, share, 0.25 + cost))
    steps.append((finish, None, 0.0, 0.3))
    return steps


ROUNDS = [("".join(reversed(o))) for o in ORDERS]


def slot(name):
    at = PLACE[name]
    return at if isinstance(at, int) else UNIT[at]


def rdirect_of(name):
    if name == "n":
        return (0, 1, 2)
    return (1, 2) if REDUCE.index(name) >= 11 else (2,)


def landing_shapes(rows, dtype, many):
    shapes = []
    for k, order in enumerate(ROUNDS if many else ROUNDS[:1]):
        for phase in range(3):
            known = order[: phase + 1]
            c = [0 if a in known else None for a in "xyz"]
            slots = 2 if many and phase == 0 else 3
            lead = (many, slots) if many else (slots,)
            shapes.append(pltpu.VMEM(lead + block_shape(rows, *c, False), dtype))
            if many and phase < 2 and order[phase] != "z":
                shapes.append(pltpu.VMEM((many, 2) + block_shape(rows, *c, True), dtype))
    return shapes


PAIR = 64


def kernel(
    tok, pos, inv, ga, gf, gq, gk, wq, wk, wv, wo, wg, wu, wd, cot,
    mixed, tgrad, fin, on,
    W, Wn, *rest,
):
    rest = list(rest)
    place = Place()
    me = place
    c = me.c
    sib = me.sibling()
    mine = pl.multiple_of(c * TOK, TOK)
    theirs = pl.multiple_of((1 - c) * TOK, TOK)
    bufs = []
    for order in ROUNDS:
        bufs.append([(rest.pop(0), rest.pop(0) if order[p] != "z" and p < 2 else None) for p in range(3)])
    nbufs = [(rest.pop(0), None, ()) for p in range(3)]
    (
        send, grecv, rrecv, lsem, psend, precv,
        X, H, FG, BG, CT, QR, KR, Q, K, VA, ATT, RL, BR, HID, ACT, H1, H2,
        COS, SIN, BIAS, ACC, SEND, RECV, MIX, GROW, GQK, SM, POSM, POSR, DG, GP, GPR, FIN, FINN,
    ) = rest

    units = {}
    for i, name in enumerate(SHARD):
        k = REDUCE.index(name)
        units[name] = Unit(
            i, name, W, (i,), (slot(name),), 128, BF, ORDERS[GATHER.index(name) % 3], ROUNDS[k % 3],
            (0, 1) if GATHER.index(name) < 3 else (0,), rdirect_of(name), me, (send, grecv, rrecv), [(w, h, (k // 3,)) for w, h in bufs[k % 3]],
        )
    gains = Unit(
        NU, "n", Wn, (), (), 16, F32, ORDERS[2], ROUNDS[0], (0, 1, 2), rdirect_of("n"), me,
        (send, grecv, rrecv), nbufs,
    )
    every = list(units.values()) + [gains]

    def pair(k, src, dst):
        return pltpu.make_async_remote_copy(
            src_ref=src, dst_ref=dst, send_sem=psend.at[k], recv_sem=precv.at[k],
            device_id=sib, device_id_type=MESH,
        )

    barrier = pltpu.get_barrier_semaphore()
    for target in [me.step(a, s) for a in "xyz" for s in (1, -1, 2)] + [sib]:
        pl.semaphore_signal(barrier, inc=1, device_id=target, device_id_type=MESH)
    tok_local = pltpu.make_async_copy(tok, X.at[pl.ds(mine, TOK)], lsem.at[NU + 1])
    tok_local.start()
    cot_local = pltpu.make_async_copy(cot, CT, lsem.at[NU + 2])
    cot_local.start()
    dp = lax.axis_index("dp")
    SM[...] = jnp.zeros_like(SM)
    SM[0:1, 0:64] = ga[...].astype(F32)
    SM[1:2, 0:64] = gf[...].astype(F32)
    SM[2:3, 0:8] = gq[...].astype(F32)
    SM[3:4, 0:8] = gk[...].astype(F32)
    rows8 = lax.broadcasted_iota(jnp.int32, (8, 128), 0)
    SM[...] = jnp.where(rows8 < 2, pltpu.roll(SM[...], c * 64, 1), pltpu.roll(SM[...], dp * 8, 1))
    POSM[...] = jnp.zeros_like(POSM)
    POSM[0:2, :] = pos[...].astype(F32)
    pl.semaphore_wait(barrier, 10)

    sources = dict(q=wq, k=wk, v=wv, o=wo, g=wg, u=wu, d=wd)

    def shard(unit):
        if unit.name == "n":
            return SM
        part = int(unit.name[1:] or 0)
        return sources[unit.name[0]].at[:, pl.ds(part * 128, 128)]

    def shard_place(unit, core):
        h = unit.rows // 2
        return unit.ref.at[
            unit.lead + (me.yh, me.zi, me.yl, me.x, pl.ds(pl.multiple_of(core * h, 8), h))
        ]

    sequence = [units[n] for n in GATHER[:3]] + [gains] + [units[n] for n in GATHER[3:]]

    @pl.when(me.own)
    def _():
        for u in sequence:
            pltpu.make_async_copy(shard(u), shard_place(u, c), lsem.at[u.number]).start()

    @pl.when(me.other)
    def _():
        for u in sequence:
            pair(u.number, shard(u), shard_place(u, c)).start()

    sched = Schedule()
    jobs = {}
    for u in sequence:

        @pl.when(me.own)
        def _(u=u):
            pltpu.make_async_copy(shard(u), shard_place(u, c), lsem.at[u.number]).wait()
            pair(u.number, shard_place(u, 1 - c), shard_place(u, 1 - c)).wait_recv()

        jobs[u.name] = Job(gather_steps(u, 0.02 if u is gains else 1.0), GATHER_BACKLOG)
        at = GATHER.index(u.name) - 3 * AHEAD if u is not gains else -1
        if at >= 0:
            before = jobs[GATHER[at]]
            jobs[u.name].gate = (len(jobs[u.name].steps) - 3, before, len(before.steps) - 1)
        sched.add(jobs[u.name])

    pos_pair = pair(NU + 1, POSM, POSR)
    pos_pair.start()
    tok_pair = pair(NU + 2, tok, X.at[pl.ds(mine, TOK)])
    tok_pair.start()
    sched.tick(0.8)

    @pl.when(me.other)
    def _():
        for u in sequence:
            pair(u.number, shard(u), shard_place(u, c)).wait_send()

    pos_pair.wait()

    lane = lax.broadcasted_iota(jnp.int32, (128, 128), 1)
    slots = lax.broadcasted_iota(jnp.int32, (128, 256), 1)
    rows2 = lax.broadcasted_iota(jnp.int32, (128, 256), 0)
    inv_row = jnp.broadcast_to(inv[...][:1], (128, 128))

    def tables(b, h):
        place_row = jnp.where(c == b, POSM[h : h + 1, :], POSR[h : h + 1, :])
        places = jnp.broadcast_to(place_row, (128, 128)).T
        angles = places * inv_row
        rs = pl.ds(b * 256 + h * 128, 128)
        COS[rs, :] = jnp.cos(angles)
        sine = jnp.sin(angles)
        SIN[rs, :] = jnp.where(lane < 64, -sine, sine)
        t = rows2 + h * 128
        first = t - jnp.concatenate([places, places], axis=1).astype(jnp.int32)
        allowed = (slots <= t) & (slots >= first)
        bias = jnp.where(allowed, 0.0, -1e30)
        BIAS[b, pl.ds(h * 128, 128), :] = bias

    for b in range(2):
        for h in range(2):
            tables(b, h)
            sched.tick(0.5)
    ones = jnp.ones((256, 128), BF)
    with_ones = lambda f, b: jnp.concatenate([VA[f, b], ones], axis=1)
    tok_local.wait()
    tok_pair.wait()
    cot_local.wait()

    def full(u, yh):
        return [W[UNIT[u], yh, zi].reshape(1024, 128) for zi in range(2)]

    def wide(u):
        return jnp.concatenate(full(u, 0) + full(u, 1), axis=1)

    def tile(names, yh, j):
        at = lambda u, zi: W[UNIT[u], yh, zi, j // 2, pl.ds(j % 2 * 2, 2)].reshape(256, 128)
        return jnp.concatenate([at(u, zi) for u in names for zi in range(2)], axis=1)

    def turn(v):
        return pltpu.roll(v, 64, 1)

    def normed(v, gain, b):
        rs = pl.ds(b * 256, 256)
        v = v * lax.rsqrt(jnp.mean(v * v, axis=-1, keepdims=True) + EPS) * gain
        return (v * COS[rs, :] + turn(v) * SIN[rs, :]).astype(BF)

    sched.need([jobs[n] for n in ("q0", "q1", "k", "n")])
    for j in range(8):
        for r in range(2):
            GROW[r : r + 1, j * 128 : (j + 1) * 128] = (
                Wn[0, 0, j // 4, j % 4, r : r + 1, :] + Wn[0, 0, j // 4, j % 4, 8 + r : 9 + r, :]
            )
    gq = jnp.zeros((8, 128), F32)
    for j in range(8):
        gq = gq + Wn[0, 0, j // 4, j % 4, 0:8, :] + Wn[0, 0, j // 4, j % 4, 8:16, :]
    GQK[...] = gq
    qgain = GQK[2:3, :]
    kgain = GQK[3:4, :]
    sched.tick(0.3)

    def heads(raw):
        for b in range(2):
            for f in range(4):
                yield b, f, raw[b * 256 : b * 256 + 256, f * 128 : f * 128 + 128]

    for r in range(2):
        raw = nn(X[...], wide("q%d" % r))
        for b, f, v in heads(raw):
            QR[f // 2, r, pl.ds(b * 256, 256), pl.ds(f % 2 * 128, 128)] = v.astype(BF)
            Q[f, b, pl.ds(r * 256, 256), :] = normed(v, qgain, b)
        sched.tick(1.2)
    raw = nn(X[...], wide("k"))
    for b, f, v in heads(raw):
        KR[f // 2, pl.ds(b * 256, 256), pl.ds(f % 2 * 128, 128)] = v.astype(BF)
        K[f, b] = normed(v, kgain, b)
    sched.tick(1.2)

    sched.need([jobs["v"]])
    raw = nn(X[...], wide("v")).astype(BF)
    for f in range(4):
        for b in range(2):
            VA[f, b] = raw[b * 256 : b * 256 + 256, f * 128 : f * 128 + 128]
    sched.tick(0.8)

    scale = HD ** -0.5
    power = scale * math.log2(math.e)

    def attend(f, b):
        yh, zi = f // 2, f % 2
        rs = pl.ds(b * 256, 256)
        for r in range(2):
            s = nt(Q[f, b, pl.ds(r * 256, 256), :], K[f, b])
            e = jnp.exp2(s * power + BIAS[b]).astype(BF)
            ol = nn(e, with_ones(f, b))
            rl = 1.0 / ol[:, 128:256]
            at = pl.ds(r * 256 + zi * 128, 128)
            ATT[yh, rs, at] = (ol[:, 0:128] * rl).astype(BF)
            RL[yh, rs, at] = rl.astype(BF)

    for f in range(4):
        for b in range(2):
            attend(f, b)
            sched.tick(0.35)

    for b in range(2):
        BIAS[b] = BIAS[b].T

    def pair_piece(base, slot, j):
        cols = pl.ds(j * 256, 256)
        return pair(base + j, SEND.at[:, cols], RECV.at[slot, :, cols])

    def pair_sum(base, slot, products, time):
        def one(rows, j):
            out = None
            for left, names, yh in products:
                p = nt(left(rows), tile(names, yh, j))
                out = p if out is None else out + p
            return out

        for j in range(4):
            SEND[:, pl.ds(j * 256, 256)] = one(pl.ds(theirs, TOK), j).astype(BF)
            pair_piece(base, slot, j).start()
        sched.tick(time)
        for j in range(4):
            ACC[:, pl.ds(j * 256, 256)] = one(pl.ds(mine, TOK), j)
        sched.tick(time)

    def pair_done(base, slot):
        for j in range(4):
            pair_piece(base, slot, j).wait()

    CH = 64

    def rows_then_send(base, dst, body):
        for j in range(TOK // CH):
            rs = pl.ds(pl.multiple_of(mine + j * CH, CH), CH)
            body(pl.ds(j * CH, CH), rs)
            pair(base + j, dst.at[rs], dst.at[rs]).start()
        sched.tick(0.5)

    def rows_done(base, dst):
        for j in range(TOK // CH):
            rs = pl.ds(pl.multiple_of(mine + j * CH, CH), CH)
            pair(base + j, dst.at[rs], dst.at[rs]).wait_send()
            rs = pl.ds(pl.multiple_of(theirs + j * CH, CH), CH)
            pair(base + j, dst.at[rs], dst.at[rs]).wait_recv()

    sched.need([jobs["o0"], jobs["o1"]])

    pair_sum(
        20, 0, [(lambda rows, yh=yh: ATT[yh, rows, :], ("o0", "o1"), yh) for yh in range(2)], 0.8
    )
    pair_done(20, 0)

    def hidden_rows(rs, abs_rs):
        v = ACC[rs, :] + RECV[0, rs, :].astype(F32)
        BR[rs, :] = v
        n = v * lax.rsqrt(jnp.mean(v * v, axis=-1, keepdims=True) + EPS) * GROW[0:1, :]
        hid = X[abs_rs, :].astype(F32) + n
        HID[rs, :] = hid
        H[abs_rs, :] = hid.astype(BF)

    rows_then_send(24, H, hidden_rows)

    def ffn_tile(s, rows):
        h = H[rows, :]
        g = nn(h, wide("g%d" % s))
        u = nn(h, wide("u%d" % s))
        sg = 0.5 * jnp.tanh(0.5 * g) + 0.5
        silu = g * sg
        act = (silu * u).astype(BF)
        h1 = ((sg + silu * (1.0 - sg)) * u).astype(BF)
        h2 = silu.astype(BF)
        for yh in range(2):
            cols, part = pl.ds(s * 256, 256), slice(yh * 256, yh * 256 + 256)
            ACT[yh, rows, cols] = act[:, part]
            H1[yh, rows, cols] = h1[:, part]
            H2[yh, rows, cols] = h2[:, part]

    sched.need([jobs["g0"], jobs["u0"]])
    ffn_tile(0, pl.ds(mine, 256))
    sched.tick(0.75)
    rows_done(24, H)
    ffn_tile(0, pl.ds(theirs, 256))
    sched.tick(0.75)
    for s in (1, 2):
        sched.need([jobs["g%d" % s], jobs["u%d" % s]])
        for m in range(2):
            ffn_tile(s, pl.ds(m * 256, 256))
            sched.tick(0.75)
    for u in every:
        if u.name[0] != "d":
            u.gather_drain()
    sched.need([jobs["d%d" % s] for s in range(3)])
    pair_sum(
        28, 1, [(lambda rows, yh=yh: ACT[yh, rows, :], ("d0", "d1", "d2"), yh) for yh in range(2)], 1.1
    )
    DG[...] = jnp.zeros_like(DG)
    GP[...] = jnp.zeros_like(GP)
    for n in ("d0", "d1", "d2"):
        units[n].gather_drain()
    pair_done(28, 1)

    def rms_back(v, r, gain, dn, at):
        gd = gain * dn
        vr = v * r
        grad = r * (gd - vr * jnp.mean(gd * vr, axis=-1, keepdims=True))
        dg = dn * vr
        DG[at, :, :] += jnp.sum(dg.reshape(CH // 8, 8, 1024), axis=0)
        return grad

    def ffn_rows(rs, abs_rs):
        v = ACC[rs, :] + RECV[1, rs, :].astype(F32)
        gain = GROW[1:2, :]
        r = lax.rsqrt(jnp.mean(v * v, axis=-1, keepdims=True) + EPS)
        MIX[rs, :] = (HID[rs, :] + v * r * gain).astype(BF)
        FG[abs_rs, :] = rms_back(v, r, gain, CT[rs, :].astype(F32), 1).astype(BF)

    rows_then_send(32, FG, ffn_rows)
    mixed_out = pltpu.make_async_copy(MIX, mixed, lsem.at[0])
    mixed_out.start()

    def weight_grad(u, left, right):
        out = tn(left[...], jnp.concatenate([right(0), right(1)], axis=1)).astype(BF)
        for yh in range(2):
            for zi in range(2):
                at = (yh * 2 + zi) * 128
                W[slot(u), yh, zi] = out[:, at : at + 128].reshape(2, 4, 128, 128)

    fin_jobs = []

    def start_reduce(u):
        unit = gains if u == "n" else units[u]
        out = FINN if u == "n" else FIN.at[unit.number]

        def finish():
            unit.reduce3(2, out)

            @pl.when(me.own)
            def _():
                fin_pair(unit, 1 - c).start()

            unit.reduce_drain()

        job = Job(reduce_steps(unit, 0.02 if u == "n" else 1.0, finish), REDUCE_BACKLOG)
        fin_jobs.append(job)
        sched.add(job)

    def fin_pair(unit, core):
        if unit.name == "n":
            ref = FINN
        else:
            ref = FIN.at[unit.number, pl.ds(pl.multiple_of(core * 64, 64), 64)]
        return pair(48 + unit.number, ref, ref)

    rows_done(32, FG)

    def act_back(s):
        cols = pl.ds(s * 256, 256)
        for m in range(2):
            rs = pl.ds(m * 256, 256)
            da = nn(FG[rs, :], wide("d%d" % s))
            for yh in range(2):
                part = da[:, yh * 256 : yh * 256 + 256]
                H1[yh, rs, cols] = (part * H1[yh, rs, cols].astype(F32)).astype(BF)
                H2[yh, rs, cols] = (part * H2[yh, rs, cols].astype(F32)).astype(BF)
        sched.tick(0.85)

    def down(u):
        weight_grad(u, FG, lambda yh: ACT[yh, :, pl.ds(int(u[1]) * 256, 256)])
        sched.tick(0.85)
        start_reduce(u)

    def gate_up(u):
        cols = pl.ds(int(u[1]) * 256, 256)
        part = H1 if u[0] == "g" else H2
        weight_grad(u, H, lambda yh: part[yh, :, cols])
        sched.tick(0.85)
        start_reduce(u)

    down("d0")
    down("d1")
    act_back(0)
    down("d2")
    act_back(1)
    gate_up("g0")
    act_back(2)
    gate_up("u0")
    pair_sum(
        36, 0,
        [(lambda rows, yh=yh: H1[yh, rows, :], ("g0", "g1", "g2"), yh) for yh in range(2)]
        + [(lambda rows, yh=yh: H2[yh, rows, :], ("u0", "u1", "u2"), yh) for yh in range(2)],
        2.2,
    )
    gate_up("g1")
    gate_up("u1")
    pair_done(36, 0)

    def branch_rows(rs, abs_rs):
        dn = CT[rs, :].astype(F32) + ACC[rs, :] + RECV[0, rs, :].astype(F32)
        HID[rs, :] = dn
        v = BR[rs, :]
        r = lax.rsqrt(jnp.mean(v * v, axis=-1, keepdims=True) + EPS)
        BG[abs_rs, :] = rms_back(v, r, GROW[0:1, :], dn, 0).astype(BF)

    rows_then_send(40, BG, branch_rows)
    gate_up("g2")
    gate_up("u2")
    rows_done(40, BG)

    DO = FG
    for r in range(2):
        out = nn(BG[...], wide("o%d" % r)).astype(BF)
        for yh in range(2):
            DO[:, pl.ds(yh * 512 + r * 256, 256)] = out[:, yh * 256 : yh * 256 + 256]
        sched.tick(0.8)
    for r in range(2):
        weight_grad("o%d" % r, BG, lambda yh: ATT[yh, :, pl.ds(r * 256, 256)])
        sched.tick(0.85)
        start_reduce("o%d" % r)

    def head_back(raw, gain, d, rs, row_at):
        d = d * COS[rs, :] - turn(d) * SIN[rs, :]
        r = lax.rsqrt(jnp.mean(raw * raw, axis=-1, keepdims=True) + EPS)
        gd = gain * d
        vr = raw * r
        gp[row_at] = gp[row_at] + jnp.sum((d * vr).reshape(32, 8, 128), axis=0)
        return (r * (gd - vr * jnp.mean(gd * vr, axis=-1, keepdims=True))).astype(BF)

    QG, KVG = ACT, H1

    gp = [jnp.zeros((8, 128), F32)] * 2

    def attend_back(f, b):
        yh, zi = f // 2, f % 2
        rs = pl.ds(b * 256, 256)
        dk, dv = None, None
        for r in range(2):
            at = pl.ds(r * 256 + zi * 128, 128)
            q = Q[f, b, pl.ds(r * 256, 256), :]
            do = DO[rs, pl.ds(yh * 512 + r * 256 + zi * 128, 128)].astype(F32) * RL[yh, rs, at].astype(F32)
            dol = do.astype(BF)
            doa = jnp.concatenate([dol, (-(do * ATT[yh, rs, at].astype(F32))).astype(BF)], axis=1)
            e = jnp.exp2(nt(K[f, b], q) * power + BIAS[b])
            ds = (e * nt(with_ones(f, b), doa)).astype(BF)
            dv_r = nn(e.astype(BF), dol)
            dk_r = nn(ds, q)
            dv = dv_r if dv is None else dv + dv_r
            dk = dk_r if dk is None else dk + dk_r
            dq = tn(ds, K[f, b]) * scale
            QG[yh, rs, at] = head_back(QR[yh, r, rs, pl.ds(zi * 128, 128)].astype(F32), qgain, dq, rs, 0)
        KVG[yh, rs, pl.ds(zi * 128, 128)] = head_back(
            KR[yh, rs, pl.ds(zi * 128, 128)].astype(F32), kgain, dk * scale, rs, 1
        )
        KVG[yh, rs, pl.ds(256 + zi * 128, 128)] = dv.astype(BF)

    for f in range(4):
        for b in range(2):
            attend_back(f, b)
        sched.tick(1.8)

    def gain_rows(at, row_at):
        summed = jnp.sum(DG[at], axis=0, keepdims=True)
        for j in range(8):
            GP[row_at + j : row_at + j + 1, :] = summed[:, j * 128 : (j + 1) * 128]

    qsum = jnp.sum(gp[0], axis=0, keepdims=True)
    ksum = jnp.sum(gp[1], axis=0, keepdims=True)
    gain_rows(0, 16)
    gain_rows(1, 24)
    GP[0:1, :] = qsum
    GP[8:9, :] = ksum
    gain_pair = pair(NU + 3, GP, GPR)
    gain_pair.start()

    def proj_grad(u, src, at):
        weight_grad(u, X, lambda yh: src[yh, :, pl.ds(at, 256)])
        sched.tick(0.85)
        start_reduce(u)

    proj_grad("q0", QG, 0)
    proj_grad("q1", QG, 256)
    proj_grad("k", KVG, 0)
    proj_grad("v", KVG, 256)
    gain_pair.wait()
    GPR[...] += GP[...]
    Wn[...] = jnp.zeros_like(Wn)
    for j in range(8):
        for f0 in range(2):
            for f1 in range(2):
                Wn[f0, f1, j // 4, j % 4, 0:1, :] = GPR[16 + j : 17 + j, :]
                Wn[f0, f1, j // 4, j % 4, 1:2, :] = GPR[24 + j : 25 + j, :]
                Wn[f0, f1, j // 4, j % 4, 8:9, :] = GPR[0:1, :]
                Wn[f0, f1, j // 4, j % 4, 9:10, :] = GPR[8:9, :]
    start_reduce("n")
    pair_sum(
        44, 1,
        [(lambda rows, yh=yh: QG[yh, rows, pl.ds(0, 512)], ("q0", "q1"), yh) for yh in range(2)]
        + [(lambda rows, yh=yh: KVG[yh, rows, pl.ds(0, 512)], ("k", "v"), yh) for yh in range(2)],
        1.4,
    )
    pair_done(44, 1)

    for j in range(TOK // CH):
        rs = pl.ds(j * CH, CH)
        HID[rs, :] = HID[rs, :] + ACC[rs, :] + RECV[1, rs, :].astype(F32)
    tgrad_out = pltpu.make_async_copy(HID, tgrad, lsem.at[1])
    tgrad_out.start()
    sched.tick(0.6)

    sched.need(fin_jobs)
    for u in every:

        @pl.when(me.own)
        def _(u=u):
            fin_pair(u, 1 - c).wait_send()

        @pl.when(me.other)
        def _(u=u):
            fin_pair(u, c).wait_recv()

    mrows = pl.ds(pl.multiple_of(c * 64, 64), 64)
    fin_out = pltpu.make_async_copy(FIN.at[:, mrows], fin, lsem.at[2])
    fin_out.start()
    on[...] = FINN[...]
    mixed_out.wait()
    tgrad_out.wait()
    fin_out.wait()


def finish_kernel(mixed_in, tgrad_in, fin, gn, mixed, tgrad, oq, ok, ov, oo, og, ou, od, oqg, okg, oag, ofg, sem):
    dp = lax.axis_index("dp")
    core = lax.rem(dp, 2)
    copies = [(mixed_in, mixed), (tgrad_in, tgrad)]
    targets = dict(q=oq, k=ok, v=ov, o=oo, g=og, u=ou, d=od)
    for i, name in enumerate(SHARD):
        part = int(name[1:] or 0)
        copies.append((fin.at[i], targets[name[0]].at[:, pl.ds(part * 128, 128)]))
    copies = [pltpu.make_async_copy(a, b, sem.at[i]) for i, (a, b) in enumerate(copies)]
    for copy in copies:
        copy.start()
    odd = core == 1
    for ref, row in ((oag, 0), (ofg, 1)):
        v = gn[...]
        v = jnp.where(odd, pltpu.roll(v, 64, 1), v)
        ref[...] = v[row : row + 1, 0:64]
    v = gn[...]
    back = lax.rem(128 - dp * 8, 128)
    v = pltpu.roll(v, back, 1)
    oqg[...] = v[8:9, 0:8]
    okg[...] = v[9:10, 0:8]
    for copy in copies:
        copy.wait()


def on_device(
    tokens, positions, w_query, w_key, w_value, w_out, w_gate, w_up, w_down,
    query_gain, key_gain, attn_gain, ffn_gain, cotangent,
):
    steps_up = np.arange(0, HD, 2).astype(np.float32) / np.float32(HD)
    inverse = (np.float32(ROPE_BASE) ** (-steps_up)).astype(np.float32)
    inv = jnp.asarray(np.tile(np.concatenate([inverse, inverse])[None], (8, 1)))
    vm = pl.BlockSpec(memory_space=pltpu.VMEM)
    hbm = pl.BlockSpec(memory_space=pl.ANY)
    far = pl.BlockSpec(memory_space=pltpu.HBM)
    n = (NU + 1) * 12
    V = pltpu.VMEM
    sems = [pltpu.SemaphoreType.DMA((n,))] * 3 + [
        pltpu.SemaphoreType.DMA((NU + 3,)),
        pltpu.SemaphoreType.DMA((PAIR,)),
        pltpu.SemaphoreType.DMA((PAIR,)),
    ]
    work = [
        V((512, D), BF), V((512, D), BF), V((512, D), BF), V((512, D), BF),
        V((TOK, D), BF),
        V((2, 2, 512, 256), BF), V((2, 512, 256), BF),
        V((4, 2, 512, 128), BF), V((4, 2, 256, 128), BF), V((4, 2, 256, 128), BF),
        V((2, 512, 512), BF), V((2, 512, 512), BF),
        V((TOK, D), F32), V((TOK, D), F32),
        V((2, 512, 768), BF), V((2, 512, 768), BF), V((2, 512, 768), BF),
        V((512, 128), F32), V((512, 128), F32), V((2, 256, 256), F32),
        V((TOK, D), F32), V((TOK, D), BF), V((2, TOK, D), BF),
        V((TOK, D), BF),
        V((8, D), F32), V((8, 128), F32), V((8, 128), F32), V((8, 128), F32), V((8, 128), F32), V((2, 8, D), F32),
        V((32, 128), F32), V((32, 128), F32),
        V((NU, 128, 128), F32), V((16, 128), F32),
    ]
    f = lambda *s: jax.ShapeDtypeStruct(s, F32)
    main_out = pl.pallas_call(
        kernel,
        out_shape=(jax.ShapeDtypeStruct((TOK, D), BF), f(TOK, D), f(NU, 64, 128), f(16, 128)),
        in_specs=[hbm] + [vm] * 6 + [hbm] * 8,
        out_specs=[hbm, hbm, hbm, vm],
        scratch_shapes=[V((NU + SPARE, 2, 2, 2, 4, 128, 128), BF), V((2, 2, 2, 4, 16, 128), F32)]
        + landing_shapes(128, BF, 5) + landing_shapes(16, F32, 0) + sems + work,
        compiler_params=pltpu.CompilerParams(
            collective_id=1, has_side_effects=True, vmem_limit_bytes=int(63.5 * 2**20)
        ),
        cost_estimate=pl.CostEstimate(flops=26 * 10**9, bytes_accessed=4 * 10**6, transcendentals=0),
    )(
        tokens, positions.reshape(2, 128), inv,
        attn_gain.reshape(1, 64), ffn_gain.reshape(1, 64), query_gain.reshape(1, 8), key_gain.reshape(1, 8),
        w_query, w_key, w_value, w_out.T, w_gate, w_up, w_down.T, cotangent,
    )
    outs = pl.pallas_call(
        finish_kernel,
        out_shape=(
            jax.ShapeDtypeStruct((TOK, D), BF), f(TOK, D),
            f(64, 256), f(64, 128), f(64, 128), f(64, 256), f(64, 384), f(64, 384), f(64, 384),
            f(1, 8), f(1, 8), f(1, 64), f(1, 64),
        ),
        in_specs=[vm] * 4,
        out_specs=[far] * 9 + [vm] * 4,
        scratch_shapes=[pltpu.SemaphoreType.DMA((NU + 2,))],
        compiler_params=pltpu.CompilerParams(vmem_limit_bytes=int(63.5 * 2**20)),
    )(*main_out)
    mixed, tgrad, gq, gk, gv, go, gg, gu, gd, nq, nk, na, nf = outs
    return (
        mixed, tgrad, gq, gk, gv, go.T, gg, gu, gd.T,
        nq.reshape(8), nk.reshape(8), na.reshape(64), nf.reshape(64),
    )


def solution(mesh):
    both, w, wt = P(("dp", "fsdp"), None), P("dp", "fsdp"), P("fsdp", "dp")
    return jax.shard_map(
        on_device,
        mesh=mesh,
        in_specs=(both, P(("dp", "fsdp")), w, w, w, wt, w, w, wt, P("dp"), P("dp"), P("dp"), P("dp"), both),
        out_specs=(both, both, w, w, w, wt, w, w, wt, P("dp"), P("dp"), P("dp"), P("dp")),
        check_vma=False,
    )
```

```python
import math

import numpy as np
import jax
import jax.numpy as jnp
from jax import lax
from jax.experimental import pallas as pl
from jax.experimental.pallas import tpu as pltpu
from jax.sharding import PartitionSpec as P

MESH = pl.DeviceIdType.MESH
F32, BF = jnp.float32, jnp.bfloat16
D, HD, TOK = 1024, 128, 256
EPS = 1e-6
ROPE_BASE = 1000000.0
GATHER = ("q0", "q1", "k", "v", "o0", "o1", "g0", "u0", "g1", "u1", "g2", "u2", "d0", "d1", "d2")
REDUCE = ("d0", "d1", "d2", "g0", "u0", "g1", "u1", "g2", "u2", "o0", "o1", "q0", "q1", "k", "v")
ORDERS = ("xyz", "yzx", "zxy")
SHARD = ("q0", "q1", "k", "v", "o0", "o1", "g0", "g1", "g2", "u0", "u1", "u2", "d0", "d1", "d2")
UNIT = {name: i for i, name in enumerate(SHARD)}
NU = len(SHARD)
LATENCY, REDUCE_LATENCY = 2.6, 10.0
GATHER_BACKLOG, REDUCE_BACKLOG, AHEAD = 1000.0, 6.0, 2
SPARE = 4
PLACE = dict(
    d0=15, d1=16, d2="d0", g0="d1", u0="d2", g1="g0", u1="u0", g2="g1", u2="u1", o0="g2", o1="u2", q0="o0", q1="o1",
    k=17, v=18,
)


def nn(a, b):
    return jnp.dot(a, b, preferred_element_type=F32)


def nt(a, b):
    return lax.dot_general(a, b, (((1,), (1,)), ((), ())), preferred_element_type=F32)


def tn(a, b):
    return lax.dot_general(a, b, (((0,), (0,)), ((), ())), preferred_element_type=F32)


def when(cond, body):
    if cond is None:
        body()
    else:
        pl.when(cond)(body)


class Place:
    def __init__(self):
        dp, fs = lax.axis_index("dp"), lax.axis_index("fsdp")
        self.c = lax.rem(dp, 2)
        self.x = lax.rem(lax.div(dp, 2), 4)
        self.yl = lax.div(dp, 8)
        self.yh = lax.div(fs, 4)
        self.z = lax.rem(fs, 4)
        self.y = self.yh * 2 + self.yl
        self.zi = lax.div(self.z, 2)
        self.own = lax.rem(self.z, 2) == self.c
        self.other = lax.rem(self.z, 2) != self.c

    def device(self, x, y, z, c):
        return (lax.rem(y, 2) * 8 + x * 2 + c, lax.div(y, 2) * 4 + z)

    def step(self, axis, by):
        go = lambda v: lax.rem(v + (by + 4), 4)
        return self.device(
            go(self.x) if axis == "x" else self.x,
            go(self.y) if axis == "y" else self.y,
            go(self.z) if axis == "z" else self.z,
            self.c,
        )

    def sibling(self):
        return self.device(self.x, self.y, self.z, 1 - self.c)

    def at(self, axis, by=0):
        if axis == "z":
            return lax.div(lax.rem(self.z + (by + 4), 4), 2)
        return lax.rem((self.x if axis == "x" else self.y) + (by + 4), 4)


def block_shape(rows, cx, cy, cz, half):
    lead = (2 if cy is None else 0, 2 if cz is None else 0, 2 if cy is None else 0, 4 if cx is None else 0)
    return tuple(v for v in lead if v) + (rows // 2 if half else rows, 128)


class Unit:
    def __init__(self, number, name, ref, lead, rlead, rows, dtype, gorder, rorder, gdirect, rdirect, place, sems, bufs):
        self.number, self.name, self.ref, self.lead, self.rlead = number, name, ref, lead, rlead
        self.rows, self.dtype, self.place = rows, dtype, place
        self.gorder, self.rorder = gorder, rorder
        self.gdirect, self.rdirect = gdirect, rdirect
        self.send, self.grecv, self.rrecv = sems
        self.bufs = bufs

    def coords(self, phase, order, v, gather):
        cur, done = order[phase], order[:phase]
        out = []
        for axis in "xyz":
            if axis == cur:
                out.append(v)
            elif (axis in done) == gather:
                out.append(None)
            else:
                out.append(self.place.at(axis))
        return out

    def index(self, cx, cy, cz, half):
        s = slice(None)
        yh, yl = (s, s) if cy is None else (lax.div(cy, 2), lax.rem(cy, 2))
        rr = s if half is None else pl.ds(half * (self.rows // 2), self.rows // 2)
        return (yh, s if cz is None else cz, yl, s if cx is None else cx, rr, s)

    def block(self, phase, order, v, half, gather):
        lead = self.lead if gather else self.rlead
        return self.ref.at[lead + self.index(*self.coords(phase, order, v, gather), half)]

    def copy(self, src, dst, phase, kind, axis, recv, by):
        k = (self.number * 3 + phase) * 4 + kind
        return pltpu.make_async_remote_copy(
            src_ref=src,
            dst_ref=dst,
            send_sem=self.send.at[k],
            recv_sem=recv.at[k],
            device_id=self.place.step(axis, by),
            device_id_type=MESH,
        )

    def way(self, kind, direct):
        if direct:
            return None, (1, -1, 2)[kind]
        return (None if kind < 2 else kind - 2), (1 if kind % 2 == 0 else -1)

    def gcopy(self, phase, kind, v):
        half, by = self.way(kind, phase in self.gdirect)
        ref = self.block(phase, self.gorder, v, half, True)
        return self.copy(ref, ref, phase, kind, self.gorder[phase], self.grecv, by)

    def gactive(self, phase, z_side):
        axis = self.gorder[phase]
        if axis == "z":
            return z_side
        return None if "z" in self.gorder[:phase] else self.place.own

    def gather1(self, phase):
        here = self.place.at(self.gorder[phase])

        def body():
            for kind in (0, 1, 2) if phase in self.gdirect else (0, 1):
                self.gcopy(phase, kind, here).start()

        when(self.gactive(phase, self.place.own), body)

    def gather2(self, phase):
        axis = self.gorder[phase]
        left, right = self.place.at(axis, -1), self.place.at(axis, 1)

        def body():
            self.gcopy(phase, 0, left).wait_recv()
            self.gcopy(phase, 2, left).start()
            self.gcopy(phase, 1, right).wait_recv()
            self.gcopy(phase, 3, right).start()

        when(self.gactive(phase, self.place.other), body)

    def gather3(self, phase):
        axis = self.gorder[phase]
        far = self.place.at(axis, 2)
        left, right = self.place.at(axis, -1), self.place.at(axis, 1)

        def near():
            self.gcopy(phase, 0, left).wait_recv()
            self.gcopy(phase, 1, right).wait_recv()

        if phase in self.gdirect:
            when(self.gactive(phase, self.place.other), near)
            when(self.gactive(phase, self.place.own), lambda: self.gcopy(phase, 2, far).wait_recv())
            return

        def body():
            self.gcopy(phase, 2, far).wait_recv()
            self.gcopy(phase, 3, far).wait_recv()

        when(self.gactive(phase, self.place.own), body)

    def gather_drain(self):
        for phase in range(3):
            here = self.place.at(self.gorder[phase])

            def sent(kinds, phase=phase, here=here):
                for kind in kinds:
                    self.gcopy(phase, kind, here).wait_send()

            if phase in self.gdirect:
                when(self.gactive(phase, self.place.own), lambda s=sent: s((0, 1, 2)))
            elif self.gorder[phase] == "z":
                when(self.place.own, lambda s=sent: s((0, 1)))
                when(self.place.other, lambda s=sent: s((2, 3)))
            else:
                when(self.gactive(phase, None), lambda s=sent: s((0, 1, 2, 3)))

    def landing(self, phase, kind):
        whole, half, lead = self.bufs[phase]
        if kind < 2 or phase in self.rdirect:
            return whole.at[lead + (kind,)]
        if self.rorder[phase] == "z":
            dims = len(whole.shape) - len(lead) - 3
            return whole.at[lead + (kind - 2,) + (slice(None),) * dims + (pl.ds(0, self.rows // 2),)]
        return half.at[lead + (kind - 2,)]

    def rcopy(self, phase, kind, v):
        half, by = self.way(kind, phase in self.rdirect)
        return self.copy(
            self.block(phase, self.rorder, v, half, False),
            self.landing(phase, kind),
            phase,
            kind,
            self.rorder[phase],
            self.rrecv,
            by,
        )

    def ractive(self, phase, z_side):
        if self.rorder[phase] == "z":
            return z_side
        return self.place.own if "z" in self.rorder[:phase] else None

    def add(self, phase, v, half, sources, out=None):
        cx, cy, cz = self.coords(phase, self.rorder, v, False)
        height = self.rows if half is None else self.rows // 2
        first = 0 if half is None else half * height
        every = slice(None)
        for yh in (0, 1) if cy is None else (lax.div(cy, 2),):
            for zi in (0, 1) if cz is None else (cz,):
                for yl in (0, 1) if cy is None else (lax.rem(cy, 2),):
                    lead = (yh,) * (cy is None) + (zi,) * (cz is None) + (yl,) * (cy is None)
                    idx = self.rlead + (yh, zi, yl, every if cx is None else cx, pl.ds(first, height))
                    if len(sources) == 1 and out is None:
                        self.ref[idx] = self.ref[idx] + sources[0][lead]
                        continue
                    total = self.ref[idx].astype(F32)
                    for src in sources:
                        total = total + src[lead].astype(F32)
                    if out is None:
                        self.ref[idx] = total.astype(self.dtype)
                    else:
                        out[...] = total

    def reduce1(self, phase):
        axis = self.rorder[phase]
        far = self.place.at(axis, 2)
        left, right = self.place.at(axis, -1), self.place.at(axis, 1)

        def body():
            self.rcopy(phase, 2, far).start()
            if phase not in self.rdirect:
                self.rcopy(phase, 3, far).start()

        when(self.ractive(phase, self.place.own), body)
        if phase in self.rdirect:

            def near():
                self.rcopy(phase, 0, right).start()
                self.rcopy(phase, 1, left).start()

            when(self.ractive(phase, self.place.other), near)

    def reduce2(self, phase):
        axis = self.rorder[phase]
        left, right = self.place.at(axis, -1), self.place.at(axis, 1)

        def body():
            self.rcopy(phase, 2, right).wait_recv()
            self.add(phase, right, 0, [self.landing(phase, 2)])
            self.rcopy(phase, 0, right).start()
            self.rcopy(phase, 3, left).wait_recv()
            self.add(phase, left, 1, [self.landing(phase, 3)])
            self.rcopy(phase, 1, left).start()

        when(self.ractive(phase, self.place.other), body)

    def reduce3(self, phase, out=None):
        here = self.place.at(self.rorder[phase])

        def body():
            kinds = (0, 1, 2) if phase in self.rdirect else (0, 1)
            for kind in kinds:
                self.rcopy(phase, kind, here).wait_recv()
            self.add(phase, here, None, [self.landing(phase, kind) for kind in kinds], out)

        when(self.ractive(phase, self.place.own), body)

    def reduce_drain(self):
        for phase in range(3):
            here = self.place.at(self.rorder[phase])

            def sent(kinds, phase=phase, here=here):
                for kind in kinds:
                    self.rcopy(phase, kind, here).wait_send()

            far = (2,) if phase in self.rdirect else (2, 3)
            if self.rorder[phase] == "z":
                when(self.place.own, lambda s=sent, far=far: s(far))
                when(self.place.other, lambda s=sent: s((0, 1)))
            else:
                when(self.ractive(phase, None), lambda s=sent, far=far: s((0, 1) + far))


class Job:
    def __init__(self, steps, backlog, latency):
        self.steps, self.backlog, self.latency, self.gate = steps, backlog, latency, None
        self.next, self.ready = 0, 0.0

    @property
    def done(self):
        return self.next == len(self.steps)


class Schedule:
    def __init__(self):
        self.now, self.busy, self.jobs = 0.0, dict(x=0.0, y=0.0, z=0.0), []

    def add(self, job):
        job.ready = self.now
        self.jobs.append(job)
        self.poll()

    def emit(self, job):
        body, axis, link, cost = job.steps[job.next]
        body()
        job.next += 1
        self.now += cost
        if axis is not None:
            self.busy[axis] = max(self.now, self.busy[axis]) + link
            job.ready = self.busy[axis] + job.latency

    def when(self, job):
        axis = job.steps[job.next][1]
        if job.gate is not None and job.next == job.gate[0] and job.gate[1].next < job.gate[2]:
            return math.inf
        if job.gate is not None and job.next == 1 and job.gate[1].next < 3:
            return math.inf
        return job.ready if axis is None else max(job.ready, self.busy[axis] - job.backlog)

    def poll(self):
        while True:
            job = next((j for j in self.jobs if not j.done and self.when(j) <= self.now), None)
            if job is None:
                return
            self.emit(job)

    def tick(self, time):
        self.now += time
        self.poll()

    def need(self, jobs):
        while not all(j.done for j in jobs):
            job = min((j for j in self.jobs if not j.done), key=self.when)
            self.now = max(self.now, self.when(job))
            self.emit(job)


def gather_steps(unit, size):
    steps = []
    for phase in range(3):
        axis, share = unit.gorder[phase], size * 5.6 / 4 ** (2 - phase)
        direct = phase in unit.gdirect

        def one(phase=phase):
            if phase:
                unit.gather3(phase - 1)
            unit.gather1(phase)

        steps.append((one, axis, share * (2 if direct else 1), 0.25))
        if not direct:
            steps.append((lambda phase=phase: unit.gather2(phase), axis, share / 2, 0.25))
    steps.append((lambda: unit.gather3(2), None, 0.0, 0.1))
    return steps


def reduce_steps(unit, size, finish):
    steps = []
    for phase in range(3):
        axis, share = unit.rorder[phase], size * 5.6 / 4 ** phase
        cost = size * 0.3 / 4 ** phase
        direct = phase in unit.rdirect

        def one(phase=phase):
            if phase:
                unit.reduce3(phase - 1)
            unit.reduce1(phase)

        steps.append((one, axis, share * (2 if direct else 0.5), 0.2 + (4 * cost if phase else 0)))
        if not direct:
            steps.append((lambda phase=phase: unit.reduce2(phase), axis, share, 0.25 + cost))
    steps.append((finish, None, 0.0, 0.3))
    return steps


ROUNDS = [("".join(reversed(o))) for o in ORDERS]


def slot(name):
    at = PLACE[name]
    return at if isinstance(at, int) else UNIT[at]


def rdirect_of(name):
    if name == "n":
        return (0, 1, 2)
    return (1, 2) if REDUCE.index(name) >= 11 else (2,)


def landing_shapes(rows, dtype, many):
    shapes = []
    for k, order in enumerate(ROUNDS if many else ROUNDS[:1]):
        for phase in range(3):
            known = order[: phase + 1]
            c = [0 if a in known else None for a in "xyz"]
            slots = 2 if many and phase == 0 else 3
            lead = (many, slots) if many else (slots,)
            shapes.append(pltpu.VMEM(lead + block_shape(rows, *c, False), dtype))
            if many and phase < 2 and order[phase] != "z":
                shapes.append(pltpu.VMEM((many, 2) + block_shape(rows, *c, True), dtype))
    return shapes


PAIR = 64


def kernel(
    tok, pos, inv, ga, gf, gq, gk, wq, wk, wv, wo, wg, wu, wd, cot,
    mixed, tgrad, fin, on,
    W, Wn, *rest,
):
    rest = list(rest)
    place = Place()
    me = place
    c = me.c
    sib = me.sibling()
    mine = pl.multiple_of(c * TOK, TOK)
    theirs = pl.multiple_of((1 - c) * TOK, TOK)
    bufs = []
    for order in ROUNDS:
        bufs.append([(rest.pop(0), rest.pop(0) if order[p] != "z" and p < 2 else None) for p in range(3)])
    nbufs = [(rest.pop(0), None, ()) for p in range(3)]
    (
        send, grecv, rrecv, lsem, psend, precv,
        X, H, FG, BG, CT, QR, KR, Q, K, VA, ATT, RL, BR, HID, ACT, H1, H2,
        COS, SIN, BIAS, PART, RECV, GROW, GQK, SM, POSM, POSR, DG, GP, GPR, FIN, FINN,
    ) = rest

    units = {}
    for i, name in enumerate(SHARD):
        k = REDUCE.index(name)
        units[name] = Unit(
            i, name, W, (i,), (slot(name),), 128, BF, ORDERS[GATHER.index(name) % 3], ROUNDS[k % 3],
            (0, 1) if GATHER.index(name) < 3 else (0,), rdirect_of(name), me, (send, grecv, rrecv), [(w, h, (k // 3,)) for w, h in bufs[k % 3]],
        )
    gains = Unit(
        NU, "n", Wn, (), (), 16, F32, ORDERS[2], ROUNDS[0], (0, 1, 2), rdirect_of("n"), me,
        (send, grecv, rrecv), nbufs,
    )
    every = list(units.values()) + [gains]

    def pair(k, src, dst):
        return pltpu.make_async_remote_copy(
            src_ref=src, dst_ref=dst, send_sem=psend.at[k], recv_sem=precv.at[k],
            device_id=sib, device_id_type=MESH,
        )

    barrier = pltpu.get_barrier_semaphore()
    for target in [me.step(a, s) for a in "xyz" for s in (1, -1, 2)] + [sib]:
        pl.semaphore_signal(barrier, inc=1, device_id=target, device_id_type=MESH)
    tok_local = pltpu.make_async_copy(tok, X.at[pl.ds(mine, TOK)], lsem.at[NU + 1])
    tok_local.start()
    cot_local = pltpu.make_async_copy(cot, CT, lsem.at[NU + 2])
    cot_local.start()
    dp = lax.axis_index("dp")
    SM[...] = jnp.zeros_like(SM)
    SM[0:1, 0:64] = ga[...].astype(F32)
    SM[1:2, 0:64] = gf[...].astype(F32)
    SM[2:3, 0:8] = gq[...].astype(F32)
    SM[3:4, 0:8] = gk[...].astype(F32)
    rows8 = lax.broadcasted_iota(jnp.int32, (8, 128), 0)
    SM[...] = jnp.where(rows8 < 2, pltpu.roll(SM[...], c * 64, 1), pltpu.roll(SM[...], dp * 8, 1))
    POSM[...] = jnp.zeros_like(POSM)
    POSM[0:2, :] = pos[...].astype(F32)
    pl.semaphore_wait(barrier, 10)

    sources = dict(q=wq, k=wk, v=wv, o=wo, g=wg, u=wu, d=wd)

    def shard(unit):
        if unit.name == "n":
            return SM
        part = int(unit.name[1:] or 0)
        return sources[unit.name[0]].at[:, pl.ds(part * 128, 128)]

    def shard_place(unit, core):
        h = unit.rows // 2
        return unit.ref.at[
            unit.lead + (me.yh, me.zi, me.yl, me.x, pl.ds(pl.multiple_of(core * h, 8), h))
        ]

    sequence = [units[n] for n in GATHER[:3]] + [gains] + [units[n] for n in GATHER[3:]]

    @pl.when(me.own)
    def _():
        for u in sequence:
            pltpu.make_async_copy(shard(u), shard_place(u, c), lsem.at[u.number]).start()

    @pl.when(me.other)
    def _():
        for u in sequence:
            pair(u.number, shard(u), shard_place(u, c)).start()

    sched = Schedule()
    jobs = {}
    for u in sequence:

        @pl.when(me.own)
        def _(u=u):
            pltpu.make_async_copy(shard(u), shard_place(u, c), lsem.at[u.number]).wait()
            pair(u.number, shard_place(u, 1 - c), shard_place(u, 1 - c)).wait_recv()

        jobs[u.name] = Job(gather_steps(u, 0.02 if u is gains else 1.0), GATHER_BACKLOG, LATENCY)
        at = GATHER.index(u.name) - 3 * AHEAD if u is not gains else -1
        if at >= 0:
            before = jobs[GATHER[at]]
            jobs[u.name].gate = (len(jobs[u.name].steps) - 3, before, len(before.steps) - 1)
        sched.add(jobs[u.name])

    pos_pair = pair(NU + 1, POSM, POSR)
    pos_pair.start()
    tok_pair = pair(NU + 2, tok, X.at[pl.ds(mine, TOK)])
    tok_pair.start()
    sched.tick(0.8)

    @pl.when(me.other)
    def _():
        for u in sequence:
            pair(u.number, shard(u), shard_place(u, c)).wait_send()

    pos_pair.wait()

    lane = lax.broadcasted_iota(jnp.int32, (128, 128), 1)
    slots = lax.broadcasted_iota(jnp.int32, (128, 256), 1)
    rows2 = lax.broadcasted_iota(jnp.int32, (128, 256), 0)
    inv_row = jnp.broadcast_to(inv[...][:1], (128, 128))

    def tables(b, h):
        place_row = jnp.where(c == b, POSM[h : h + 1, :], POSR[h : h + 1, :])
        places = jnp.broadcast_to(place_row, (128, 128)).T
        angles = places * inv_row
        rs = pl.ds(b * 256 + h * 128, 128)
        COS[rs, :] = jnp.cos(angles)
        sine = jnp.sin(angles)
        SIN[rs, :] = jnp.where(lane < 64, -sine, sine)
        t = rows2 + h * 128
        first = t - jnp.concatenate([places, places], axis=1).astype(jnp.int32)
        allowed = (slots <= t) & (slots >= first)
        bias = jnp.where(allowed, 0.0, -1e30)
        BIAS[b, pl.ds(h * 128, 128), :] = bias

    for b in range(2):
        for h in range(2):
            tables(b, h)
            sched.tick(0.5)
    ones = jnp.ones((256, 128), BF)
    with_ones = lambda f, b: jnp.concatenate([VA[f, b], ones], axis=1)
    tok_local.wait()
    tok_pair.wait()
    cot_local.wait()

    def full(u, yh):
        return [W[UNIT[u] if isinstance(u, str) else u, yh, zi].reshape(1024, 128) for zi in range(2)]

    def wide(u):
        return jnp.concatenate(full(u, 0) + full(u, 1), axis=1)

    def tile(names, yh, j):
        at = lambda u, zi: W[UNIT[u], yh, zi, j // 2, pl.ds(j % 2 * 2, 2)].reshape(256, 128)
        return jnp.concatenate([at(u, zi) for u in names for zi in range(2)], axis=1)

    def turn(v):
        return pltpu.roll(v, 64, 1)

    def normed(v, gain, b):
        rs = pl.ds(b * 256, 256)
        v = v * lax.rsqrt(jnp.mean(v * v, axis=-1, keepdims=True) + EPS) * gain
        return (v * COS[rs, :] + turn(v) * SIN[rs, :]).astype(BF)

    sched.need([jobs[n] for n in ("q0", "q1", "k", "n")])
    for j in range(8):
        for r in range(2):
            GROW[r : r + 1, j * 128 : (j + 1) * 128] = (
                Wn[0, 0, j // 4, j % 4, r : r + 1, :] + Wn[0, 0, j // 4, j % 4, 8 + r : 9 + r, :]
            )
    gq = jnp.zeros((8, 128), F32)
    for j in range(8):
        gq = gq + Wn[0, 0, j // 4, j % 4, 0:8, :] + Wn[0, 0, j // 4, j % 4, 8:16, :]
    GQK[...] = gq
    qgain = GQK[2:3, :]
    kgain = GQK[3:4, :]
    sched.tick(0.3)

    def heads(raw):
        for b in range(2):
            for f in range(4):
                yield b, f, raw[b * 256 : b * 256 + 256, f * 128 : f * 128 + 128]

    def queries(r, carry):
        raw = nn(X[...], wide(r))
        for b, f, v in heads(raw):
            QR[f // 2, r, pl.ds(b * 256, 256), pl.ds(f % 2 * 128, 128)] = v.astype(BF)
            Q[f, b, pl.ds(pl.multiple_of(r * 256, 256), 256), :] = normed(v, qgain, b)
        return carry

    lax.fori_loop(0, 2, queries, 0)
    sched.tick(2.4)
    raw = nn(X[...], wide("k"))
    for b, f, v in heads(raw):
        KR[f // 2, pl.ds(b * 256, 256), pl.ds(f % 2 * 128, 128)] = v.astype(BF)
        K[f, b] = normed(v, kgain, b)
    sched.tick(1.2)

    sched.need([jobs["v"]])
    raw = nn(X[...], wide("v")).astype(BF)
    for f in range(4):
        for b in range(2):
            VA[f, b] = raw[b * 256 : b * 256 + 256, f * 128 : f * 128 + 128]
    sched.tick(0.8)

    scale = HD ** -0.5
    power = scale * math.log2(math.e)

    def attend(f, b):
        yh, zi = f // 2, f % 2
        rs = pl.ds(b * 256, 256)
        for r in range(2):
            s = nt(Q[f, b, pl.ds(r * 256, 256), :], K[f, b])
            e = jnp.exp2(s * power + BIAS[b]).astype(BF)
            ol = nn(e, with_ones(f, b))
            rl = 1.0 / ol[:, 128:256]
            at = pl.ds(r * 256 + zi * 128, 128)
            ATT[yh, rs, at] = (ol[:, 0:128] * rl).astype(BF)
            RL[yh, rs, at] = rl.astype(BF)

    for f in range(4):
        for b in range(2):
            attend(f, b)
            sched.tick(0.35)

    for b in range(2):
        BIAS[b] = BIAS[b].T

    def pair_piece(base, slot, j):
        cols = pl.ds(j * 256, 256)
        return pair(base + j, PART.at[0, :, cols], RECV.at[slot, :, cols])

    def pair_sum(base, slot, products, time):
        def one(rows, j):
            out = None
            for left, names, yh in products:
                p = nt(left(rows), tile(names, yh, j))
                out = p if out is None else out + p
            return out

        def side(i, carry):
            rows = pl.ds(pl.multiple_of(lax.rem(1 - c + i, 2) * TOK, TOK), TOK)
            for j in range(4):
                PART[i, :, pl.ds(j * 256, 256)] = one(rows, j).astype(BF)
                if j % 2:

                    @pl.when(i == 0)
                    def _(j=j):
                        pair_piece(base, slot, j - 1).start()
                        pair_piece(base, slot, j).start()

            return carry

        lax.fori_loop(0, 2, side, 0)
        sched.tick(2 * time)

    def pair_done(base, slot):
        for j in range(4):
            pair_piece(base, slot, j).wait()

    CH = 64

    def rows_then_send(base, dst, body):
        for j in range(TOK // CH):
            rs = pl.ds(pl.multiple_of(mine + j * CH, CH), CH)
            body(pl.ds(j * CH, CH), rs)
            pair(base + j, dst.at[rs], dst.at[rs]).start()
        sched.tick(0.5)

    def rows_done(base, dst):
        for j in range(TOK // CH):
            rs = pl.ds(pl.multiple_of(mine + j * CH, CH), CH)
            pair(base + j, dst.at[rs], dst.at[rs]).wait_send()
            rs = pl.ds(pl.multiple_of(theirs + j * CH, CH), CH)
            pair(base + j, dst.at[rs], dst.at[rs]).wait_recv()

    sched.need([jobs["o0"], jobs["o1"]])

    pair_sum(
        20, 0, [(lambda rows, yh=yh: ATT[yh, rows, :], ("o0", "o1"), yh) for yh in range(2)], 0.8
    )
    pair_done(20, 0)

    def hidden_rows(rs, abs_rs):
        v = PART[1, rs, :].astype(F32) + RECV[0, rs, :].astype(F32)
        BR[rs, :] = v
        n = v * lax.rsqrt(jnp.mean(v * v, axis=-1, keepdims=True) + EPS) * GROW[0:1, :]
        hid = X[abs_rs, :].astype(F32) + n
        HID[rs, :] = hid
        H[abs_rs, :] = hid.astype(BF)

    rows_then_send(24, H, hidden_rows)

    def ffn_tile(s, rows):
        h = H[rows, :]
        g = nn(h, wide("g%d" % s))
        u = nn(h, wide("u%d" % s))
        sg = 0.5 * jnp.tanh(0.5 * g) + 0.5
        silu = g * sg
        act = (silu * u).astype(BF)
        h1 = ((sg + silu * (1.0 - sg)) * u).astype(BF)
        h2 = silu.astype(BF)
        for yh in range(2):
            cols, part = pl.ds(s * 256, 256), slice(yh * 256, yh * 256 + 256)
            ACT[yh, rows, cols] = act[:, part]
            H1[yh, rows, cols] = h1[:, part]
            H2[yh, rows, cols] = h2[:, part]

    sched.need([jobs["g0"], jobs["u0"]])

    def first_tiles(i, carry):
        @pl.when(i == 1)
        def _():
            rows_done(24, H)

        ffn_tile(0, pl.ds(pl.multiple_of(lax.rem(c + i, 2) * TOK, TOK), TOK))
        return carry

    lax.fori_loop(0, 2, first_tiles, 0)
    sched.tick(1.5)
    for s in (1, 2):
        sched.need([jobs["g%d" % s], jobs["u%d" % s]])

        def tiles(m, carry, s=s):
            ffn_tile(s, pl.ds(pl.multiple_of(m * 256, 256), 256))
            return carry

        lax.fori_loop(0, 2, tiles, 0)
        sched.tick(1.5)
    for u in every:
        if u.name[0] != "d":
            u.gather_drain()
    sched.need([jobs["d%d" % s] for s in range(3)])
    pair_sum(
        28, 1, [(lambda rows, yh=yh: ACT[yh, rows, :], ("d0", "d1", "d2"), yh) for yh in range(2)], 1.1
    )
    DG[...] = jnp.zeros_like(DG)
    GP[...] = jnp.zeros_like(GP)
    for n in ("d0", "d1", "d2"):
        units[n].gather_drain()
    pair_done(28, 1)

    def rms_back(v, r, gain, dn, at):
        gd = gain * dn
        vr = v * r
        grad = r * (gd - vr * jnp.mean(gd * vr, axis=-1, keepdims=True))
        dg = dn * vr
        DG[at, :, :] += jnp.sum(dg.reshape(CH // 8, 8, 1024), axis=0)
        return grad

    def ffn_rows(rs, abs_rs):
        v = PART[1, rs, :].astype(F32) + RECV[1, rs, :].astype(F32)
        gain = GROW[1:2, :]
        r = lax.rsqrt(jnp.mean(v * v, axis=-1, keepdims=True) + EPS)
        PART[0, rs, :] = (HID[rs, :] + v * r * gain).astype(BF)
        FG[abs_rs, :] = rms_back(v, r, gain, CT[rs, :].astype(F32), 1).astype(BF)

    rows_then_send(32, FG, ffn_rows)
    mixed_out = pltpu.make_async_copy(PART.at[0], mixed, lsem.at[0])
    mixed_out.start()

    def weight_grad(u, left, right):
        def half(j, carry):
            cols = pl.ds(pl.multiple_of(j * 512, 512), 512)
            out = tn(left[:, cols], jnp.concatenate([right(0), right(1)], axis=1)).astype(BF)
            for yh in range(2):
                for zi in range(2):
                    at = (yh * 2 + zi) * 128
                    W[slot(u), yh, zi, j] = out[:, at : at + 128].reshape(4, 128, 128)
            return carry

        lax.fori_loop(0, 2, half, 0)

    fin_jobs = []

    def start_reduce(u):
        unit = gains if u == "n" else units[u]
        out = FINN if u == "n" else FIN.at[unit.number]

        def finish():
            unit.reduce3(2, out)

            @pl.when(me.own)
            def _():
                fin_pair(unit, 1 - c).start()

            unit.reduce_drain()

        job = Job(reduce_steps(unit, 0.02 if u == "n" else 1.0, finish), REDUCE_BACKLOG, REDUCE_LATENCY)
        fin_jobs.append(job)
        sched.add(job)

    def fin_pair(unit, core):
        if unit.name == "n":
            ref = FINN
        else:
            ref = FIN.at[unit.number, pl.ds(pl.multiple_of(core * 64, 64), 64)]
        return pair(48 + unit.number, ref, ref)

    def act_back(s, rs, time):
        cols = pl.ds(s * 256, 256)
        da = nn(FG[rs, :], wide("d%d" % s))
        for yh in range(2):
            part = da[:, yh * 256 : yh * 256 + 256]
            H1[yh, rs, cols] = (part * H1[yh, rs, cols].astype(F32)).astype(BF)
            H2[yh, rs, cols] = (part * H2[yh, rs, cols].astype(F32)).astype(BF)
        sched.tick(time)

    for s in range(3):
        act_back(s, pl.ds(mine, TOK), 0.0)
    rows_done(32, FG)

    def down(u):
        weight_grad(u, FG, lambda yh: ACT[yh, :, pl.ds(int(u[1]) * 256, 256)])
        sched.tick(0.85)
        start_reduce(u)

    def gate_up(u):
        cols = pl.ds(int(u[1]) * 256, 256)
        part = H1 if u[0] == "g" else H2
        weight_grad(u, H, lambda yh: part[yh, :, cols])
        sched.tick(0.85)
        start_reduce(u)

    down("d0")
    down("d1")
    act_back(0, pl.ds(theirs, TOK), 0.45)
    down("d2")
    act_back(1, pl.ds(theirs, TOK), 0.45)
    gate_up("g0")
    act_back(2, pl.ds(theirs, TOK), 0.45)
    gate_up("u0")
    mixed_out.wait()
    pair_sum(
        36, 0,
        [(lambda rows, yh=yh: H1[yh, rows, :], ("g0", "g1", "g2"), yh) for yh in range(2)]
        + [(lambda rows, yh=yh: H2[yh, rows, :], ("u0", "u1", "u2"), yh) for yh in range(2)],
        2.2,
    )
    gate_up("g1")
    gate_up("u1")
    pair_done(36, 0)

    def branch_rows(rs, abs_rs):
        dn = CT[rs, :].astype(F32) + PART[1, rs, :].astype(F32) + RECV[0, rs, :].astype(F32)
        HID[rs, :] = dn
        v = BR[rs, :]
        r = lax.rsqrt(jnp.mean(v * v, axis=-1, keepdims=True) + EPS)
        BG[abs_rs, :] = rms_back(v, r, GROW[0:1, :], dn, 0).astype(BF)

    rows_then_send(40, BG, branch_rows)
    gate_up("g2")
    gate_up("u2")
    rows_done(40, BG)

    DO = FG
    for r in range(2):
        out = nn(BG[...], wide("o%d" % r)).astype(BF)
        for yh in range(2):
            DO[:, pl.ds(yh * 512 + r * 256, 256)] = out[:, yh * 256 : yh * 256 + 256]
        sched.tick(0.8)
    for r in range(2):
        weight_grad("o%d" % r, BG, lambda yh: ATT[yh, :, pl.ds(r * 256, 256)])
        sched.tick(0.85)
        start_reduce("o%d" % r)

    def head_back(raw, gain, d, rs, row_at):
        d = d * COS[rs, :] - turn(d) * SIN[rs, :]
        r = lax.rsqrt(jnp.mean(raw * raw, axis=-1, keepdims=True) + EPS)
        gd = gain * d
        vr = raw * r
        GP[pl.ds(row_at, 8), :] += jnp.sum((d * vr).reshape(32, 8, 128), axis=0)
        return (r * (gd - vr * jnp.mean(gd * vr, axis=-1, keepdims=True))).astype(BF)

    QG, KVG = ACT, H1

    def attend_back(zi, n):
        yh, b = lax.div(n, 2), lax.rem(n, 2)
        f = yh * 2 + zi
        rs = pl.ds(pl.multiple_of(b * 256, 256), 256)
        dk, dv = None, None
        for r in range(2):
            at = pl.ds(r * 256 + zi * 128, 128)
            q = Q[f, b, pl.ds(r * 256, 256), :]
            do = DO[rs, pl.ds(pl.multiple_of(yh * 512 + (r * 256 + zi * 128), 128), 128)]
            do = do.astype(F32) * RL[yh, rs, at].astype(F32)
            dol = do.astype(BF)
            doa = jnp.concatenate([dol, (-(do * ATT[yh, rs, at].astype(F32))).astype(BF)], axis=1)
            e = jnp.exp2(nt(K[f, b], q) * power + BIAS[b])
            ds = (e * nt(with_ones(f, b), doa)).astype(BF)
            dv_r = nn(e.astype(BF), dol)
            dk_r = nn(ds, q)
            dv = dv_r if dv is None else dv + dv_r
            dk = dk_r if dk is None else dk + dk_r
            dq = tn(ds, K[f, b]) * scale
            raw = QR[yh, r, rs, pl.ds(zi * 128, 128)].astype(F32)
            QG[yh, rs, at] = head_back(raw, qgain, dq, rs, 0)
        raw = KR[yh, rs, pl.ds(zi * 128, 128)].astype(F32)
        KVG[yh, rs, pl.ds(zi * 128, 128)] = head_back(raw, kgain, dk * scale, rs, 8)
        KVG[yh, rs, pl.ds(256 + zi * 128, 128)] = dv.astype(BF)

    for zi in range(2):

        def back(n, carry, zi=zi):
            attend_back(zi, n)
            return carry

        lax.fori_loop(0, 4, back, 0)
        sched.tick(4.0)

    def gain_rows(at, row_at):
        summed = jnp.sum(DG[at], axis=0, keepdims=True)
        for j in range(8):
            GP[row_at + j : row_at + j + 1, :] = summed[:, j * 128 : (j + 1) * 128]

    qsum = jnp.sum(GP[0:8, :], axis=0, keepdims=True)
    ksum = jnp.sum(GP[8:16, :], axis=0, keepdims=True)
    gain_rows(0, 16)
    gain_rows(1, 24)
    GP[0:1, :] = qsum
    GP[8:9, :] = ksum
    gain_pair = pair(NU + 3, GP, GPR)
    gain_pair.start()

    def proj_grad(u, src, at):
        weight_grad(u, X, lambda yh: src[yh, :, pl.ds(at, 256)])
        sched.tick(0.85)
        start_reduce(u)

    proj_grad("q0", QG, 0)
    proj_grad("q1", QG, 256)
    proj_grad("k", KVG, 0)
    proj_grad("v", KVG, 256)
    gain_pair.wait()
    GPR[...] += GP[...]
    Wn[...] = jnp.zeros_like(Wn)
    for j in range(8):
        for f0 in range(2):
            for f1 in range(2):
                Wn[f0, f1, j // 4, j % 4, 0:1, :] = GPR[16 + j : 17 + j, :]
                Wn[f0, f1, j // 4, j % 4, 1:2, :] = GPR[24 + j : 25 + j, :]
                Wn[f0, f1, j // 4, j % 4, 8:9, :] = GPR[0:1, :]
                Wn[f0, f1, j // 4, j % 4, 9:10, :] = GPR[8:9, :]
    start_reduce("n")
    pair_sum(
        44, 1,
        [(lambda rows, yh=yh: QG[yh, rows, pl.ds(0, 512)], ("q0", "q1"), yh) for yh in range(2)]
        + [(lambda rows, yh=yh: KVG[yh, rows, pl.ds(0, 512)], ("k", "v"), yh) for yh in range(2)],
        1.4,
    )
    pair_done(44, 1)

    for j in range(TOK // CH):
        rs = pl.ds(j * CH, CH)
        HID[rs, :] = HID[rs, :] + PART[1, rs, :].astype(F32) + RECV[1, rs, :].astype(F32)
    tgrad_out = pltpu.make_async_copy(HID, tgrad, lsem.at[1])
    tgrad_out.start()
    sched.tick(0.6)

    sched.need(fin_jobs)
    for u in every:

        @pl.when(me.own)
        def _(u=u):
            fin_pair(u, 1 - c).wait_send()

        @pl.when(me.other)
        def _(u=u):
            fin_pair(u, c).wait_recv()

    mrows = pl.ds(pl.multiple_of(c * 64, 64), 64)
    fin_out = pltpu.make_async_copy(FIN.at[:, mrows], fin, lsem.at[2])
    fin_out.start()
    on_out = pltpu.make_async_copy(FINN, on, lsem.at[3])
    on_out.start()
    tgrad_out.wait()
    fin_out.wait()
    on_out.wait()


def finish_kernel(mixed_in, tgrad_in, fin, gn, mixed, tgrad, oq, ok, ov, oo, og, ou, od, oqg, okg, oag, ofg, sem):
    dp = lax.axis_index("dp")
    core = lax.rem(dp, 2)
    copies = [(mixed_in, mixed), (tgrad_in, tgrad)]
    targets = dict(q=oq, k=ok, v=ov, o=oo, g=og, u=ou, d=od)
    for i, name in enumerate(SHARD):
        part = int(name[1:] or 0)
        copies.append((fin.at[i], targets[name[0]].at[:, pl.ds(part * 128, 128)]))
    copies = [pltpu.make_async_copy(a, b, sem.at[i]) for i, (a, b) in enumerate(copies)]
    for copy in copies:
        copy.start()
    odd = core == 1
    for ref, row in ((oag, 0), (ofg, 1)):
        v = gn[...]
        v = jnp.where(odd, pltpu.roll(v, 64, 1), v)
        ref[...] = v[row : row + 1, 0:64]
    v = gn[...]
    back = lax.rem(128 - dp * 8, 128)
    v = pltpu.roll(v, back, 1)
    oqg[...] = v[8:9, 0:8]
    okg[...] = v[9:10, 0:8]
    for copy in copies:
        copy.wait()


def on_device(
    tokens, positions, w_query, w_key, w_value, w_out, w_gate, w_up, w_down,
    query_gain, key_gain, attn_gain, ffn_gain, cotangent,
):
    steps_up = np.arange(0, HD, 2).astype(np.float32) / np.float32(HD)
    inverse = (np.float32(ROPE_BASE) ** (-steps_up)).astype(np.float32)
    inv = jnp.asarray(np.tile(np.concatenate([inverse, inverse])[None], (8, 1)))
    vm = pl.BlockSpec(memory_space=pltpu.VMEM)
    hbm = pl.BlockSpec(memory_space=pl.ANY)
    far = pl.BlockSpec(memory_space=pltpu.HBM)
    n = (NU + 1) * 12
    V = pltpu.VMEM
    sems = [pltpu.SemaphoreType.DMA((n,))] * 3 + [
        pltpu.SemaphoreType.DMA((NU + 3,)),
        pltpu.SemaphoreType.DMA((PAIR,)),
        pltpu.SemaphoreType.DMA((PAIR,)),
    ]
    work = [
        V((512, D), BF), V((512, D), BF), V((512, D), BF), V((512, D), BF),
        V((TOK, D), BF),
        V((2, 2, 512, 256), BF), V((2, 512, 256), BF),
        V((4, 2, 512, 128), BF), V((4, 2, 256, 128), BF), V((4, 2, 256, 128), BF),
        V((2, 512, 512), BF), V((2, 512, 512), BF),
        V((TOK, D), F32), V((TOK, D), F32),
        V((2, 512, 768), BF), V((2, 512, 768), BF), V((2, 512, 768), BF),
        V((512, 128), F32), V((512, 128), F32), V((2, 256, 256), F32),
        V((2, TOK, D), BF), V((2, TOK, D), BF),
        V((8, D), F32), V((8, 128), F32), V((8, 128), F32), V((8, 128), F32), V((8, 128), F32), V((2, 8, D), F32),
        V((32, 128), F32), V((32, 128), F32),
        V((NU, 128, 128), F32), V((16, 128), F32),
    ]
    f = lambda *s: jax.ShapeDtypeStruct(s, F32)
    main_out = pl.pallas_call(
        kernel,
        out_shape=(jax.ShapeDtypeStruct((TOK, D), BF), f(TOK, D), f(NU, 64, 128), f(16, 128)),
        in_specs=[hbm] + [vm] * 6 + [hbm] * 8,
        out_specs=[hbm] * 4,
        scratch_shapes=[V((NU + SPARE, 2, 2, 2, 4, 128, 128), BF), V((2, 2, 2, 4, 16, 128), F32)]
        + landing_shapes(128, BF, 5) + landing_shapes(16, F32, 0) + sems + work,
        compiler_params=pltpu.CompilerParams(
            collective_id=1, has_side_effects=True, vmem_limit_bytes=int(63.5 * 2**20)
        ),
        cost_estimate=pl.CostEstimate(flops=26 * 10**9, bytes_accessed=4 * 10**6, transcendentals=0),
    )(
        tokens, positions.reshape(2, 128), inv,
        attn_gain.reshape(1, 64), ffn_gain.reshape(1, 64), query_gain.reshape(1, 8), key_gain.reshape(1, 8),
        w_query, w_key, w_value, w_out.T, w_gate, w_up, w_down.T, cotangent,
    )
    outs = pl.pallas_call(
        finish_kernel,
        out_shape=(
            jax.ShapeDtypeStruct((TOK, D), BF), f(TOK, D),
            f(64, 256), f(64, 128), f(64, 128), f(64, 256), f(64, 384), f(64, 384), f(64, 384),
            f(1, 8), f(1, 8), f(1, 64), f(1, 64),
        ),
        in_specs=[vm] * 4,
        out_specs=[far] * 9 + [vm] * 4,
        scratch_shapes=[pltpu.SemaphoreType.DMA((NU + 2,))],
        compiler_params=pltpu.CompilerParams(vmem_limit_bytes=int(63.5 * 2**20)),
    )(*main_out)
    mixed, tgrad, gq, gk, gv, go, gg, gu, gd, nq, nk, na, nf = outs
    return (
        mixed, tgrad, gq, gk, gv, go.T, gg, gu, gd.T,
        nq.reshape(8), nk.reshape(8), na.reshape(64), nf.reshape(64),
    )


def solution(mesh):
    both, w, wt = P(("dp", "fsdp"), None), P("dp", "fsdp"), P("fsdp", "dp")
    return jax.shard_map(
        on_device,
        mesh=mesh,
        in_specs=(both, P(("dp", "fsdp")), w, w, w, wt, w, w, wt, P("dp"), P("dp"), P("dp"), P("dp"), both),
        out_specs=(both, both, w, w, w, wt, w, w, wt, P("dp"), P("dp"), P("dp"), P("dp")),
        check_vma=False,
    )
```

```python
import math

import numpy as np
import jax
import jax.numpy as jnp
from jax import lax
from jax.experimental import pallas as pl
from jax.experimental.pallas import tpu as pltpu
from jax.sharding import PartitionSpec as P

MESH = pl.DeviceIdType.MESH
F32, BF = jnp.float32, jnp.bfloat16
D, HD, TOK = 1024, 128, 256
EPS = 1e-6
ROPE_BASE = 1000000.0
GATHER = ("q0", "q1", "k", "v", "o0", "o1", "g0", "u0", "g1", "u1", "g2", "u2", "d0", "d1", "d2")
REDUCE = ("d0", "d1", "d2", "g0", "u0", "g1", "u1", "g2", "u2", "o0", "o1", "q0", "q1", "k", "v")
ORDERS = ("xyz", "yzx", "zxy")
SHARD = ("q0", "q1", "k", "v", "o0", "o1", "g0", "g1", "g2", "u0", "u1", "u2", "d0", "d1", "d2")
UNIT = {name: i for i, name in enumerate(SHARD)}
NU = len(SHARD)
LATENCY, REDUCE_LATENCY = 2.6, 10.0
GATHER_BACKLOG, REDUCE_BACKLOG, AHEAD = 1000.0, 6.0, 3
SPARE = 4
PLACE = dict(
    d0=15, d1=16, d2="d0", g0="d1", u0="d2", g1="g0", u1="u0", g2="g1", u2="u1", o0="g2", o1="u2", q0="o0", q1="o1",
    k=17, v=18,
)


def nn(a, b):
    return jnp.dot(a, b, preferred_element_type=F32)


def nt(a, b):
    return lax.dot_general(a, b, (((1,), (1,)), ((), ())), preferred_element_type=F32)


def tn(a, b):
    return lax.dot_general(a, b, (((0,), (0,)), ((), ())), preferred_element_type=F32)


def when(cond, body):
    if cond is None:
        body()
    else:
        pl.when(cond)(body)


class Place:
    def __init__(self):
        dp, fs = lax.axis_index("dp"), lax.axis_index("fsdp")
        self.c = lax.rem(dp, 2)
        self.x = lax.rem(lax.div(dp, 2), 4)
        self.yl = lax.div(dp, 8)
        self.yh = lax.div(fs, 4)
        self.z = lax.rem(fs, 4)
        self.y = self.yh * 2 + self.yl
        self.zi = lax.div(self.z, 2)
        self.own = lax.rem(self.z, 2) == self.c
        self.other = lax.rem(self.z, 2) != self.c

    def device(self, x, y, z, c):
        return (lax.rem(y, 2) * 8 + x * 2 + c, lax.div(y, 2) * 4 + z)

    def step(self, axis, by):
        go = lambda v: lax.rem(v + (by + 4), 4)
        return self.device(
            go(self.x) if axis == "x" else self.x,
            go(self.y) if axis == "y" else self.y,
            go(self.z) if axis == "z" else self.z,
            self.c,
        )

    def sibling(self):
        return self.device(self.x, self.y, self.z, 1 - self.c)

    def at(self, axis, by=0):
        if axis == "z":
            return lax.div(lax.rem(self.z + (by + 4), 4), 2)
        return lax.rem((self.x if axis == "x" else self.y) + (by + 4), 4)


def block_shape(rows, cx, cy, cz, half):
    lead = (2 if cy is None else 0, 2 if cz is None else 0, 2 if cy is None else 0, 4 if cx is None else 0)
    return tuple(v for v in lead if v) + (rows // 2 if half else rows, 128)


class Unit:
    def __init__(self, number, name, ref, lead, rlead, rows, dtype, gorder, rorder, gdirect, rdirect, place, sems, bufs):
        self.number, self.name, self.ref, self.lead, self.rlead = number, name, ref, lead, rlead
        self.rows, self.dtype, self.place = rows, dtype, place
        self.gorder, self.rorder = gorder, rorder
        self.gdirect, self.rdirect = gdirect, rdirect
        self.send, self.grecv, self.rrecv = sems
        self.bufs = bufs

    def coords(self, phase, order, v, gather):
        cur, done = order[phase], order[:phase]
        out = []
        for axis in "xyz":
            if axis == cur:
                out.append(v)
            elif (axis in done) == gather:
                out.append(None)
            else:
                out.append(self.place.at(axis))
        return out

    def index(self, cx, cy, cz, half):
        s = slice(None)
        yh, yl = (s, s) if cy is None else (lax.div(cy, 2), lax.rem(cy, 2))
        rr = s if half is None else pl.ds(half * (self.rows // 2), self.rows // 2)
        return (yh, s if cz is None else cz, yl, s if cx is None else cx, rr, s)

    def block(self, phase, order, v, half, gather):
        lead = self.lead if gather else self.rlead
        return self.ref.at[lead + self.index(*self.coords(phase, order, v, gather), half)]

    def copy(self, src, dst, phase, kind, axis, recv, by):
        k = (self.number * 3 + phase) * 4 + kind
        return pltpu.make_async_remote_copy(
            src_ref=src,
            dst_ref=dst,
            send_sem=self.send.at[k],
            recv_sem=recv.at[k],
            device_id=self.place.step(axis, by),
            device_id_type=MESH,
        )

    def way(self, kind, direct):
        if direct:
            return None, (1, -1, 2)[kind]
        return (None if kind < 2 else kind - 2), (1 if kind % 2 == 0 else -1)

    def gcopy(self, phase, kind, v):
        half, by = self.way(kind, phase in self.gdirect)
        ref = self.block(phase, self.gorder, v, half, True)
        return self.copy(ref, ref, phase, kind, self.gorder[phase], self.grecv, by)

    def gactive(self, phase, z_side):
        axis = self.gorder[phase]
        if axis == "z":
            return z_side
        return None if "z" in self.gorder[:phase] else self.place.own

    def gather1(self, phase):
        here = self.place.at(self.gorder[phase])

        def body():
            for kind in (0, 1, 2) if phase in self.gdirect else (0, 1):
                self.gcopy(phase, kind, here).start()

        when(self.gactive(phase, self.place.own), body)

    def gather2(self, phase):
        axis = self.gorder[phase]
        left, right = self.place.at(axis, -1), self.place.at(axis, 1)

        def body():
            self.gcopy(phase, 0, left).wait_recv()
            self.gcopy(phase, 2, left).start()
            self.gcopy(phase, 1, right).wait_recv()
            self.gcopy(phase, 3, right).start()

        when(self.gactive(phase, self.place.other), body)

    def gather3(self, phase):
        axis = self.gorder[phase]
        far = self.place.at(axis, 2)
        left, right = self.place.at(axis, -1), self.place.at(axis, 1)

        def near():
            self.gcopy(phase, 0, left).wait_recv()
            self.gcopy(phase, 1, right).wait_recv()

        if phase in self.gdirect:
            when(self.gactive(phase, self.place.other), near)
            when(self.gactive(phase, self.place.own), lambda: self.gcopy(phase, 2, far).wait_recv())
            return

        def body():
            self.gcopy(phase, 2, far).wait_recv()
            self.gcopy(phase, 3, far).wait_recv()

        when(self.gactive(phase, self.place.own), body)

    def gather_drain(self):
        for phase in range(3):
            here = self.place.at(self.gorder[phase])

            def sent(kinds, phase=phase, here=here):
                for kind in kinds:
                    self.gcopy(phase, kind, here).wait_send()

            if phase in self.gdirect:
                when(self.gactive(phase, self.place.own), lambda s=sent: s((0, 1, 2)))
            elif self.gorder[phase] == "z":
                when(self.place.own, lambda s=sent: s((0, 1)))
                when(self.place.other, lambda s=sent: s((2, 3)))
            else:
                when(self.gactive(phase, None), lambda s=sent: s((0, 1, 2, 3)))

    def landing(self, phase, kind):
        whole, half, lead = self.bufs[phase]
        if kind < 2 or phase in self.rdirect:
            return whole.at[lead + (kind,)]
        if self.rorder[phase] == "z":
            dims = len(whole.shape) - len(lead) - 3
            return whole.at[lead + (kind - 2,) + (slice(None),) * dims + (pl.ds(0, self.rows // 2),)]
        return half.at[lead + (kind - 2,)]

    def rcopy(self, phase, kind, v):
        half, by = self.way(kind, phase in self.rdirect)
        return self.copy(
            self.block(phase, self.rorder, v, half, False),
            self.landing(phase, kind),
            phase,
            kind,
            self.rorder[phase],
            self.rrecv,
            by,
        )

    def ractive(self, phase, z_side):
        if self.rorder[phase] == "z":
            return z_side
        return self.place.own if "z" in self.rorder[:phase] else None

    def add(self, phase, v, half, sources, out=None):
        cx, cy, cz = self.coords(phase, self.rorder, v, False)
        height = self.rows if half is None else self.rows // 2
        first = 0 if half is None else half * height
        every = slice(None)
        for yh in (0, 1) if cy is None else (lax.div(cy, 2),):
            for zi in (0, 1) if cz is None else (cz,):
                for yl in (0, 1) if cy is None else (lax.rem(cy, 2),):
                    lead = (yh,) * (cy is None) + (zi,) * (cz is None) + (yl,) * (cy is None)
                    idx = self.rlead + (yh, zi, yl, every if cx is None else cx, pl.ds(first, height))
                    if len(sources) == 1 and out is None:
                        self.ref[idx] = self.ref[idx] + sources[0][lead]
                        continue
                    total = self.ref[idx].astype(F32)
                    for src in sources:
                        total = total + src[lead].astype(F32)
                    if out is None:
                        self.ref[idx] = total.astype(self.dtype)
                    else:
                        out[...] = total

    def reduce1(self, phase):
        axis = self.rorder[phase]
        far = self.place.at(axis, 2)
        left, right = self.place.at(axis, -1), self.place.at(axis, 1)

        def body():
            self.rcopy(phase, 2, far).start()
            if phase not in self.rdirect:
                self.rcopy(phase, 3, far).start()

        when(self.ractive(phase, self.place.own), body)
        if phase in self.rdirect:

            def near():
                self.rcopy(phase, 0, right).start()
                self.rcopy(phase, 1, left).start()

            when(self.ractive(phase, self.place.other), near)

    def reduce2(self, phase):
        axis = self.rorder[phase]
        left, right = self.place.at(axis, -1), self.place.at(axis, 1)

        def body():
            self.rcopy(phase, 2, right).wait_recv()
            self.add(phase, right, 0, [self.landing(phase, 2)])
            self.rcopy(phase, 0, right).start()
            self.rcopy(phase, 3, left).wait_recv()
            self.add(phase, left, 1, [self.landing(phase, 3)])
            self.rcopy(phase, 1, left).start()

        when(self.ractive(phase, self.place.other), body)

    def reduce3(self, phase, out=None):
        here = self.place.at(self.rorder[phase])

        def body():
            kinds = (0, 1, 2) if phase in self.rdirect else (0, 1)
            for kind in kinds:
                self.rcopy(phase, kind, here).wait_recv()
            self.add(phase, here, None, [self.landing(phase, kind) for kind in kinds], out)

        when(self.ractive(phase, self.place.own), body)

    def reduce_drain(self):
        for phase in range(3):
            here = self.place.at(self.rorder[phase])

            def sent(kinds, phase=phase, here=here):
                for kind in kinds:
                    self.rcopy(phase, kind, here).wait_send()

            far = (2,) if phase in self.rdirect else (2, 3)
            if self.rorder[phase] == "z":
                when(self.place.own, lambda s=sent, far=far: s(far))
                when(self.place.other, lambda s=sent: s((0, 1)))
            else:
                when(self.ractive(phase, None), lambda s=sent, far=far: s((0, 1) + far))


class Job:
    def __init__(self, steps, backlog, latency):
        self.steps, self.backlog, self.latency, self.gate = steps, backlog, latency, None
        self.next, self.ready = 0, 0.0

    @property
    def done(self):
        return self.next == len(self.steps)


class Schedule:
    def __init__(self):
        self.now, self.busy, self.jobs = 0.0, dict(x=0.0, y=0.0, z=0.0), []

    def add(self, job):
        job.ready = self.now
        self.jobs.append(job)
        self.poll()

    def emit(self, job):
        body, axis, link, cost = job.steps[job.next]
        body()
        job.next += 1
        self.now += cost
        if axis is not None:
            self.busy[axis] = max(self.now, self.busy[axis]) + link
            job.ready = self.busy[axis] + job.latency

    def when(self, job):
        axis = job.steps[job.next][1]
        if job.gate is not None and job.next == job.gate[0] and job.gate[1].next < job.gate[2]:
            return math.inf
        if job.gate is not None and job.next == 1 and job.gate[1].next < 3:
            return math.inf
        return job.ready if axis is None else max(job.ready, self.busy[axis] - job.backlog)

    def poll(self):
        while True:
            job = next((j for j in self.jobs if not j.done and self.when(j) <= self.now), None)
            if job is None:
                return
            self.emit(job)

    def tick(self, time):
        self.now += time
        self.poll()

    def need(self, jobs):
        while not all(j.done for j in jobs):
            job = min((j for j in self.jobs if not j.done), key=self.when)
            self.now = max(self.now, self.when(job))
            self.emit(job)


def gather_steps(unit, size):
    steps = []
    for phase in range(3):
        axis, share = unit.gorder[phase], size * 5.6 / 4 ** (2 - phase)
        direct = phase in unit.gdirect

        def one(phase=phase):
            if phase:
                unit.gather3(phase - 1)
            unit.gather1(phase)

        steps.append((one, axis, share * (2 if direct else 1), 0.25))
        if not direct:
            steps.append((lambda phase=phase: unit.gather2(phase), axis, share / 2, 0.25))
    steps.append((lambda: unit.gather3(2), None, 0.0, 0.1))
    return steps


def reduce_steps(unit, size, finish):
    steps = []
    for phase in range(3):
        axis, share = unit.rorder[phase], size * 5.6 / 4 ** phase
        cost = size * 0.3 / 4 ** phase
        direct = phase in unit.rdirect

        def one(phase=phase):
            if phase:
                unit.reduce3(phase - 1)
            unit.reduce1(phase)

        steps.append((one, axis, share * (2 if direct else 0.5), 0.2 + (4 * cost if phase else 0)))
        if not direct:
            steps.append((lambda phase=phase: unit.reduce2(phase), axis, share, 0.25 + cost))
    steps.append((finish, None, 0.0, 0.3))
    return steps


ROUNDS = [("".join(reversed(o))) for o in ORDERS]


def slot(name):
    at = PLACE[name]
    return at if isinstance(at, int) else UNIT[at]


def rdirect_of(name):
    if name == "n":
        return (0, 1, 2)
    return (1, 2) if REDUCE.index(name) >= 11 else (2,)


def landing_shapes(rows, dtype, many):
    shapes = []
    for k, order in enumerate(ROUNDS if many else ROUNDS[:1]):
        for phase in range(3):
            known = order[: phase + 1]
            c = [0 if a in known else None for a in "xyz"]
            slots = 2 if many and phase == 0 else 3
            lead = (many, slots) if many else (slots,)
            shapes.append(pltpu.VMEM(lead + block_shape(rows, *c, False), dtype))
            if many and phase < 2 and order[phase] != "z":
                shapes.append(pltpu.VMEM((many, 2) + block_shape(rows, *c, True), dtype))
    return shapes


PAIR = 64


def kernel(
    tok, pos, inv, ga, gf, gq, gk, wq, wk, wv, wo, wg, wu, wd, cot,
    mixed, tgrad, fin, on,
    W, Wn, *rest,
):
    rest = list(rest)
    place = Place()
    me = place
    c = me.c
    sib = me.sibling()
    mine = pl.multiple_of(c * TOK, TOK)
    theirs = pl.multiple_of((1 - c) * TOK, TOK)
    bufs = []
    for order in ROUNDS:
        bufs.append([(rest.pop(0), rest.pop(0) if order[p] != "z" and p < 2 else None) for p in range(3)])
    nbufs = [(rest.pop(0), None, ()) for p in range(3)]
    (
        send, grecv, rrecv, lsem, psend, precv,
        X, H, FG, BG, CT, QR, KR, Q, K, VA, ATT, RL, BR, HID, ACT, H1, H2,
        COS, SIN, BIAS, PART, RECV, GROW, GQK, SM, POSM, POSR, DG, GP, GPR, FIN, FINN,
    ) = rest

    units = {}
    for i, name in enumerate(SHARD):
        k = REDUCE.index(name)
        units[name] = Unit(
            i, name, W, (i,), (slot(name),), 128, BF, ORDERS[GATHER.index(name) % 3], ROUNDS[k % 3],
            (0, 1) if GATHER.index(name) < 3 else (0,), rdirect_of(name), me, (send, grecv, rrecv), [(w, h, (k // 3,)) for w, h in bufs[k % 3]],
        )
    gains = Unit(
        NU, "n", Wn, (), (), 16, F32, ORDERS[2], ROUNDS[0], (0, 1, 2), rdirect_of("n"), me,
        (send, grecv, rrecv), nbufs,
    )
    every = list(units.values()) + [gains]

    def pair(k, src, dst):
        return pltpu.make_async_remote_copy(
            src_ref=src, dst_ref=dst, send_sem=psend.at[k], recv_sem=precv.at[k],
            device_id=sib, device_id_type=MESH,
        )

    barrier = pltpu.get_barrier_semaphore()
    for target in [me.step(a, s) for a in "xyz" for s in (1, -1, 2)] + [sib]:
        pl.semaphore_signal(barrier, inc=1, device_id=target, device_id_type=MESH)
    tok_local = pltpu.make_async_copy(tok, X.at[pl.ds(mine, TOK)], lsem.at[NU + 1])
    tok_local.start()
    cot_local = pltpu.make_async_copy(cot, CT, lsem.at[NU + 2])
    cot_local.start()
    dp = lax.axis_index("dp")
    SM[...] = jnp.zeros_like(SM)
    SM[0:1, 0:64] = ga[...].astype(F32)
    SM[1:2, 0:64] = gf[...].astype(F32)
    SM[2:3, 0:8] = gq[...].astype(F32)
    SM[3:4, 0:8] = gk[...].astype(F32)
    rows8 = lax.broadcasted_iota(jnp.int32, (8, 128), 0)
    SM[...] = jnp.where(rows8 < 2, pltpu.roll(SM[...], c * 64, 1), pltpu.roll(SM[...], dp * 8, 1))
    POSM[...] = jnp.zeros_like(POSM)
    POSM[0:2, :] = pos[...].astype(F32)
    pl.semaphore_wait(barrier, 10)

    sources = dict(q=wq, k=wk, v=wv, o=wo, g=wg, u=wu, d=wd)

    def shard(unit):
        if unit.name == "n":
            return SM
        part = int(unit.name[1:] or 0)
        return sources[unit.name[0]].at[:, pl.ds(part * 128, 128)]

    def shard_place(unit, core):
        h = unit.rows // 2
        return unit.ref.at[
            unit.lead + (me.yh, me.zi, me.yl, me.x, pl.ds(pl.multiple_of(core * h, 8), h))
        ]

    sequence = [units[n] for n in GATHER[:3]] + [gains] + [units[n] for n in GATHER[3:]]

    @pl.when(me.own)
    def _():
        for u in sequence:
            pltpu.make_async_copy(shard(u), shard_place(u, c), lsem.at[u.number]).start()

    @pl.when(me.other)
    def _():
        for u in sequence:
            pair(u.number, shard(u), shard_place(u, c)).start()

    sched = Schedule()
    jobs = {}
    for u in sequence:

        @pl.when(me.own)
        def _(u=u):
            pltpu.make_async_copy(shard(u), shard_place(u, c), lsem.at[u.number]).wait()
            pair(u.number, shard_place(u, 1 - c), shard_place(u, 1 - c)).wait_recv()

        jobs[u.name] = Job(gather_steps(u, 0.02 if u is gains else 1.0), GATHER_BACKLOG, LATENCY)
        at = GATHER.index(u.name) - 3 * AHEAD if u is not gains else -1
        if at >= 0:
            before = jobs[GATHER[at]]
            jobs[u.name].gate = (len(jobs[u.name].steps) - 3, before, len(before.steps) - 1)
        sched.add(jobs[u.name])

    pos_pair = pair(NU + 1, POSM, POSR)
    pos_pair.start()
    tok_pair = pair(NU + 2, tok, X.at[pl.ds(mine, TOK)])
    tok_pair.start()
    sched.tick(0.8)

    @pl.when(me.other)
    def _():
        for u in sequence:
            pair(u.number, shard(u), shard_place(u, c)).wait_send()

    pos_pair.wait()

    lane = lax.broadcasted_iota(jnp.int32, (128, 128), 1)
    slots = lax.broadcasted_iota(jnp.int32, (128, 256), 1)
    rows2 = lax.broadcasted_iota(jnp.int32, (128, 256), 0)
    inv_row = jnp.broadcast_to(inv[...][:1], (128, 128))

    def tables(b, h):
        place_row = jnp.where(c == b, POSM[h : h + 1, :], POSR[h : h + 1, :])
        places = jnp.broadcast_to(place_row, (128, 128)).T
        angles = places * inv_row
        rs = pl.ds(b * 256 + h * 128, 128)
        COS[rs, :] = jnp.cos(angles)
        sine = jnp.sin(angles)
        SIN[rs, :] = jnp.where(lane < 64, -sine, sine)
        t = rows2 + h * 128
        first = t - jnp.concatenate([places, places], axis=1).astype(jnp.int32)
        allowed = (slots <= t) & (slots >= first)
        bias = jnp.where(allowed, 0.0, -1e30)
        BIAS[b, pl.ds(h * 128, 128), :] = bias

    for b in range(2):
        for h in range(2):
            tables(b, h)
            sched.tick(0.5)
    ones = jnp.ones((256, 128), BF)
    with_ones = lambda f, b: jnp.concatenate([VA[f, b], ones], axis=1)
    tok_local.wait()
    tok_pair.wait()
    cot_local.wait()

    def full(u, yh):
        return [W[UNIT[u] if isinstance(u, str) else u, yh, zi].reshape(1024, 128) for zi in range(2)]

    def wide(u):
        return jnp.concatenate(full(u, 0) + full(u, 1), axis=1)

    def tile(names, yh, j):
        at = lambda u, zi: W[UNIT[u], yh, zi, j // 2, pl.ds(j % 2 * 2, 2)].reshape(256, 128)
        return jnp.concatenate([at(u, zi) for u in names for zi in range(2)], axis=1)

    def turn(v):
        return pltpu.roll(v, 64, 1)

    def normed(v, gain, b):
        rs = pl.ds(b * 256, 256)
        v = v * lax.rsqrt(jnp.mean(v * v, axis=-1, keepdims=True) + EPS) * gain
        return (v * COS[rs, :] + turn(v) * SIN[rs, :]).astype(BF)

    sched.need([jobs[n] for n in ("q0", "q1", "k", "n")])
    for j in range(8):
        for r in range(2):
            GROW[r : r + 1, j * 128 : (j + 1) * 128] = (
                Wn[0, 0, j // 4, j % 4, r : r + 1, :] + Wn[0, 0, j // 4, j % 4, 8 + r : 9 + r, :]
            )
    gq = jnp.zeros((8, 128), F32)
    for j in range(8):
        gq = gq + Wn[0, 0, j // 4, j % 4, 0:8, :] + Wn[0, 0, j // 4, j % 4, 8:16, :]
    GQK[...] = gq
    qgain = GQK[2:3, :]
    kgain = GQK[3:4, :]
    sched.tick(0.3)

    def heads(raw):
        for b in range(2):
            for f in range(4):
                yield b, f, raw[b * 256 : b * 256 + 256, f * 128 : f * 128 + 128]

    def queries(r, carry):
        raw = nn(X[...], wide(r))
        for b, f, v in heads(raw):
            QR[f // 2, r, pl.ds(b * 256, 256), pl.ds(f % 2 * 128, 128)] = v.astype(BF)
            Q[f, b, pl.ds(pl.multiple_of(r * 256, 256), 256), :] = normed(v, qgain, b)
        return carry

    lax.fori_loop(0, 2, queries, 0)
    sched.tick(2.4)
    raw = nn(X[...], wide("k"))
    for b, f, v in heads(raw):
        KR[f // 2, pl.ds(b * 256, 256), pl.ds(f % 2 * 128, 128)] = v.astype(BF)
        K[f, b] = normed(v, kgain, b)
    sched.tick(1.2)

    sched.need([jobs["v"]])
    raw = nn(X[...], wide("v")).astype(BF)
    for f in range(4):
        for b in range(2):
            VA[f, b] = raw[b * 256 : b * 256 + 256, f * 128 : f * 128 + 128]
    sched.tick(0.8)

    scale = HD ** -0.5
    power = scale * math.log2(math.e)

    def attend(f, b):
        yh, zi = f // 2, f % 2
        rs = pl.ds(b * 256, 256)
        for r in range(2):
            s = nt(Q[f, b, pl.ds(r * 256, 256), :], K[f, b])
            e = jnp.exp2(s * power + BIAS[b]).astype(BF)
            ol = nn(e, with_ones(f, b))
            rl = 1.0 / ol[:, 128:256]
            at = pl.ds(r * 256 + zi * 128, 128)
            ATT[yh, rs, at] = (ol[:, 0:128] * rl).astype(BF)
            RL[yh, rs, at] = rl.astype(BF)

    for f in range(4):
        for b in range(2):
            attend(f, b)
            sched.tick(0.35)

    for b in range(2):
        BIAS[b] = BIAS[b].T

    def pair_piece(base, slot, j):
        cols = pl.ds(j * 256, 256)
        return pair(base + j, PART.at[0, :, cols], RECV.at[slot, :, cols])

    def pair_sum(base, slot, products, time):
        def one(rows, j):
            out = None
            for left, names, yh in products:
                p = nt(left(rows), tile(names, yh, j))
                out = p if out is None else out + p
            return out

        def side(i, carry):
            rows = pl.ds(pl.multiple_of(lax.rem(1 - c + i, 2) * TOK, TOK), TOK)
            for j in range(4):
                PART[i, :, pl.ds(j * 256, 256)] = one(rows, j).astype(BF)
                if j % 2:

                    @pl.when(i == 0)
                    def _(j=j):
                        pair_piece(base, slot, j - 1).start()
                        pair_piece(base, slot, j).start()

            return carry

        lax.fori_loop(0, 2, side, 0)
        sched.tick(2 * time)

    def pair_done(base, slot):
        for j in range(4):
            pair_piece(base, slot, j).wait()

    CH = 64

    def rows_then_send(base, dst, body):
        for j in range(TOK // CH):
            rs = pl.ds(pl.multiple_of(mine + j * CH, CH), CH)
            body(pl.ds(j * CH, CH), rs)
            pair(base + j, dst.at[rs], dst.at[rs]).start()
        sched.tick(0.5)

    def rows_done(base, dst):
        for j in range(TOK // CH):
            rs = pl.ds(pl.multiple_of(mine + j * CH, CH), CH)
            pair(base + j, dst.at[rs], dst.at[rs]).wait_send()
            rs = pl.ds(pl.multiple_of(theirs + j * CH, CH), CH)
            pair(base + j, dst.at[rs], dst.at[rs]).wait_recv()

    sched.need([jobs["o0"], jobs["o1"]])

    pair_sum(
        20, 0, [(lambda rows, yh=yh: ATT[yh, rows, :], ("o0", "o1"), yh) for yh in range(2)], 0.8
    )
    pair_done(20, 0)

    def hidden_rows(rs, abs_rs):
        v = PART[1, rs, :].astype(F32) + RECV[0, rs, :].astype(F32)
        BR[rs, :] = v
        n = v * lax.rsqrt(jnp.mean(v * v, axis=-1, keepdims=True) + EPS) * GROW[0:1, :]
        hid = X[abs_rs, :].astype(F32) + n
        HID[rs, :] = hid
        H[abs_rs, :] = hid.astype(BF)

    rows_then_send(24, H, hidden_rows)

    def ffn_tile(s, rows):
        h = H[rows, :]
        g = nn(h, wide("g%d" % s))
        u = nn(h, wide("u%d" % s))
        sg = 0.5 * jnp.tanh(0.5 * g) + 0.5
        silu = g * sg
        act = (silu * u).astype(BF)
        h1 = ((sg + silu * (1.0 - sg)) * u).astype(BF)
        h2 = silu.astype(BF)
        for yh in range(2):
            cols, part = pl.ds(s * 256, 256), slice(yh * 256, yh * 256 + 256)
            ACT[yh, rows, cols] = act[:, part]
            H1[yh, rows, cols] = h1[:, part]
            H2[yh, rows, cols] = h2[:, part]

    sched.need([jobs["g0"], jobs["u0"]])

    def first_tiles(i, carry):
        @pl.when(i == 1)
        def _():
            rows_done(24, H)

        ffn_tile(0, pl.ds(pl.multiple_of(lax.rem(c + i, 2) * TOK, TOK), TOK))
        return carry

    lax.fori_loop(0, 2, first_tiles, 0)
    sched.tick(1.5)
    for s in (1, 2):
        sched.need([jobs["g%d" % s], jobs["u%d" % s]])

        def tiles(m, carry, s=s):
            ffn_tile(s, pl.ds(pl.multiple_of(m * 256, 256), 256))
            return carry

        lax.fori_loop(0, 2, tiles, 0)
        sched.tick(1.5)
    for u in every:
        if u.name[0] != "d":
            u.gather_drain()
    sched.need([jobs["d%d" % s] for s in range(3)])
    pair_sum(
        28, 1, [(lambda rows, yh=yh: ACT[yh, rows, :], ("d0", "d1", "d2"), yh) for yh in range(2)], 1.1
    )
    DG[...] = jnp.zeros_like(DG)
    GP[...] = jnp.zeros_like(GP)
    for n in ("d0", "d1", "d2"):
        units[n].gather_drain()
    pair_done(28, 1)

    def rms_back(v, r, gain, dn, at):
        gd = gain * dn
        vr = v * r
        grad = r * (gd - vr * jnp.mean(gd * vr, axis=-1, keepdims=True))
        dg = dn * vr
        DG[at, :, :] += jnp.sum(dg.reshape(CH // 8, 8, 1024), axis=0)
        return grad

    def ffn_rows(rs, abs_rs):
        v = PART[1, rs, :].astype(F32) + RECV[1, rs, :].astype(F32)
        gain = GROW[1:2, :]
        r = lax.rsqrt(jnp.mean(v * v, axis=-1, keepdims=True) + EPS)
        PART[0, rs, :] = (HID[rs, :] + v * r * gain).astype(BF)
        FG[abs_rs, :] = rms_back(v, r, gain, CT[rs, :].astype(F32), 1).astype(BF)

    rows_then_send(32, FG, ffn_rows)
    mixed_out = pltpu.make_async_copy(PART.at[0], mixed, lsem.at[0])
    mixed_out.start()

    def weight_grad(u, left, right):
        def half(j, carry):
            cols = pl.ds(pl.multiple_of(j * 512, 512), 512)
            out = tn(left[:, cols], jnp.concatenate([right(0), right(1)], axis=1)).astype(BF)
            for yh in range(2):
                for zi in range(2):
                    at = (yh * 2 + zi) * 128
                    W[slot(u), yh, zi, j] = out[:, at : at + 128].reshape(4, 128, 128)
            return carry

        lax.fori_loop(0, 2, half, 0)

    fin_jobs = []

    def start_reduce(u):
        unit = gains if u == "n" else units[u]
        out = FINN if u == "n" else FIN.at[unit.number]

        def finish():
            unit.reduce3(2, out)

            @pl.when(me.own)
            def _():
                fin_pair(unit, 1 - c).start()

            unit.reduce_drain()

        job = Job(reduce_steps(unit, 0.02 if u == "n" else 1.0, finish), REDUCE_BACKLOG, REDUCE_LATENCY)
        fin_jobs.append(job)
        sched.add(job)

    def fin_pair(unit, core):
        if unit.name == "n":
            ref = FINN
        else:
            ref = FIN.at[unit.number, pl.ds(pl.multiple_of(core * 64, 64), 64)]
        return pair(48 + unit.number, ref, ref)

    def act_back(s, rs, time):
        cols = pl.ds(s * 256, 256)
        da = nn(FG[rs, :], wide("d%d" % s))
        for yh in range(2):
            part = da[:, yh * 256 : yh * 256 + 256]
            H1[yh, rs, cols] = (part * H1[yh, rs, cols].astype(F32)).astype(BF)
            H2[yh, rs, cols] = (part * H2[yh, rs, cols].astype(F32)).astype(BF)
        sched.tick(time)

    for s in range(3):
        act_back(s, pl.ds(mine, TOK), 0.0)
    rows_done(32, FG)

    def down(u):
        weight_grad(u, FG, lambda yh: ACT[yh, :, pl.ds(int(u[1]) * 256, 256)])
        sched.tick(0.85)
        start_reduce(u)

    def gate_up(u):
        cols = pl.ds(int(u[1]) * 256, 256)
        part = H1 if u[0] == "g" else H2
        weight_grad(u, H, lambda yh: part[yh, :, cols])
        sched.tick(0.85)
        start_reduce(u)

    down("d0")
    down("d1")
    act_back(0, pl.ds(theirs, TOK), 0.45)
    down("d2")
    act_back(1, pl.ds(theirs, TOK), 0.45)
    gate_up("g0")
    act_back(2, pl.ds(theirs, TOK), 0.45)
    gate_up("u0")
    mixed_out.wait()
    pair_sum(
        36, 0,
        [(lambda rows, yh=yh: H1[yh, rows, :], ("g0", "g1", "g2"), yh) for yh in range(2)]
        + [(lambda rows, yh=yh: H2[yh, rows, :], ("u0", "u1", "u2"), yh) for yh in range(2)],
        2.2,
    )
    gate_up("g1")
    gate_up("u1")
    pair_done(36, 0)

    def branch_rows(rs, abs_rs):
        dn = CT[rs, :].astype(F32) + PART[1, rs, :].astype(F32) + RECV[0, rs, :].astype(F32)
        HID[rs, :] = dn
        v = BR[rs, :]
        r = lax.rsqrt(jnp.mean(v * v, axis=-1, keepdims=True) + EPS)
        BG[abs_rs, :] = rms_back(v, r, GROW[0:1, :], dn, 0).astype(BF)

    rows_then_send(40, BG, branch_rows)
    gate_up("g2")
    gate_up("u2")
    rows_done(40, BG)

    DO = FG
    for r in range(2):
        out = nn(BG[...], wide("o%d" % r)).astype(BF)
        for yh in range(2):
            DO[:, pl.ds(yh * 512 + r * 256, 256)] = out[:, yh * 256 : yh * 256 + 256]
        sched.tick(0.8)
    for r in range(2):
        weight_grad("o%d" % r, BG, lambda yh: ATT[yh, :, pl.ds(r * 256, 256)])
        sched.tick(0.85)
        start_reduce("o%d" % r)

    def head_back(raw, gain, d, rs, row_at):
        d = d * COS[rs, :] - turn(d) * SIN[rs, :]
        r = lax.rsqrt(jnp.mean(raw * raw, axis=-1, keepdims=True) + EPS)
        gd = gain * d
        vr = raw * r
        GP[pl.ds(row_at, 8), :] += jnp.sum((d * vr).reshape(32, 8, 128), axis=0)
        return (r * (gd - vr * jnp.mean(gd * vr, axis=-1, keepdims=True))).astype(BF)

    QG, KVG = ACT, H1

    def attend_back(zi, n):
        yh, b = lax.div(n, 2), lax.rem(n, 2)
        f = yh * 2 + zi
        rs = pl.ds(pl.multiple_of(b * 256, 256), 256)
        dk, dv = None, None
        for r in range(2):
            at = pl.ds(r * 256 + zi * 128, 128)
            q = Q[f, b, pl.ds(r * 256, 256), :]
            do = DO[rs, pl.ds(pl.multiple_of(yh * 512 + (r * 256 + zi * 128), 128), 128)]
            do = do.astype(F32) * RL[yh, rs, at].astype(F32)
            dol = do.astype(BF)
            doa = jnp.concatenate([dol, (-(do * ATT[yh, rs, at].astype(F32))).astype(BF)], axis=1)
            e = jnp.exp2(nt(K[f, b], q) * power + BIAS[b])
            ds = (e * nt(with_ones(f, b), doa)).astype(BF)
            dv_r = nn(e.astype(BF), dol)
            dk_r = nn(ds, q)
            dv = dv_r if dv is None else dv + dv_r
            dk = dk_r if dk is None else dk + dk_r
            dq = tn(ds, K[f, b]) * scale
            raw = QR[yh, r, rs, pl.ds(zi * 128, 128)].astype(F32)
            QG[yh, rs, at] = head_back(raw, qgain, dq, rs, 0)
        raw = KR[yh, rs, pl.ds(zi * 128, 128)].astype(F32)
        KVG[yh, rs, pl.ds(zi * 128, 128)] = head_back(raw, kgain, dk * scale, rs, 8)
        KVG[yh, rs, pl.ds(256 + zi * 128, 128)] = dv.astype(BF)

    for zi in range(2):

        def back(n, carry, zi=zi):
            attend_back(zi, n)
            return carry

        lax.fori_loop(0, 4, back, 0)
        sched.tick(4.0)

    def gain_rows(at, row_at):
        summed = jnp.sum(DG[at], axis=0, keepdims=True)
        for j in range(8):
            GP[row_at + j : row_at + j + 1, :] = summed[:, j * 128 : (j + 1) * 128]

    qsum = jnp.sum(GP[0:8, :], axis=0, keepdims=True)
    ksum = jnp.sum(GP[8:16, :], axis=0, keepdims=True)
    gain_rows(0, 16)
    gain_rows(1, 24)
    GP[0:1, :] = qsum
    GP[8:9, :] = ksum
    gain_pair = pair(NU + 3, GP, GPR)
    gain_pair.start()

    def proj_grad(u, src, at):
        weight_grad(u, X, lambda yh: src[yh, :, pl.ds(at, 256)])
        sched.tick(0.85)
        start_reduce(u)

    proj_grad("q0", QG, 0)
    proj_grad("q1", QG, 256)
    proj_grad("k", KVG, 0)
    proj_grad("v", KVG, 256)
    gain_pair.wait()
    GPR[...] += GP[...]
    Wn[...] = jnp.zeros_like(Wn)
    for j in range(8):
        for f0 in range(2):
            for f1 in range(2):
                Wn[f0, f1, j // 4, j % 4, 0:1, :] = GPR[16 + j : 17 + j, :]
                Wn[f0, f1, j // 4, j % 4, 1:2, :] = GPR[24 + j : 25 + j, :]
                Wn[f0, f1, j // 4, j % 4, 8:9, :] = GPR[0:1, :]
                Wn[f0, f1, j // 4, j % 4, 9:10, :] = GPR[8:9, :]
    start_reduce("n")
    pair_sum(
        44, 1,
        [(lambda rows, yh=yh: QG[yh, rows, pl.ds(0, 512)], ("q0", "q1"), yh) for yh in range(2)]
        + [(lambda rows, yh=yh: KVG[yh, rows, pl.ds(0, 512)], ("k", "v"), yh) for yh in range(2)],
        1.4,
    )
    pair_done(44, 1)

    for j in range(TOK // CH):
        rs = pl.ds(j * CH, CH)
        HID[rs, :] = HID[rs, :] + PART[1, rs, :].astype(F32) + RECV[1, rs, :].astype(F32)
    tgrad_out = pltpu.make_async_copy(HID, tgrad, lsem.at[1])
    tgrad_out.start()
    sched.tick(0.6)

    sched.need(fin_jobs)
    for u in every:

        @pl.when(me.own)
        def _(u=u):
            fin_pair(u, 1 - c).wait_send()

        @pl.when(me.other)
        def _(u=u):
            fin_pair(u, c).wait_recv()

    mrows = pl.ds(pl.multiple_of(c * 64, 64), 64)
    fin_out = pltpu.make_async_copy(FIN.at[:, mrows], fin, lsem.at[2])
    fin_out.start()
    on_out = pltpu.make_async_copy(FINN, on, lsem.at[3])
    on_out.start()
    tgrad_out.wait()
    fin_out.wait()
    on_out.wait()


def finish_kernel(mixed_in, tgrad_in, fin, gn, mixed, tgrad, oq, ok, ov, oo, og, ou, od, oqg, okg, oag, ofg, sem):
    dp = lax.axis_index("dp")
    core = lax.rem(dp, 2)
    copies = [(mixed_in, mixed), (tgrad_in, tgrad)]
    targets = dict(q=oq, k=ok, v=ov, o=oo, g=og, u=ou, d=od)
    for i, name in enumerate(SHARD):
        part = int(name[1:] or 0)
        copies.append((fin.at[i], targets[name[0]].at[:, pl.ds(part * 128, 128)]))
    copies = [pltpu.make_async_copy(a, b, sem.at[i]) for i, (a, b) in enumerate(copies)]
    for copy in copies:
        copy.start()
    odd = core == 1
    for ref, row in ((oag, 0), (ofg, 1)):
        v = gn[...]
        v = jnp.where(odd, pltpu.roll(v, 64, 1), v)
        ref[...] = v[row : row + 1, 0:64]
    v = gn[...]
    back = lax.rem(128 - dp * 8, 128)
    v = pltpu.roll(v, back, 1)
    oqg[...] = v[8:9, 0:8]
    okg[...] = v[9:10, 0:8]
    for copy in copies:
        copy.wait()


def on_device(
    tokens, positions, w_query, w_key, w_value, w_out, w_gate, w_up, w_down,
    query_gain, key_gain, attn_gain, ffn_gain, cotangent,
):
    steps_up = np.arange(0, HD, 2).astype(np.float32) / np.float32(HD)
    inverse = (np.float32(ROPE_BASE) ** (-steps_up)).astype(np.float32)
    inv = jnp.asarray(np.tile(np.concatenate([inverse, inverse])[None], (8, 1)))
    vm = pl.BlockSpec(memory_space=pltpu.VMEM)
    hbm = pl.BlockSpec(memory_space=pl.ANY)
    far = pl.BlockSpec(memory_space=pltpu.HBM)
    n = (NU + 1) * 12
    V = pltpu.VMEM
    sems = [pltpu.SemaphoreType.DMA((n,))] * 3 + [
        pltpu.SemaphoreType.DMA((NU + 3,)),
        pltpu.SemaphoreType.DMA((PAIR,)),
        pltpu.SemaphoreType.DMA((PAIR,)),
    ]
    work = [
        V((512, D), BF), V((512, D), BF), V((512, D), BF), V((512, D), BF),
        V((TOK, D), BF),
        V((2, 2, 512, 256), BF), V((2, 512, 256), BF),
        V((4, 2, 512, 128), BF), V((4, 2, 256, 128), BF), V((4, 2, 256, 128), BF),
        V((2, 512, 512), BF), V((2, 512, 512), BF),
        V((TOK, D), F32), V((TOK, D), F32),
        V((2, 512, 768), BF), V((2, 512, 768), BF), V((2, 512, 768), BF),
        V((512, 128), F32), V((512, 128), F32), V((2, 256, 256), F32),
        V((2, TOK, D), BF), V((2, TOK, D), BF),
        V((8, D), F32), V((8, 128), F32), V((8, 128), F32), V((8, 128), F32), V((8, 128), F32), V((2, 8, D), F32),
        V((32, 128), F32), V((32, 128), F32),
        V((NU, 128, 128), F32), V((16, 128), F32),
    ]
    f = lambda *s: jax.ShapeDtypeStruct(s, F32)
    main_out = pl.pallas_call(
        kernel,
        out_shape=(jax.ShapeDtypeStruct((TOK, D), BF), f(TOK, D), f(NU, 64, 128), f(16, 128)),
        in_specs=[hbm] + [vm] * 6 + [hbm] * 8,
        out_specs=[hbm] * 4,
        scratch_shapes=[V((NU + SPARE, 2, 2, 2, 4, 128, 128), BF), V((2, 2, 2, 4, 16, 128), F32)]
        + landing_shapes(128, BF, 5) + landing_shapes(16, F32, 0) + sems + work,
        compiler_params=pltpu.CompilerParams(
            collective_id=1, has_side_effects=True, vmem_limit_bytes=int(63.5 * 2**20)
        ),
        cost_estimate=pl.CostEstimate(flops=26 * 10**9, bytes_accessed=4 * 10**6, transcendentals=0),
    )(
        tokens, positions.reshape(2, 128), inv,
        attn_gain.reshape(1, 64), ffn_gain.reshape(1, 64), query_gain.reshape(1, 8), key_gain.reshape(1, 8),
        w_query, w_key, w_value, w_out.T, w_gate, w_up, w_down.T, cotangent,
    )
    outs = pl.pallas_call(
        finish_kernel,
        out_shape=(
            jax.ShapeDtypeStruct((TOK, D), BF), f(TOK, D),
            f(64, 256), f(64, 128), f(64, 128), f(64, 256), f(64, 384), f(64, 384), f(64, 384),
            f(1, 8), f(1, 8), f(1, 64), f(1, 64),
        ),
        in_specs=[vm] * 4,
        out_specs=[far] * 9 + [vm] * 4,
        scratch_shapes=[pltpu.SemaphoreType.DMA((NU + 2,))],
        compiler_params=pltpu.CompilerParams(vmem_limit_bytes=int(63.5 * 2**20)),
    )(*main_out)
    mixed, tgrad, gq, gk, gv, go, gg, gu, gd, nq, nk, na, nf = outs
    return (
        mixed, tgrad, gq, gk, gv, go.T, gg, gu, gd.T,
        nq.reshape(8), nk.reshape(8), na.reshape(64), nf.reshape(64),
    )


def solution(mesh):
    both, w, wt = P(("dp", "fsdp"), None), P("dp", "fsdp"), P("fsdp", "dp")
    return jax.shard_map(
        on_device,
        mesh=mesh,
        in_specs=(both, P(("dp", "fsdp")), w, w, w, wt, w, w, wt, P("dp"), P("dp"), P("dp"), P("dp"), both),
        out_specs=(both, both, w, w, w, wt, w, w, wt, P("dp"), P("dp"), P("dp"), P("dp")),
        check_vma=False,
    )
```
